32 devices in a mesh: obs: 8 (over y, x, core), row: 4 (over z).
Axes of the slice: x: 2, y: 2, z: 4, core: 2. Of those that a mesh axis runs over, the one named last changes fastest.
Arguments:
- camera_jacobian: float32 [18, 32768], P(None, ('obs', 'row')), may hold values from -0.75 to 0.75
- point_jacobian: float32 [6, 32768], P(None, ('obs', 'row')), may hold values from -6 to 6
- residual: float32 [2, 32768], P(None, ('obs', 'row')), may hold values from -6 to 6
- send_order: int32 [32768], P(('obs', 'row')), may hold values from 0 to 1023, as said below
- camera_of: int32 [32768], P(('obs', 'row')), may hold values from 0 to 63, as said below
- track_of: int32 [32768], P(('obs', 'row')), may hold values from 0 to 511, as said below
- partner: int32 [7, 32768], P(None, ('obs', 'row')), may hold values from 0 to 1023, as said below
- pair_slot: int32 [7, 32768], P(None, ('obs', 'row')), may hold values from 0 to 896, as said below
Outputs:
- camera_hessian: float32 [81, 512], P(None, ('obs', 'row'))
- camera_gradient: float32 [9, 512], P(None, ('obs', 'row'))
- pair_hessian: float32 [81, 7168], P(None, ('obs', 'row'))
The draws below stay inside these ranges and needn't reach their ends.
Inputs may be any that keep to these rules, and one draw needn't show every extreme that they name: `send_order`: on each device a permutation of the device's 1024 observations. `camera_of`: A device's observations are ordered by camera. `track_of`: local track of each received slot of one track owner; a track has 2 to 8 observations, at most one from each source obs index, from cyclically consecutive source obs indices; some track ids are unused. partner[k] of a received slot is the slot of the k-th other observation of its track in track order, or the slot itself where the track has fewer than k + 2 observations. pair_slot[k] of a send slot is c * 14 + o, where c is the observation's camera and o encodes its partner's camera; 896 exactly where partner[k] is the slot itself.
All inputs are finite; a program needn't handle non-finite values.
Results may differ from the reference program's by a relative error of at most 0.00014.
Values sent between devices are 32-bit elements; how exact they have to be, the bound alone decides.
A program may use at most 64 MiB of HBM per device.

```python
import jax
import jax.numpy as jnp

OBS_DEV = 1024
CAM_ROW = 16
CAMP = 9
PNTP = 3
LMAX = 8
NBR = 14
NOBS = 32768
N_OBS = 8
N_ROW = 4


slot_track = [[0, 0, 0, 0, 0, 0, 0, 0], [0, 0, 0, 0, 1, 1, 1, 1], [0, 0, 0, 0, 0, 1, 1, 1], [0, 0, 0, 0, 0, 0, 1, 1], [0, 0, 1, 1, 2, 2, 3, 3], [0, 0, 0, 1, 1, 1, 2, 2], [0, 0, 0, 0, 1, 1, 2, 2]]


slot_place = [[0, 1, 2, 3, 4, 5, 6, 7], [0, 1, 2, 3, 0, 1, 2, 3], [0, 1, 2, 3, 4, 0, 1, 2], [0, 1, 2, 3, 4, 5, 0, 1], [0, 1, 0, 1, 0, 1, 0, 1], [0, 1, 2, 0, 1, 2, 0, 1], [0, 1, 2, 3, 0, 1, 0, 1]]


slot_length = [[8, 8, 8, 8, 8, 8, 8, 8], [4, 4, 4, 4, 4, 4, 4, 4], [5, 5, 5, 5, 5, 3, 3, 3], [6, 6, 6, 6, 6, 6, 2, 2], [2, 2, 2, 2, 2, 2, 2, 2], [3, 3, 3, 3, 3, 3, 2, 2], [4, 4, 4, 4, 2, 2, 2, 2]]


def layout(key):
    base_key = jax.random.fold_in(key, 11)
    subkeys = jax.random.split(base_key, 5)
    per_peer = OBS_DEV // N_OBS
    block_count = N_OBS // 8
    camera_count = CAM_ROW * N_ROW
    slot_count = camera_count * NBR
    rotation = jax.random.randint(subkeys[0], (N_ROW, N_OBS, per_peer, 1), 0, 8)
    pattern = jax.random.randint(subkeys[1], (N_ROW, N_OBS, per_peer, block_count), 0, 7)
    dense_row = jax.random.randint(subkeys[2], (), 0, N_ROW)
    row_ids = jnp.arange(N_ROW, dtype=jnp.int32).reshape(N_ROW, 1, 1, 1)
    pattern = jnp.where(row_ids == dense_row, 0, pattern)
    start_camera = jax.random.randint(subkeys[3], (N_ROW, N_OBS, per_peer, block_count * 4), 0, camera_count - 1)
    scores = jax.random.randint(subkeys[4], (N_ROW, N_OBS, N_OBS, per_peer), 0, 1 << 20) * per_peer
    scores = scores + jnp.arange(per_peer, dtype=jnp.int32)
    place = jnp.argsort(scores, axis=3).astype(jnp.int32)
    inverse = jnp.argsort(place, axis=3).astype(jnp.int32)
    sources = jnp.arange(N_OBS, dtype=jnp.int32).reshape(1, 1, 1, N_OBS)
    column = (sources - rotation) % N_OBS
    block = column // 8
    within = column % 8
    kind = jnp.take_along_axis(pattern, block, axis=3)
    track_sub = jnp.asarray(slot_track, dtype=jnp.int32)[kind, within]
    position = jnp.asarray(slot_place, dtype=jnp.int32)[kind, within]
    length = jnp.asarray(slot_length, dtype=jnp.int32)[kind, within]
    track_id = jnp.arange(per_peer, dtype=jnp.int32).reshape(1, 1, per_peer, 1) * (block_count * 4) + block * 4 + track_sub
    start_local = jnp.take_along_axis(start_camera, block * 4 + track_sub, axis=3)
    first_source = (sources - position) % N_OBS
    capture = first_source + N_OBS * start_local + position
    camera_local = capture // N_OBS
    place_by_source = jnp.transpose(place, (0, 1, 3, 2))
    self_slot = sources * per_peer + place_by_source
    partner_slots = []
    pair_slots = []
    for partner_rank in range(7):
        other = partner_rank + (partner_rank >= position).astype(jnp.int32)
        valid = other < length
        other_source = (sources + other - position) % N_OBS
        other_slot = other_source * per_peer + jnp.take_along_axis(place_by_source, other_source, axis=3)
        partner_slots.append(jnp.where(valid, other_slot, self_slot))
        offset = other - position
        neighbour = jnp.where(offset < 0, offset + 7, offset + 6)
        pair_slots.append(jnp.where(valid, camera_local * NBR + neighbour, slot_count))

    def to_owner(values):
        return jnp.take_along_axis(jnp.transpose(values, (0, 1, 3, 2)), inverse, axis=3)

    def owner_flat(values):
        return jnp.transpose(to_owner(values), (1, 0, 2, 3)).reshape(-1)

    def image_flat(values):
        return jnp.transpose(to_owner(values), (2, 0, 1, 3)).reshape(-1)
    track_of = owner_flat(track_id).astype(jnp.int32)
    partner = jnp.stack([owner_flat(entry) for entry in partner_slots]).astype(jnp.int32)
    pair_slot = jnp.stack([image_flat(entry) for entry in pair_slots]).astype(jnp.int32)
    camera_send = image_flat(camera_local).reshape(N_OBS * N_ROW, OBS_DEV)
    order_keys = camera_send * OBS_DEV + jnp.arange(OBS_DEV, dtype=jnp.int32)
    sorted_pos = jnp.argsort(order_keys, axis=1).astype(jnp.int32)
    camera_of = jnp.take_along_axis(camera_send, sorted_pos, axis=1).astype(jnp.int32)
    send_order = jnp.argsort(sorted_pos, axis=1).astype(jnp.int32)
    return (send_order.reshape(-1), camera_of.reshape(-1), track_of, partner, pair_slot)


def draw_send_order(key, part):
    return layout(key)[0]


def draw_camera_of(key, part):
    return layout(key)[1]


def draw_track_of(key, part):
    return layout(key)[2]


def draw_partner(key, part):
    return layout(key)[3]


def draw_pair_slot(key, part):
    return layout(key)[4]


def block_scale(own_key, shape, cuts, least, largest):
    gain, own = 1.0, jax.random.fold_in(own_key, 6)
    for dim, blocks in cuts:
        draws = jnp.exp(jax.random.uniform(jax.random.fold_in(own, dim), (blocks,), jnp.float32, least / len(cuts), largest / len(cuts)))
        gain = gain * jnp.repeat(draws, shape[dim] // blocks).reshape([-1 if axis == dim else 1 for axis in range(len(shape))])
    return gain


def bell_draw(stream_key, shape, deviation, most, cuts=(), held_as=jnp.bfloat16):
    result = deviation * jax.random.normal(stream_key, shape, jnp.float32)
    if cuts:
        result = result * block_scale(stream_key, shape, cuts, -0.22, 0.18)
    return jnp.clip(result, -most, most).astype(held_as)


def setup_inputs(seed: int = 0) -> dict:
    arg_keys = jax.random.split(jax.random.key(seed), 9)
    return {
        "camera_jacobian": bell_draw(arg_keys[0], (2 * CAMP, NOBS), 0.125, 0.75, ((1, 32),), jnp.float32),
        "point_jacobian": bell_draw(arg_keys[1], (2 * PNTP, NOBS), 1.0, 6.0, ((1, 32),), jnp.float32),
        "residual": bell_draw(arg_keys[2], (2, NOBS), 1.0, 6.0, ((1, 32),), jnp.float32),
        "send_order": draw_send_order(jax.random.fold_in(arg_keys[8], 71), 0),
        "camera_of": draw_camera_of(jax.random.fold_in(arg_keys[8], 71), 0),
        "track_of": draw_track_of(jax.random.fold_in(arg_keys[8], 71), 0),
        "partner": draw_partner(jax.random.fold_in(arg_keys[8], 71), 0),
        "pair_slot": draw_pair_slot(jax.random.fold_in(arg_keys[8], 71), 0),
    }


damping = 1.0

def eliminate(camera_rows, point_rows, resid_rows, track_of, track_count):
    camera = camera_rows.reshape(2, 9, -1)
    point_jac = point_rows.reshape(2, 3, -1)
    normal = jnp.stack([point_jac[0, 0] * point_jac[0, 0] + point_jac[1, 0] * point_jac[1, 0], point_jac[0, 0] * point_jac[0, 1] + point_jac[1, 0] * point_jac[1, 1], point_jac[0, 0] * point_jac[0, 2] + point_jac[1, 0] * point_jac[1, 2], point_jac[0, 1] * point_jac[0, 1] + point_jac[1, 1] * point_jac[1, 1], point_jac[0, 1] * point_jac[0, 2] + point_jac[1, 1] * point_jac[1, 2], point_jac[0, 2] * point_jac[0, 2] + point_jac[1, 2] * point_jac[1, 2], point_jac[0, 0] * resid_rows[0] + point_jac[1, 0] * resid_rows[1], point_jac[0, 1] * resid_rows[0] + point_jac[1, 1] * resid_rows[1], point_jac[0, 2] * resid_rows[0] + point_jac[1, 2] * resid_rows[1]])
    totals = jnp.zeros((9, track_count), jnp.float32).at[:, track_of].add(normal)
    pivot_first = jnp.sqrt(totals[0] + damping)
    lower_one = totals[1] / pivot_first
    lower_two = totals[2] / pivot_first
    pivot_second = jnp.sqrt(totals[3] + damping - lower_one * lower_one)
    lower_mid = (totals[4] - lower_two * lower_one) / pivot_second
    pivot_third = jnp.sqrt(totals[5] + damping - lower_two * lower_two - lower_mid * lower_mid)
    solved_one = totals[6] / pivot_first
    solved_two = (totals[7] - lower_one * solved_one) / pivot_second
    solved_three = (totals[8] - lower_two * solved_one - lower_mid * solved_two) / pivot_third
    per_track = jnp.stack([pivot_first, lower_one, lower_two, pivot_second, lower_mid, pivot_third, solved_one, solved_two, solved_three])
    per_obs = per_track[:, track_of]
    weights = camera[0][:, None, :] * point_jac[0][None, :, :] + camera[1][:, None, :] * point_jac[1][None, :, :]
    column_one = weights[:, 0] / per_obs[0]
    column_two = (weights[:, 1] - per_obs[1] * column_one) / per_obs[3]
    column_three = (weights[:, 2] - per_obs[2] * column_one - per_obs[4] * column_two) / per_obs[5]
    factor = jnp.stack([column_one, column_two, column_three])
    point_shift = column_one * per_obs[6] + column_two * per_obs[7] + column_three * per_obs[8]
    return (factor, point_shift)

def camera_terms(camera_rows, resid_rows, factor, point_shift):
    camera = camera_rows.reshape(2, 9, -1)
    normal = camera[0][:, None, :] * camera[0][None, :, :] + camera[1][:, None, :] * camera[1][None, :, :]
    schur_part = factor[0][:, None, :] * factor[0][None, :, :] + factor[1][:, None, :] * factor[1][None, :, :] + factor[2][:, None, :] * factor[2][None, :, :]
    gradient = camera[0] * resid_rows[0] + camera[1] * resid_rows[1] - point_shift
    return jnp.concatenate([(normal - schur_part).reshape(81, -1), gradient], axis=0)

def pair_product(left, right):
    total = left[0][:, None, :] * right[0][None, :, :] + left[1][:, None, :] * right[1][None, :, :] + left[2][:, None, :] * right[2][None, :, :]
    return -total.reshape(81, -1)

def reference(camera_jacobian, point_jacobian, residual, send_order, camera_of, track_of, partner, pair_slot):
    device_count = N_OBS * N_ROW
    per_peer = OBS_DEV // N_OBS
    camera_count = CAM_ROW * N_ROW
    slot_count = camera_count * NBR
    send_perm = send_order.reshape(device_count, OBS_DEV)

    def outgoing(values):
        shaped = values.reshape(values.shape[0], device_count, OBS_DEV)
        return jnp.take_along_axis(shaped, jnp.broadcast_to(send_perm[None], shaped.shape), axis=2)

    def regroup(values):
        height = values.shape[0]
        moved = values.reshape(height, N_OBS, N_ROW, N_OBS, per_peer).transpose(0, 3, 2, 1, 4)
        return moved.reshape(height, device_count, OBS_DEV)
    camera_sent = outgoing(camera_jacobian)
    point_sent = outgoing(point_jacobian)
    resid_sent = outgoing(residual)
    tracks = track_of.reshape(device_count, OBS_DEV)
    factor, point_shift = jax.vmap(eliminate, in_axes=(1, 1, 1, 0, None), out_axes=(2, 1))(regroup(camera_sent), regroup(point_sent), regroup(resid_sent), tracks, OBS_DEV // 2)
    factor_back = regroup(factor.reshape(27, -1)).reshape(3, 9, -1)
    shift_back = regroup(point_shift.reshape(9, -1)).reshape(9, -1)
    local_terms = camera_terms(camera_sent.reshape(18, -1), resid_sent.reshape(2, -1), factor_back, shift_back)
    camera_ids = jnp.take_along_axis(camera_of.reshape(device_count, OBS_DEV), send_perm, axis=1)
    group_of = (jnp.arange(device_count) // N_ROW).astype(jnp.int32)
    camera_index = (group_of[:, None] * camera_count + camera_ids).astype(jnp.int32).reshape(-1)
    camera_sum = jnp.zeros((90, N_OBS * camera_count), jnp.float32).at[:, camera_index].add(local_terms)
    flat_factor = factor.reshape(3, 9, device_count, OBS_DEV)
    partners = partner.reshape(LMAX - 1, device_count, OBS_DEV)
    slot_index = pair_slot.reshape(LMAX - 1, device_count, OBS_DEV)
    group_base = (group_of * slot_count).astype(jnp.int32)[:, None]
    pair_total = jnp.zeros((81, N_OBS * slot_count + 1), jnp.float32)
    for partner_rank in range(LMAX - 1):
        chosen = jnp.take_along_axis(flat_factor, jnp.broadcast_to(partners[partner_rank][None, None], flat_factor.shape), axis=3)
        block_values = pair_product(flat_factor.reshape(3, 9, -1), chosen.reshape(3, 9, -1))
        arrived = regroup(block_values).reshape(81, -1)
        target = jnp.where(slot_index[partner_rank] == slot_count, N_OBS * slot_count, group_base + slot_index[partner_rank]).astype(jnp.int32).reshape(-1)
        pair_total = pair_total.at[:, target].add(arrived)
    return (camera_sum[:81], camera_sum[81:], pair_total[:, :N_OBS * slot_count])
```

```python
import functools

import jax
import jax.numpy as jnp
from jax import lax
from jax.experimental import pallas as pl
from jax.experimental.pallas import tpu as pltpu
from jax.sharding import PartitionSpec as P

CAM_ROW = 16
NBR = 14
LANES = 128
SUBLANES = 8
CHUNK = 256
VMEM_BYTES = 48 * 1024 * 1024


def lane_gather(values, index):
    return jnp.take_along_axis(values, index, axis=1, mode="promise_in_bounds")


def permute_kernel(camera_ref, point_ref, resid_ref, order_ref, ids_ref, sent_ref, cam_ref):
    blocks = order_ref.shape[0]
    order = order_ref[...]
    block_of = lax.shift_right_logical(order, LANES.bit_length() - 1)
    lane_of = lax.bitwise_and(order, LANES - 1)

    def permuted(row_of_block):
        total = None
        for b in range(blocks):
            row = jnp.broadcast_to(row_of_block(b), (blocks, LANES))
            picked = lane_gather(row, lane_of)
            total = picked if b == 0 else jnp.where(block_of == b, picked, total)
        return total

    start = 0
    for ref in (camera_ref, point_ref, resid_ref):
        for f in range(ref.shape[0]):
            sent_ref[start + f] = permuted(
                lambda b: ref[f : f + 1, b * LANES : (b + 1) * LANES]
            )
        start += ref.shape[0]
    cam_ref[...] = permuted(lambda b: ids_ref[b : b + 1, :])


def exchange_kernel(
    n, sent_ref, partner_ref, recv_ref, part_ref, staged, send_sem, recv_sem, id_send, id_recv
):
    me = lax.axis_index("obs")
    ranks = partner_ref.shape[0]
    barrier = pltpu.get_barrier_semaphore()
    for d in range(1, n):
        pl.semaphore_signal(
            barrier,
            inc=1,
            device_id={"obs": lax.rem(me + d, n)},
            device_id_type=pl.DeviceIdType.MESH,
        )
    for x in range(n):
        staged[x] = jnp.zeros((SUBLANES, LANES), jnp.int32)
        staged[x, 0:ranks] = partner_ref[:, x * LANES : (x + 1) * LANES]
    pl.semaphore_wait(barrier, n - 1)

    def rows_copy(d):
        peer = lax.rem(me + d, n)
        return pltpu.make_async_remote_copy(
            src_ref=sent_ref,
            dst_ref=recv_ref.at[me],
            send_sem=send_sem.at[peer],
            recv_sem=recv_sem.at[me],
            device_id={"obs": peer},
            device_id_type=pl.DeviceIdType.MESH,
        )

    def ids_copy(d):
        peer = lax.rem(me + d, n)
        return pltpu.make_async_remote_copy(
            src_ref=staged.at[peer],
            dst_ref=part_ref.at[me],
            send_sem=id_send.at[peer],
            recv_sem=id_recv.at[me],
            device_id={"obs": peer},
            device_id_type=pl.DeviceIdType.MESH,
        )

    for d in range(1, n):
        ids_copy(d).start()
        rows_copy(d).start()
    part_ref[me] = staged[me]
    for d in range(1, n):
        peer = lax.rem(me + n - d, n)
        pltpu.make_async_remote_copy(
            src_ref=staged.at[peer],
            dst_ref=part_ref.at[peer],
            send_sem=id_send.at[peer],
            recv_sem=id_recv.at[peer],
            device_id={"obs": peer},
            device_id_type=pl.DeviceIdType.MESH,
        ).wait_recv()
        pltpu.make_async_remote_copy(
            src_ref=sent_ref,
            dst_ref=recv_ref.at[peer],
            send_sem=send_sem.at[peer],
            recv_sem=recv_sem.at[peer],
            device_id={"obs": peer},
            device_id_type=pl.DeviceIdType.MESH,
        ).wait_recv()
    for d in range(1, n):
        ids_copy(d).wait_send()
        rows_copy(d).wait_send()


def normal_rows(camera_point):
    a, b, e = camera_point[0:3], camera_point[3:6], camera_point[6:8]
    return [
        a[0] * a[0] + b[0] * b[0],
        a[0] * a[1] + b[0] * b[1],
        a[0] * a[2] + b[0] * b[2],
        a[1] * a[1] + b[1] * b[1],
        a[1] * a[2] + b[1] * b[2],
        a[2] * a[2] + b[2] * b[2],
        a[0] * e[0] + b[0] * e[1],
        a[1] * e[0] + b[1] * e[1],
        a[2] * e[0] + b[2] * e[1],
    ]


def terms_kernel(
    n, cameras, sent_ref, cam_ref, recv_ref, part_ref, pair_ref, out_ref,
    pairs, rows_of, offset_of, solve, own, factor_of, prod, marks,
):
    ranks = pair_ref.shape[0]
    shift = LANES.bit_length() - 1
    cam = cam_ref[...]
    for j in range(n):
        pairs[pl.ds(j, ranks, stride=n), :] = pair_ref[:, j * LANES : (j + 1) * LANES]
    sources, places, offsets = [], [], []
    for k in range(ranks):
        slot = part_ref[pl.ds(k, n, stride=SUBLANES), :]
        pair = pairs[pl.ds(k * n, n), :]
        sources.append(
            jnp.where(pair == cameras * NBR, -1, lax.shift_right_logical(slot, shift))
        )
        places.append(lax.bitwise_and(slot, LANES - 1))
        offsets.append(pair - cam * NBR)

    def add_source(x, totals):
        place = jnp.zeros((n, LANES), jnp.int32)
        offset = jnp.full((n, LANES), -1, jnp.int32)
        for k in range(ranks):
            match = sources[k] == x
            place = jnp.where(match, places[k], place)
            offset = jnp.where(match, offsets[k], offset)
        offset_of[x] = offset
        found = offset >= 0
        values = []
        for f in range(26):
            value = jnp.where(found, lane_gather(recv_ref[x, f], place), 0.0)
            values.append(value)
            if f < 24:
                rows_of[x, f] = value
        return tuple(t + v for t, v in zip(totals, normal_rows(values[18:26])))

    totals = normal_rows([sent_ref[f] for f in range(18, 26)])
    totals = lax.fori_loop(0, n, add_source, tuple(totals))
    pivot_one = jnp.sqrt(totals[0] + 1.0)
    inv_one = 1.0 / pivot_one
    low_one = totals[1] * inv_one
    low_two = totals[2] * inv_one
    inv_two = 1.0 / jnp.sqrt(totals[3] + 1.0 - low_one * low_one)
    low_mid = (totals[4] - low_two * low_one) * inv_two
    inv_three = 1.0 / jnp.sqrt(totals[5] + 1.0 - low_two * low_two - low_mid * low_mid)
    h_one = totals[6] * inv_one
    h_two = (totals[7] - low_one * h_one) * inv_two
    h_three = (totals[8] - low_two * h_one - low_mid * h_two) * inv_three
    for i, value in enumerate([inv_one, low_one, low_two, inv_two, low_mid, inv_three]):
        solve[i] = value

    def factors(rows):
        tri = [solve[i] for i in range(6)]
        columns = []
        for i in range(2):
            jp = [rows(18 + 3 * i + c) for c in range(3)]
            one = jp[0] * tri[0]
            two = (jp[1] - tri[1] * one) * tri[3]
            three = (jp[2] - tri[2] * one - tri[4] * two) * tri[5]
            columns.append((one, two, three))
        result = [[None] * 9 for _ in range(3)]
        for p in range(9):
            first, second = rows(p), rows(9 + p)
            for c in range(3):
                result[c][p] = first * columns[0][c] + second * columns[1][c]
        return result

    mine = factors(lambda f: sent_ref[f])
    jac = [sent_ref[f] for f in range(18)]
    for c in range(3):
        for p in range(9):
            own[c * 9 + p] = -mine[c][p]
    base = NBR * 81

    def put(row, value):
        prod[pl.ds(row * n, n), :] = value

    for p in range(9):
        for q in range(p, 9):
            value = jac[p] * jac[q] + jac[9 + p] * jac[9 + q]
            value = value - (
                mine[0][p] * mine[0][q] + mine[1][p] * mine[1][q] + mine[2][p] * mine[2][q]
            )
            put(base + 9 * p + q, value)
            if q != p:
                put(base + 9 * q + p, value)
        back = mine[0][p] * h_one + mine[1][p] * h_two + mine[2][p] * h_three
        put(base + 81 + p, jac[p] * sent_ref[24] + jac[9 + p] * sent_ref[25] - back)

    def source_factors(x, carry):
        got = factors(lambda f: rows_of[x, f])
        for c in range(3):
            for p in range(9):
                factor_of[x, c * 9 + p] = got[c][p]
        return carry

    lax.fori_loop(0, n, source_factors, 0)

    def at_offset(o, carry):
        picked = [None] * 27
        for x in range(n):
            match = offset_of[x] == o
            for i in range(27):
                value = jnp.where(match, factor_of[x, i], 0.0)
                picked[i] = value if x == 0 else picked[i] + value
        for p in range(9):
            left = [own[c * 9 + p] for c in range(3)]
            for q in range(9):
                value = left[0] * picked[q] + left[1] * picked[9 + q] + left[2] * picked[18 + q]
                prod[pl.ds((o * 81 + 9 * p + q) * n, n), :] = value
        return carry

    lax.fori_loop(0, NBR, at_offset, 0)

    ids = lax.broadcasted_iota(jnp.int32, (cameras, LANES), 0)
    halves = [
        jnp.where(ids == cam[j : j + 1, :], 1.0, 0.0).astype(jnp.bfloat16) for j in range(n)
    ]
    for i in range(n // 2):
        marks[i] = jnp.concatenate([halves[2 * i], halves[2 * i + 1]], axis=1)
    contract = (((1,), (1,)), ((), ()))
    chunks = out_ref.shape[1] // CHUNK

    for ch in range(chunks):
        total = jnp.zeros((cameras, CHUNK), jnp.float32)
        for i in range(n // 2):
            first = prod[pl.ds(ch * CHUNK * n + 2 * i, CHUNK, stride=n), :]
            second = prod[pl.ds(ch * CHUNK * n + 2 * i + 1, CHUNK, stride=n), :]
            both = jnp.concatenate([first, second], axis=1)
            high = both.astype(jnp.bfloat16)
            low = (both - high.astype(jnp.float32)).astype(jnp.bfloat16)
            for half in (high, low):
                total += lax.dot_general(
                    marks[i], half, contract, preferred_element_type=jnp.float32
                )
        out_ref[:, ch * CHUNK : (ch + 1) * CHUNK] = total


def sum_kernel(n, part_ref, out_ref, landed, send_sem, recv_sem):
    me = lax.axis_index("row")
    rows = out_ref.shape[0]
    barrier = pltpu.get_barrier_semaphore()
    for d in range(1, n):
        pl.semaphore_signal(
            barrier,
            inc=1,
            device_id={"row": lax.rem(me + d, n)},
            device_id_type=pl.DeviceIdType.MESH,
        )
    pl.semaphore_wait(barrier, n - 1)

    def block(peer):
        return part_ref.at[pl.ds(pl.multiple_of(peer * rows, SUBLANES), rows)]

    def copy(peer, slot):
        return pltpu.make_async_remote_copy(
            src_ref=block(peer),
            dst_ref=landed.at[slot],
            send_sem=send_sem.at[peer],
            recv_sem=recv_sem.at[slot],
            device_id={"row": peer},
            device_id_type=pl.DeviceIdType.MESH,
        )

    for d in range(1, n):
        copy(lax.rem(me + d, n), me).start()
    total = part_ref[pl.ds(pl.multiple_of(me * rows, SUBLANES), rows), :]
    for d in range(1, n):
        peer = lax.rem(me + d, n)
        copy(peer, peer).wait_recv()
        total = total + landed[peer]
    out_ref[...] = total
    for d in range(1, n):
        copy(lax.rem(me + d, n), me).wait_send()


def by_lanes(
    camera_jacobian, point_jacobian, residual, send_order, camera_of, track_of, partner, pair_slot
):
    n = lax.axis_size("obs")
    n_row = lax.axis_size("row")
    cameras = CAM_ROW * n_row
    ranks = partner.shape[0]
    width = -(-(NBR * 81 + 90) // CHUNK) * CHUNK
    vmem = pl.BlockSpec(memory_space=pltpu.VMEM)
    f32, i32 = jnp.float32, jnp.int32
    sent, cam = pl.pallas_call(
        permute_kernel,
        out_shape=(
            jax.ShapeDtypeStruct((26, n, LANES), f32),
            jax.ShapeDtypeStruct((n, LANES), i32),
        ),
        in_specs=[vmem] * 5,
        out_specs=(vmem, vmem),
        name="permute",
    )(
        camera_jacobian,
        point_jacobian,
        residual,
        send_order.reshape(n, LANES),
        camera_of.reshape(n, LANES),
    )
    recv, part = pl.pallas_call(
        functools.partial(exchange_kernel, n),
        out_shape=(
            jax.ShapeDtypeStruct((n, 26, n, LANES), f32),
            jax.ShapeDtypeStruct((n, SUBLANES, LANES), i32),
        ),
        in_specs=[vmem] * 2,
        out_specs=(vmem, vmem),
        scratch_shapes=[
            pltpu.VMEM((n, SUBLANES, LANES), i32),
            pltpu.SemaphoreType.DMA((n,)),
            pltpu.SemaphoreType.DMA((n,)),
            pltpu.SemaphoreType.DMA((n,)),
            pltpu.SemaphoreType.DMA((n,)),
        ],
        compiler_params=pltpu.CompilerParams(collective_id=0, has_side_effects=True),
        name="exchange",
    )(sent, partner)
    partial = pl.pallas_call(
        functools.partial(terms_kernel, n, cameras),
        out_shape=jax.ShapeDtypeStruct((cameras, width), f32),
        in_specs=[vmem] * 5,
        out_specs=vmem,
        scratch_shapes=[
            pltpu.VMEM((ranks * n, LANES), i32),
            pltpu.VMEM((n, 24, n, LANES), f32),
            pltpu.VMEM((n, n, LANES), i32),
            pltpu.VMEM((6, n, LANES), f32),
            pltpu.VMEM((27, n, LANES), f32),
            pltpu.VMEM((n, 27, n, LANES), f32),
            pltpu.VMEM((width * n, LANES), f32),
            pltpu.VMEM((n // 2, cameras, 2 * LANES), jnp.bfloat16),
        ],
        compiler_params=pltpu.CompilerParams(vmem_limit_bytes=VMEM_BYTES),
        name="terms",
    )(sent, cam, recv, part.reshape(n * SUBLANES, LANES), pair_slot)
    mine = pl.pallas_call(
        functools.partial(sum_kernel, n_row),
        out_shape=jax.ShapeDtypeStruct((CAM_ROW, width), f32),
        in_specs=[vmem],
        out_specs=vmem,
        scratch_shapes=[
            pltpu.VMEM((n_row, CAM_ROW, width), f32),
            pltpu.SemaphoreType.DMA((n_row,)),
            pltpu.SemaphoreType.DMA((n_row,)),
        ],
        compiler_params=pltpu.CompilerParams(collective_id=1, has_side_effects=True),
        name="row_sum",
    )(partial)
    base = NBR * 81
    pair = mine[:, :base].reshape(CAM_ROW, NBR, 81).transpose(2, 0, 1).reshape(81, CAM_ROW * NBR)
    return (mine[:, base : base + 81].T, mine[:, base + 81 : base + 90].T, pair)


damping = 1.0


def eliminate(camera_rows, point_rows, resid_rows, track_of, track_count):
    camera = camera_rows.reshape(2, 9, -1)
    point_jac = point_rows.reshape(2, 3, -1)
    normal = jnp.stack(
        [
            point_jac[0, 0] * point_jac[0, 0] + point_jac[1, 0] * point_jac[1, 0],
            point_jac[0, 0] * point_jac[0, 1] + point_jac[1, 0] * point_jac[1, 1],
            point_jac[0, 0] * point_jac[0, 2] + point_jac[1, 0] * point_jac[1, 2],
            point_jac[0, 1] * point_jac[0, 1] + point_jac[1, 1] * point_jac[1, 1],
            point_jac[0, 1] * point_jac[0, 2] + point_jac[1, 1] * point_jac[1, 2],
            point_jac[0, 2] * point_jac[0, 2] + point_jac[1, 2] * point_jac[1, 2],
            point_jac[0, 0] * resid_rows[0] + point_jac[1, 0] * resid_rows[1],
            point_jac[0, 1] * resid_rows[0] + point_jac[1, 1] * resid_rows[1],
            point_jac[0, 2] * resid_rows[0] + point_jac[1, 2] * resid_rows[1],
        ]
    )
    totals = jnp.zeros((9, track_count), jnp.float32).at[:, track_of].add(normal)
    pivot_first = jnp.sqrt(totals[0] + damping)
    lower_one = totals[1] / pivot_first
    lower_two = totals[2] / pivot_first
    pivot_second = jnp.sqrt(totals[3] + damping - lower_one * lower_one)
    lower_mid = (totals[4] - lower_two * lower_one) / pivot_second
    pivot_third = jnp.sqrt(totals[5] + damping - lower_two * lower_two - lower_mid * lower_mid)
    solved_one = totals[6] / pivot_first
    solved_two = (totals[7] - lower_one * solved_one) / pivot_second
    solved_three = (totals[8] - lower_two * solved_one - lower_mid * solved_two) / pivot_third
    per_track = jnp.stack(
        [
            pivot_first,
            lower_one,
            lower_two,
            pivot_second,
            lower_mid,
            pivot_third,
            solved_one,
            solved_two,
            solved_three,
        ]
    )
    per_obs = per_track[:, track_of]
    weights = (
        camera[0][:, None, :] * point_jac[0][None, :, :]
        + camera[1][:, None, :] * point_jac[1][None, :, :]
    )
    column_one = weights[:, 0] / per_obs[0]
    column_two = (weights[:, 1] - per_obs[1] * column_one) / per_obs[3]
    column_three = (weights[:, 2] - per_obs[2] * column_one - per_obs[4] * column_two) / per_obs[5]
    factor = jnp.stack([column_one, column_two, column_three])
    point_shift = column_one * per_obs[6] + column_two * per_obs[7] + column_three * per_obs[8]
    return (factor, point_shift)


def camera_terms(camera_rows, resid_rows, factor, point_shift):
    camera = camera_rows.reshape(2, 9, -1)
    normal = (
        camera[0][:, None, :] * camera[0][None, :, :]
        + camera[1][:, None, :] * camera[1][None, :, :]
    )
    schur_part = (
        factor[0][:, None, :] * factor[0][None, :, :]
        + factor[1][:, None, :] * factor[1][None, :, :]
        + factor[2][:, None, :] * factor[2][None, :, :]
    )
    gradient = camera[0] * resid_rows[0] + camera[1] * resid_rows[1] - point_shift
    return jnp.concatenate([(normal - schur_part).reshape(81, -1), gradient], axis=0)


def pair_product(left, right):
    total = (
        left[0][:, None] * right[0][None, :]
        + left[1][:, None] * right[1][None, :]
        + left[2][:, None] * right[2][None, :]
    )
    return -total.reshape(81, -1)


def on_device(
    camera_jacobian, point_jacobian, residual, send_order, camera_of, track_of, partner, pair_slot
):
    obs_count = camera_jacobian.shape[1]
    ranks = partner.shape[0]
    camera_count = CAM_ROW * lax.axis_size("row")
    slot_count = camera_count * NBR
    stacked = jnp.concatenate([camera_jacobian, point_jacobian, residual], axis=0)
    sent = jnp.take(stacked, send_order, axis=1)
    owned = lax.all_to_all(sent, "obs", split_axis=1, concat_axis=1, tiled=True)
    factor, point_shift = eliminate(
        owned[:18], owned[18:24], owned[24:26], track_of, obs_count // 2
    )
    flat_factor = factor.reshape(27, obs_count)
    chosen = jnp.take(flat_factor, partner.reshape(-1), axis=1)
    together = jnp.concatenate(
        [
            flat_factor,
            point_shift,
            chosen.reshape(27, ranks, obs_count).reshape(27 * ranks, obs_count),
        ],
        axis=0,
    )
    back = lax.all_to_all(together, "obs", split_axis=1, concat_axis=1, tiled=True)
    factor_back = back[:27].reshape(3, 9, obs_count)
    shift_back = back[27:36]
    remote = back[36:].reshape(3, 9, ranks, obs_count)
    arrived = pair_product(factor_back[:, :, None, :], remote)
    local_terms = camera_terms(sent[:18], sent[24:26], factor_back, shift_back)
    camera_ids = jnp.take(camera_of, send_order)
    indicator = (camera_ids[:, None] == jnp.arange(camera_count, dtype=jnp.int32)[None, :]).astype(
        jnp.float32
    )
    camera_partial = jnp.dot(
        local_terms, indicator, precision=lax.Precision.HIGHEST, preferred_element_type=jnp.float32
    )
    camera_mine = lax.psum_scatter(camera_partial, "row", scatter_dimension=1, tiled=True)
    pair_total = (
        jnp.zeros((81, slot_count + 1), jnp.float32).at[:, pair_slot.reshape(-1)].add(arrived)
    )
    pair_mine = lax.psum_scatter(pair_total[:, :slot_count], "row", scatter_dimension=1, tiled=True)
    return (camera_mine[:81], camera_mine[81:], pair_mine)


def on_mesh(*arguments):
    share = arguments[0].shape[1] // lax.axis_size("obs")
    if share == LANES and lax.axis_size("obs") % 2 == 0:
        return by_lanes(*arguments)
    return on_device(*arguments)


def solution(mesh):
    return jax.shard_map(
        on_mesh,
        mesh=mesh,
        in_specs=(
            P(None, ("obs", "row")),
            P(None, ("obs", "row")),
            P(None, ("obs", "row")),
            P(("obs", "row")),
            P(("obs", "row")),
            P(("obs", "row")),
            P(None, ("obs", "row")),
            P(None, ("obs", "row")),
        ),
        out_specs=(P(None, ("obs", "row")), P(None, ("obs", "row")), P(None, ("obs", "row"))),
        check_vma=False,
    )
```

```python
import functools

import jax
import jax.numpy as jnp
from jax import lax
from jax.experimental import pallas as pl
from jax.experimental.pallas import tpu as pltpu
from jax.sharding import PartitionSpec as P

CAM_ROW = 16
NBR = 14
LANES = 128
SUBLANES = 8
CHUNK = 256
PACK = 3
PIECES = 2
MESH = pl.DeviceIdType.MESH
VMEM_BYTES = 48 * 1024 * 1024


def lane_gather(values, index):
    return jnp.take_along_axis(values, index, axis=1, mode="promise_in_bounds")


def normal_rows(camera_point):
    a, b, e = camera_point[0:3], camera_point[3:6], camera_point[6:8]
    return [
        a[0] * a[0] + b[0] * b[0],
        a[0] * a[1] + b[0] * b[1],
        a[0] * a[2] + b[0] * b[2],
        a[1] * a[1] + b[1] * b[1],
        a[1] * a[2] + b[1] * b[2],
        a[2] * a[2] + b[2] * b[2],
        a[0] * e[0] + b[0] * e[1],
        a[1] * e[0] + b[1] * e[1],
        a[2] * e[0] + b[2] * e[1],
    ]


def step_kernel(
    n, n_row, cameras,
    camera_ref, point_ref, resid_ref, order_ref, ids_ref, partner_ref, pair_ref,
    hessian_ref, gradient_ref, pair_out_ref,
    rows_in, part, staged, pairs, rows_of, offset_of, solve, own, factor_of, prod, marks,
    partial, landed, turned,
    id_send, id_recv, row_send, row_recv, pass_send, sum_send, sum_recv,
):
    me = lax.axis_index("obs")
    my_row = lax.axis_index("row")
    chips = n // 2
    chip = me // 2
    core = lax.rem(me, 2)
    sibling = chip * 2 + 1 - core
    ranks = partner_ref.shape[0]
    shift = LANES.bit_length() - 1
    size = 26 // PIECES
    chunks = partial.shape[0]

    barrier = pltpu.get_barrier_semaphore()
    for d in range(1, n):
        pl.semaphore_signal(
            barrier, inc=1, device_id={"obs": lax.rem(me + d, n)}, device_id_type=MESH
        )
    for d in range(1, n_row):
        pl.semaphore_signal(
            barrier, inc=1, device_id={"row": lax.rem(my_row + d, n_row)}, device_id_type=MESH
        )

    for x in range(n):
        staged[x] = jnp.zeros((SUBLANES, LANES), jnp.int32)
        staged[x, 0:ranks] = partner_ref[:, x * LANES : (x + 1) * LANES]

    def ids_copy(peer, source):
        return pltpu.make_async_remote_copy(
            src_ref=staged.at[peer],
            dst_ref=part.at[pl.ds(pl.multiple_of(source * SUBLANES, SUBLANES), SUBLANES)],
            send_sem=id_send.at[peer],
            recv_sem=id_recv.at[source],
            device_id={"obs": peer},
            device_id_type=MESH,
        )

    def rows_copy(source, piece, peer, sem):
        block = rows_in.at[source, pl.ds(piece * size, size)]
        return pltpu.make_async_remote_copy(
            src_ref=block,
            dst_ref=block,
            send_sem=sem.at[peer if sem is row_send else source, piece],
            recv_sem=row_recv.at[source, piece],
            device_id={"obs": peer},
            device_id_type=MESH,
        )

    def twin(d):
        return lax.rem(chip + d, chips) * 2 + core

    order = order_ref[...]
    block_of = lax.shift_right_logical(order, shift)
    lane_of = lax.bitwise_and(order, LANES - 1)

    def permuted(row_of_block):
        total = None
        for b in range(n):
            row = jnp.broadcast_to(row_of_block(b), (n, LANES))
            picked = lane_gather(row, lane_of)
            total = picked if b == 0 else jnp.where(block_of == b, picked, total)
        return total

    table = [(point_ref, f) for f in range(6)] + [(resid_ref, f) for f in range(2)]
    table = table + [(camera_ref, f) for f in range(18)]
    targets = [twin(d) for d in range(1, chips)] + [sibling]
    for piece in range(PIECES):
        for f in range(piece * size, (piece + 1) * size):
            ref, r = table[f]
            rows_in[me, f] = permuted(lambda b: ref[r : r + 1, b * LANES : (b + 1) * LANES])
        if piece == 0:
            pl.semaphore_wait(barrier, n - 1 + n_row - 1)
        for peer in targets:
            rows_copy(me, piece, peer, row_send).start()
        if piece == 0:
            for d in range(1, n):
                ids_copy(lax.rem(me + d, n), me).start()
    part[pl.ds(pl.multiple_of(me * SUBLANES, SUBLANES), SUBLANES), :] = staged[me]

    cam = permuted(lambda b: ids_ref[b : b + 1, :])
    ids = lax.broadcasted_iota(jnp.int32, (cameras, LANES), 0)
    halves = [
        jnp.where(ids == cam[j : j + 1, :], 1.0, 0.0).astype(jnp.bfloat16) for j in range(n)
    ]
    for i in range(n // 2):
        marks[i] = jnp.concatenate([halves[2 * i], halves[2 * i + 1]], axis=1)
    for j in range(n):
        pairs[pl.ds(j, ranks, stride=n), :] = pair_ref[:, j * LANES : (j + 1) * LANES]
    turned[...] = jnp.zeros_like(turned)
    pair_out_ref[...] = jnp.zeros_like(pair_out_ref)

    for d in range(1, n):
        peer = lax.rem(me + d, n)
        ids_copy(peer, peer).wait_recv()
    sources, places, offsets = [], [], []
    for k in range(ranks):
        slot = part[pl.ds(k, n, stride=SUBLANES), :]
        pair = pairs[pl.ds(k * n, n), :]
        sources.append(
            jnp.where(pair == cameras * NBR, -1, lax.shift_right_logical(slot, shift))
        )
        places.append(lax.bitwise_and(slot, LANES - 1))
        offsets.append(pair - cam * NBR)

    for d in range(1, chips):
        for piece in range(PIECES):
            rows_copy(twin(d), piece, sibling, row_send).wait_recv()
            rows_copy(twin(d), piece, sibling, pass_send).start()
    for piece in range(PIECES):
        rows_copy(sibling, piece, sibling, row_send).wait_recv()

    def add_source(t, totals):
        x = lax.rem(chip + t // 2, chips) * 2 + lax.rem(core + t, 2)

        @pl.when(jnp.logical_and(lax.rem(t, 2) == 1, t > 1))
        def _():
            for piece in range(PIECES):
                rows_copy(x, piece, sibling, pass_send).wait_recv()

        place = jnp.zeros((n, LANES), jnp.int32)
        offset = jnp.full((n, LANES), -1, jnp.int32)
        for k in range(ranks):
            match = sources[k] == x
            place = jnp.where(match, places[k], place)
            offset = jnp.where(match, offsets[k], offset)
        offset_of[t] = offset
        found = offset >= 0
        values = []
        for f in range(26):
            value = jnp.where(found, lane_gather(rows_in[x, f], place), 0.0)
            rows_of[t, f] = value
            values.append(value)
        return tuple(t + v for t, v in zip(totals, normal_rows(values[0:8])))

    totals = normal_rows([rows_in[me, f] for f in range(8)])
    totals = lax.fori_loop(0, n, add_source, tuple(totals))
    pivot_one = jnp.sqrt(totals[0] + 1.0)
    inv_one = 1.0 / pivot_one
    low_one = totals[1] * inv_one
    low_two = totals[2] * inv_one
    inv_two = 1.0 / jnp.sqrt(totals[3] + 1.0 - low_one * low_one)
    low_mid = (totals[4] - low_two * low_one) * inv_two
    inv_three = 1.0 / jnp.sqrt(totals[5] + 1.0 - low_two * low_two - low_mid * low_mid)
    h_one = totals[6] * inv_one
    h_two = (totals[7] - low_one * h_one) * inv_two
    h_three = (totals[8] - low_two * h_one - low_mid * h_two) * inv_three
    for i, value in enumerate([inv_one, low_one, low_two, inv_two, low_mid, inv_three]):
        solve[i] = value

    def factors(rows):
        tri = [solve[i] for i in range(6)]
        columns = []
        for i in range(2):
            jp = [rows(3 * i + c) for c in range(3)]
            one = jp[0] * tri[0]
            two = (jp[1] - tri[1] * one) * tri[3]
            three = (jp[2] - tri[2] * one - tri[4] * two) * tri[5]
            columns.append((one, two, three))
        result = [[None] * 9 for _ in range(3)]
        for p in range(9):
            first, second = rows(8 + p), rows(17 + p)
            for c in range(3):
                result[c][p] = first * columns[0][c] + second * columns[1][c]
        return result

    mine = factors(lambda f: rows_in[me, f])
    jac = [rows_in[me, 8 + f] for f in range(18)]
    for c in range(3):
        for p in range(9):
            own[c * 9 + p] = -mine[c][p]
    last = chunks - 1
    base = last * CHUNK + (NBR - last * PACK) * 81

    def put(row, value):
        prod[pl.ds(row * n, n), :] = value

    for p in range(9):
        for q in range(p, 9):
            value = jac[p] * jac[q] + jac[9 + p] * jac[9 + q]
            value = value - (
                mine[0][p] * mine[0][q] + mine[1][p] * mine[1][q] + mine[2][p] * mine[2][q]
            )
            put(base + 9 * p + q, value)
            if q != p:
                put(base + 9 * q + p, value)
        back = mine[0][p] * h_one + mine[1][p] * h_two + mine[2][p] * h_three
        put(base + 81 + p, jac[p] * rows_in[me, 6] + jac[9 + p] * rows_in[me, 7] - back)

    def source_factors(x, carry):
        got = factors(lambda f: rows_of[x, f])
        for c in range(3):
            for p in range(9):
                factor_of[x, c * 9 + p] = got[c][p]
        return carry

    lax.fori_loop(0, n, source_factors, 0)

    def at_offset(o, row):
        picked = [None] * 27
        for x in range(n):
            match = offset_of[x] == o
            for i in range(27):
                value = jnp.where(match, factor_of[x, i], 0.0)
                picked[i] = value if x == 0 else picked[i] + value
        for p in range(9):
            left = [own[c * 9 + p] for c in range(3)]
            for q in range(9):
                value = left[0] * picked[q] + left[1] * picked[9 + q] + left[2] * picked[18 + q]
                prod[pl.ds(pl.multiple_of((row + 9 * p + q) * n, n), n), :] = value

    contract = (((1,), (1,)), ((), ()))

    def sum_copy(peer, slot, chunk):
        return pltpu.make_async_remote_copy(
            src_ref=partial.at[chunk, pl.ds(pl.multiple_of(peer * CAM_ROW, CAM_ROW), CAM_ROW)],
            dst_ref=landed.at[slot, chunk],
            send_sem=sum_send.at[peer, chunk],
            recv_sem=sum_recv.at[slot, chunk],
            device_id={"row": peer},
            device_id_type=MESH,
        )

    def chunk_step(chunk, carry):
        def offset_step(i, inner):
            at_offset(chunk * PACK + i, chunk * CHUNK + i * 81)
            return inner

        lax.fori_loop(0, jnp.minimum(PACK, NBR - chunk * PACK), offset_step, 0)
        total = jnp.zeros((cameras, CHUNK), jnp.float32)
        for i in range(n // 2):
            start = chunk * (CHUNK * n) + 2 * i
            first = prod[pl.ds(start, CHUNK, stride=n), :]
            second = prod[pl.ds(start + 1, CHUNK, stride=n), :]
            both = jnp.concatenate([first, second], axis=1)
            high = both.astype(jnp.bfloat16)
            low = (both - high.astype(jnp.float32)).astype(jnp.bfloat16)
            for half in (high, low):
                total += lax.dot_general(
                    marks[i], half, contract, preferred_element_type=jnp.float32
                )
        partial[chunk] = total
        for d in range(1, n_row):
            sum_copy(lax.rem(my_row + d, n_row), my_row, chunk).start()
        return carry

    lax.fori_loop(0, chunks, chunk_step, 0)

    slots = pair_out_ref.shape[1]
    lane = lax.broadcasted_iota(jnp.int32, (LANES, slots), 1)
    line = lax.broadcasted_iota(jnp.int32, (LANES, slots), 0)
    for chunk in range(chunks):
        total = partial[chunk, pl.ds(pl.multiple_of(my_row * CAM_ROW, CAM_ROW), CAM_ROW), :]
        for d in range(1, n_row):
            peer = lax.rem(my_row + d, n_row)
            sum_copy(peer, peer, chunk).wait_recv()
            total = total + landed[peer, chunk]
        count = min(PACK, NBR - chunk * PACK)
        for i in range(count):
            turned[i * CAM_ROW : (i + 1) * CAM_ROW, 0:81] = total[:, i * 81 : (i + 1) * 81]
        if chunk == last:
            turned[count * CAM_ROW : (count + 1) * CAM_ROW, 0:90] = total[
                :, count * 81 : count * 81 + 90
            ]
        flipped = turned[...].T
        offset = chunk * PACK + line // CAM_ROW
        chosen = jnp.logical_and(
            lane == lax.rem(line, CAM_ROW) * NBR + offset, line < count * CAM_ROW
        )
        select = jnp.where(chosen, 1.0, 0.0).astype(jnp.bfloat16)
        rows = flipped[0:88]
        high = rows.astype(jnp.bfloat16)
        low = (rows - high.astype(jnp.float32)).astype(jnp.bfloat16)
        placed = jnp.dot(high, select, preferred_element_type=jnp.float32)
        placed = placed + jnp.dot(low, select, preferred_element_type=jnp.float32)
        pair_out_ref[...] += placed[0:81]
        if chunk == last:
            mine_lanes = flipped[:, count * CAM_ROW : (count + 1) * CAM_ROW]
            hessian_ref[...] = mine_lanes[0:81]
            gradient_ref[...] = mine_lanes[81:90]

    for d in range(1, n):
        ids_copy(lax.rem(me + d, n), me).wait_send()
    for piece in range(PIECES):
        for peer in targets:
            rows_copy(me, piece, peer, row_send).wait_send()
        for d in range(1, chips):
            rows_copy(twin(d), piece, sibling, pass_send).wait_send()
    for chunk in range(chunks):
        for d in range(1, n_row):
            sum_copy(lax.rem(my_row + d, n_row), my_row, chunk).wait_send()


def by_lanes(
    camera_jacobian, point_jacobian, residual, send_order, camera_of, track_of, partner, pair_slot
):
    n = lax.axis_size("obs")
    n_row = lax.axis_size("row")
    cameras = CAM_ROW * n_row
    ranks = partner.shape[0]
    chunks = -(-NBR // PACK)
    vmem = pl.BlockSpec(memory_space=pltpu.VMEM)
    f32, i32 = jnp.float32, jnp.int32
    dma = pltpu.SemaphoreType.DMA
    return pl.pallas_call(
        functools.partial(step_kernel, n, n_row, cameras),
        out_shape=(
            jax.ShapeDtypeStruct((81, CAM_ROW), f32),
            jax.ShapeDtypeStruct((9, CAM_ROW), f32),
            jax.ShapeDtypeStruct((81, CAM_ROW * NBR), f32),
        ),
        in_specs=[vmem] * 7,
        out_specs=(vmem, vmem, vmem),
        scratch_shapes=[
            pltpu.VMEM((n, 26, n, LANES), f32),
            pltpu.VMEM((n * SUBLANES, LANES), i32),
            pltpu.VMEM((n, SUBLANES, LANES), i32),
            pltpu.VMEM((ranks * n, LANES), i32),
            pltpu.VMEM((n, 26, n, LANES), f32),
            pltpu.VMEM((n, n, LANES), i32),
            pltpu.VMEM((6, n, LANES), f32),
            pltpu.VMEM((27, n, LANES), f32),
            pltpu.VMEM((n, 27, n, LANES), f32),
            pltpu.VMEM((chunks * CHUNK * n, LANES), f32),
            pltpu.VMEM((n // 2, cameras, 2 * LANES), jnp.bfloat16),
            pltpu.VMEM((chunks, cameras, CHUNK), f32),
            pltpu.VMEM((n_row, chunks, CAM_ROW, CHUNK), f32),
            pltpu.VMEM((LANES, LANES), f32),
            dma((n,)),
            dma((n,)),
            dma((n, PIECES)),
            dma((n, PIECES)),
            dma((n, PIECES)),
            dma((n_row, chunks)),
            dma((n_row, chunks)),
        ],
        compiler_params=pltpu.CompilerParams(
            collective_id=0, has_side_effects=True, vmem_limit_bytes=VMEM_BYTES
        ),
        name="gauss_newton_step",
    )(
        camera_jacobian,
        point_jacobian,
        residual,
        send_order.reshape(n, LANES),
        camera_of.reshape(n, LANES),
        partner,
        pair_slot,
    )


damping = 1.0


def eliminate(camera_rows, point_rows, resid_rows, track_of, track_count):
    camera = camera_rows.reshape(2, 9, -1)
    point_jac = point_rows.reshape(2, 3, -1)
    normal = jnp.stack(
        [
            point_jac[0, 0] * point_jac[0, 0] + point_jac[1, 0] * point_jac[1, 0],
            point_jac[0, 0] * point_jac[0, 1] + point_jac[1, 0] * point_jac[1, 1],
            point_jac[0, 0] * point_jac[0, 2] + point_jac[1, 0] * point_jac[1, 2],
            point_jac[0, 1] * point_jac[0, 1] + point_jac[1, 1] * point_jac[1, 1],
            point_jac[0, 1] * point_jac[0, 2] + point_jac[1, 1] * point_jac[1, 2],
            point_jac[0, 2] * point_jac[0, 2] + point_jac[1, 2] * point_jac[1, 2],
            point_jac[0, 0] * resid_rows[0] + point_jac[1, 0] * resid_rows[1],
            point_jac[0, 1] * resid_rows[0] + point_jac[1, 1] * resid_rows[1],
            point_jac[0, 2] * resid_rows[0] + point_jac[1, 2] * resid_rows[1],
        ]
    )
    totals = jnp.zeros((9, track_count), jnp.float32).at[:, track_of].add(normal)
    pivot_first = jnp.sqrt(totals[0] + damping)
    lower_one = totals[1] / pivot_first
    lower_two = totals[2] / pivot_first
    pivot_second = jnp.sqrt(totals[3] + damping - lower_one * lower_one)
    lower_mid = (totals[4] - lower_two * lower_one) / pivot_second
    pivot_third = jnp.sqrt(totals[5] + damping - lower_two * lower_two - lower_mid * lower_mid)
    solved_one = totals[6] / pivot_first
    solved_two = (totals[7] - lower_one * solved_one) / pivot_second
    solved_three = (totals[8] - lower_two * solved_one - lower_mid * solved_two) / pivot_third
    per_track = jnp.stack(
        [
            pivot_first,
            lower_one,
            lower_two,
            pivot_second,
            lower_mid,
            pivot_third,
            solved_one,
            solved_two,
            solved_three,
        ]
    )
    per_obs = per_track[:, track_of]
    weights = (
        camera[0][:, None, :] * point_jac[0][None, :, :]
        + camera[1][:, None, :] * point_jac[1][None, :, :]
    )
    column_one = weights[:, 0] / per_obs[0]
    column_two = (weights[:, 1] - per_obs[1] * column_one) / per_obs[3]
    column_three = (weights[:, 2] - per_obs[2] * column_one - per_obs[4] * column_two) / per_obs[5]
    factor = jnp.stack([column_one, column_two, column_three])
    point_shift = column_one * per_obs[6] + column_two * per_obs[7] + column_three * per_obs[8]
    return (factor, point_shift)


def camera_terms(camera_rows, resid_rows, factor, point_shift):
    camera = camera_rows.reshape(2, 9, -1)
    normal = (
        camera[0][:, None, :] * camera[0][None, :, :]
        + camera[1][:, None, :] * camera[1][None, :, :]
    )
    schur_part = (
        factor[0][:, None, :] * factor[0][None, :, :]
        + factor[1][:, None, :] * factor[1][None, :, :]
        + factor[2][:, None, :] * factor[2][None, :, :]
    )
    gradient = camera[0] * resid_rows[0] + camera[1] * resid_rows[1] - point_shift
    return jnp.concatenate([(normal - schur_part).reshape(81, -1), gradient], axis=0)


def pair_product(left, right):
    total = (
        left[0][:, None] * right[0][None, :]
        + left[1][:, None] * right[1][None, :]
        + left[2][:, None] * right[2][None, :]
    )
    return -total.reshape(81, -1)


def on_device(
    camera_jacobian, point_jacobian, residual, send_order, camera_of, track_of, partner, pair_slot
):
    obs_count = camera_jacobian.shape[1]
    ranks = partner.shape[0]
    camera_count = CAM_ROW * lax.axis_size("row")
    slot_count = camera_count * NBR
    stacked = jnp.concatenate([camera_jacobian, point_jacobian, residual], axis=0)
    sent = jnp.take(stacked, send_order, axis=1)
    owned = lax.all_to_all(sent, "obs", split_axis=1, concat_axis=1, tiled=True)
    factor, point_shift = eliminate(
        owned[:18], owned[18:24], owned[24:26], track_of, obs_count // 2
    )
    flat_factor = factor.reshape(27, obs_count)
    chosen = jnp.take(flat_factor, partner.reshape(-1), axis=1)
    together = jnp.concatenate(
        [
            flat_factor,
            point_shift,
            chosen.reshape(27, ranks, obs_count).reshape(27 * ranks, obs_count),
        ],
        axis=0,
    )
    back = lax.all_to_all(together, "obs", split_axis=1, concat_axis=1, tiled=True)
    factor_back = back[:27].reshape(3, 9, obs_count)
    shift_back = back[27:36]
    remote = back[36:].reshape(3, 9, ranks, obs_count)
    arrived = pair_product(factor_back[:, :, None, :], remote)
    local_terms = camera_terms(sent[:18], sent[24:26], factor_back, shift_back)
    camera_ids = jnp.take(camera_of, send_order)
    indicator = (camera_ids[:, None] == jnp.arange(camera_count, dtype=jnp.int32)[None, :]).astype(
        jnp.float32
    )
    camera_partial = jnp.dot(
        local_terms, indicator, precision=lax.Precision.HIGHEST, preferred_element_type=jnp.float32
    )
    camera_mine = lax.psum_scatter(camera_partial, "row", scatter_dimension=1, tiled=True)
    pair_total = (
        jnp.zeros((81, slot_count + 1), jnp.float32).at[:, pair_slot.reshape(-1)].add(arrived)
    )
    pair_mine = lax.psum_scatter(pair_total[:, :slot_count], "row", scatter_dimension=1, tiled=True)
    return (camera_mine[:81], camera_mine[81:], pair_mine)


def on_mesh(*arguments):
    share = arguments[0].shape[1] // lax.axis_size("obs")
    if share == LANES and lax.axis_size("obs") % 2 == 0:
        return by_lanes(*arguments)
    return on_device(*arguments)


def solution(mesh):
    return jax.shard_map(
        on_mesh,
        mesh=mesh,
        in_specs=(
            P(None, ("obs", "row")),
            P(None, ("obs", "row")),
            P(None, ("obs", "row")),
            P(("obs", "row")),
            P(("obs", "row")),
            P(("obs", "row")),
            P(None, ("obs", "row")),
            P(None, ("obs", "row")),
        ),
        out_specs=(P(None, ("obs", "row")), P(None, ("obs", "row")), P(None, ("obs", "row"))),
        check_vma=False,
    )
```

```python
import functools

import jax
import jax.numpy as jnp
from jax import lax
from jax.experimental import pallas as pl
from jax.experimental.pallas import tpu as pltpu
from jax.sharding import PartitionSpec as P

CAM_ROW = 16
NBR = 14
LANES = 128
SUBLANES = 8
CHUNK = 256
PACK = 3
PIECES = 2
MESH = pl.DeviceIdType.MESH
VMEM_BYTES = 64 * 1024 * 1024


def lane_gather(values, index):
    return jnp.take_along_axis(values, index, axis=1, mode="promise_in_bounds")


def normal_rows(camera_point):
    a, b, e = camera_point[0:3], camera_point[3:6], camera_point[6:8]
    return [
        a[0] * a[0] + b[0] * b[0],
        a[0] * a[1] + b[0] * b[1],
        a[0] * a[2] + b[0] * b[2],
        a[1] * a[1] + b[1] * b[1],
        a[1] * a[2] + b[1] * b[2],
        a[2] * a[2] + b[2] * b[2],
        a[0] * e[0] + b[0] * e[1],
        a[1] * e[0] + b[1] * e[1],
        a[2] * e[0] + b[2] * e[1],
    ]


def step_kernel(
    n, n_row, cameras,
    camera_in, point_in, resid_in, order_in, ids_in, partner_in, pair_in,
    hessian_ref, gradient_ref, pair_out_ref,
    camera_ref, point_ref, resid_ref, order_ref, ids_ref, partner_ref, pair_ref, load_sem,
    rows_in, part, staged, pairs, rows_of, offset_of, solve, own, factor_of, prod, marks,
    partial, landed, turned,
    id_send, id_recv, row_send, row_recv, pass_send, sum_send, sum_recv,
):
    me = lax.axis_index("obs")
    my_row = lax.axis_index("row")
    chips = n // 2
    chip = me // 2
    core = lax.rem(me, 2)
    sibling = chip * 2 + 1 - core
    ranks = partner_ref.shape[0]
    shift = LANES.bit_length() - 1
    size = 26 // PIECES
    chunks = partial.shape[0]

    moves = [
        pltpu.make_async_copy(source, target, load_sem.at[i])
        for i, (source, target) in enumerate(
            [
                (order_in, order_ref),
                (point_in, point_ref),
                (resid_in, resid_ref),
                (camera_in, camera_ref),
                (partner_in, partner_ref),
                (ids_in, ids_ref),
                (pair_in, pair_ref),
            ]
        )
    ]
    for move in moves:
        move.start()
    barrier = pltpu.get_barrier_semaphore()
    for d in range(1, n):
        pl.semaphore_signal(
            barrier, inc=1, device_id={"obs": lax.rem(me + d, n)}, device_id_type=MESH
        )
    for d in range(1, n_row):
        pl.semaphore_signal(
            barrier, inc=1, device_id={"row": lax.rem(my_row + d, n_row)}, device_id_type=MESH
        )

    def ids_copy(peer, source):
        return pltpu.make_async_remote_copy(
            src_ref=staged.at[peer],
            dst_ref=part.at[pl.ds(pl.multiple_of(source * SUBLANES, SUBLANES), SUBLANES)],
            send_sem=id_send.at[peer],
            recv_sem=id_recv.at[source],
            device_id={"obs": peer},
            device_id_type=MESH,
        )

    def rows_copy(source, piece, peer, sem):
        block = rows_in.at[source, pl.ds(piece * size, size)]
        return pltpu.make_async_remote_copy(
            src_ref=block,
            dst_ref=block,
            send_sem=sem.at[peer if sem is row_send else source, piece],
            recv_sem=row_recv.at[source, piece],
            device_id={"obs": peer},
            device_id_type=MESH,
        )

    def twin(d):
        return lax.rem(chip + d, chips) * 2 + core

    for move in moves[:4]:
        move.wait()
    order = order_ref[...]
    block_of = lax.shift_right_logical(order, shift)
    lane_of = lax.bitwise_and(order, LANES - 1)

    def permuted(row_of_block):
        total = None
        for b in range(n):
            row = jnp.broadcast_to(row_of_block(b), (n, LANES))
            picked = lane_gather(row, lane_of)
            total = picked if b == 0 else jnp.where(block_of == b, picked, total)
        return total

    table = [(point_ref, f) for f in range(6)] + [(resid_ref, f) for f in range(2)]
    table = table + [(camera_ref, f) for f in range(18)]
    targets = [twin(d) for d in range(1, chips)] + [sibling]
    for piece in range(PIECES):
        for f in range(piece * size, (piece + 1) * size):
            ref, r = table[f]
            rows_in[me, f] = permuted(lambda b: ref[r : r + 1, b * LANES : (b + 1) * LANES])
        if piece == 0:
            pl.semaphore_wait(barrier, n - 1 + n_row - 1)
        for peer in targets:
            rows_copy(me, piece, peer, row_send).start()
        if piece == 0:
            for move in moves[4:]:
                move.wait()
            for x in range(n):
                staged[x] = jnp.zeros((SUBLANES, LANES), jnp.int32)
                staged[x, 0:ranks] = partner_ref[:, x * LANES : (x + 1) * LANES]
            for d in range(1, n):
                ids_copy(lax.rem(me + d, n), me).start()
    part[pl.ds(pl.multiple_of(me * SUBLANES, SUBLANES), SUBLANES), :] = staged[me]

    cam = permuted(lambda b: ids_ref[b : b + 1, :])
    ids = lax.broadcasted_iota(jnp.int32, (cameras, LANES), 0)
    halves = [
        jnp.where(ids == cam[j : j + 1, :], 1.0, 0.0).astype(jnp.bfloat16) for j in range(n)
    ]
    for i in range(n // 2):
        marks[i] = jnp.concatenate([halves[2 * i], halves[2 * i + 1]], axis=1)
    for j in range(n):
        pairs[pl.ds(j, ranks, stride=n), :] = pair_ref[:, j * LANES : (j + 1) * LANES]
    turned[...] = jnp.zeros_like(turned)
    pair_out_ref[...] = jnp.zeros_like(pair_out_ref)

    for d in range(1, n):
        peer = lax.rem(me + d, n)
        ids_copy(peer, peer).wait_recv()
    sources, places, offsets = [], [], []
    for k in range(ranks):
        slot = part[pl.ds(k, n, stride=SUBLANES), :]
        pair = pairs[pl.ds(k * n, n), :]
        sources.append(
            jnp.where(pair == cameras * NBR, -1, lax.shift_right_logical(slot, shift))
        )
        places.append(lax.bitwise_and(slot, LANES - 1))
        offsets.append(pair - cam * NBR)

    def add_source(x, totals):
        place = jnp.zeros((n, LANES), jnp.int32)
        offset = jnp.full((n, LANES), -1, jnp.int32)
        for k in range(ranks):
            match = sources[k] == x
            place = jnp.where(match, places[k], place)
            offset = jnp.where(match, offsets[k], offset)
        offset_of[x] = offset
        found = offset >= 0
        values = []
        for f in range(26):
            value = jnp.where(found, lane_gather(rows_in[x, f], place), 0.0)
            rows_of[x, f] = value
            values.append(value)
        return tuple(t + v for t, v in zip(totals, normal_rows(values[0:8])))

    totals = normal_rows([rows_in[me, f] for f in range(8)])
    totals = add_source(me, tuple(totals))
    for piece in range(PIECES):
        rows_copy(sibling, piece, sibling, row_send).wait_recv()
    totals = add_source(sibling, totals)
    for piece in range(PIECES):
        for d in range(1, chips):
            rows_copy(twin(d), piece, sibling, row_send).wait_recv()
            rows_copy(twin(d), piece, sibling, pass_send).start()
    totals = lax.fori_loop(1, chips, lambda d, t: add_source(twin(d), t), totals)

    def add_passed(d, totals):
        x = lax.rem(chip + d, chips) * 2 + 1 - core
        for piece in range(PIECES):
            rows_copy(x, piece, sibling, pass_send).wait_recv()
        return add_source(x, totals)

    totals = lax.fori_loop(1, chips, add_passed, totals)
    pivot_one = jnp.sqrt(totals[0] + 1.0)
    inv_one = 1.0 / pivot_one
    low_one = totals[1] * inv_one
    low_two = totals[2] * inv_one
    inv_two = 1.0 / jnp.sqrt(totals[3] + 1.0 - low_one * low_one)
    low_mid = (totals[4] - low_two * low_one) * inv_two
    inv_three = 1.0 / jnp.sqrt(totals[5] + 1.0 - low_two * low_two - low_mid * low_mid)
    h_one = totals[6] * inv_one
    h_two = (totals[7] - low_one * h_one) * inv_two
    h_three = (totals[8] - low_two * h_one - low_mid * h_two) * inv_three
    for i, value in enumerate([inv_one, low_one, low_two, inv_two, low_mid, inv_three]):
        solve[i] = value

    def factors(rows):
        tri = [solve[i] for i in range(6)]
        columns = []
        for i in range(2):
            jp = [rows(3 * i + c) for c in range(3)]
            one = jp[0] * tri[0]
            two = (jp[1] - tri[1] * one) * tri[3]
            three = (jp[2] - tri[2] * one - tri[4] * two) * tri[5]
            columns.append((one, two, three))
        result = [[None] * 9 for _ in range(3)]
        for p in range(9):
            first, second = rows(8 + p), rows(17 + p)
            for c in range(3):
                result[c][p] = first * columns[0][c] + second * columns[1][c]
        return result

    mine = factors(lambda f: rows_in[me, f])
    jac = [rows_in[me, 8 + f] for f in range(18)]
    for c in range(3):
        for p in range(9):
            own[c * 9 + p] = -mine[c][p]
    last = chunks - 1
    base = last * CHUNK + (NBR - last * PACK) * 81

    def put(row, value):
        prod[pl.ds(row * n, n), :] = value

    for p in range(9):
        for q in range(p, 9):
            value = jac[p] * jac[q] + jac[9 + p] * jac[9 + q]
            value = value - (
                mine[0][p] * mine[0][q] + mine[1][p] * mine[1][q] + mine[2][p] * mine[2][q]
            )
            put(base + 9 * p + q, value)
            if q != p:
                put(base + 9 * q + p, value)
        back = mine[0][p] * h_one + mine[1][p] * h_two + mine[2][p] * h_three
        put(base + 81 + p, jac[p] * rows_in[me, 6] + jac[9 + p] * rows_in[me, 7] - back)

    def source_factors(x, carry):
        got = factors(lambda f: rows_of[x, f])
        for c in range(3):
            for p in range(9):
                factor_of[x, c * 9 + p] = got[c][p]
        return carry

    lax.fori_loop(0, n, source_factors, 0)

    def at_offset(o, row):
        picked = [None] * 27
        for x in range(n):
            match = offset_of[x] == o
            for i in range(27):
                value = jnp.where(match, factor_of[x, i], 0.0)
                picked[i] = value if x == 0 else picked[i] + value
        for p in range(9):
            left = [own[c * 9 + p] for c in range(3)]
            for q in range(9):
                value = left[0] * picked[q] + left[1] * picked[9 + q] + left[2] * picked[18 + q]
                prod[pl.ds(pl.multiple_of((row + 9 * p + q) * n, n), n), :] = value

    contract = (((1,), (1,)), ((), ()))

    def sum_copy(peer, slot, chunk):
        return pltpu.make_async_remote_copy(
            src_ref=partial.at[chunk, pl.ds(pl.multiple_of(peer * CAM_ROW, CAM_ROW), CAM_ROW)],
            dst_ref=landed.at[slot, chunk],
            send_sem=sum_send.at[peer, chunk],
            recv_sem=sum_recv.at[slot, chunk],
            device_id={"row": peer},
            device_id_type=MESH,
        )

    def chunk_step(chunk, carry):
        def offset_step(i, inner):
            at_offset(chunk * PACK + i, chunk * CHUNK + i * 81)
            return inner

        lax.fori_loop(0, jnp.minimum(PACK, NBR - chunk * PACK), offset_step, 0)
        total = jnp.zeros((cameras, CHUNK), jnp.float32)
        for i in range(n // 2):
            start = chunk * (CHUNK * n) + 2 * i
            first = prod[pl.ds(start, CHUNK, stride=n), :]
            second = prod[pl.ds(start + 1, CHUNK, stride=n), :]
            both = jnp.concatenate([first, second], axis=1)
            high = both.astype(jnp.bfloat16)
            low = (both - high.astype(jnp.float32)).astype(jnp.bfloat16)
            for half in (high, low):
                total += lax.dot_general(
                    marks[i], half, contract, preferred_element_type=jnp.float32
                )
        partial[chunk] = total
        for d in range(1, n_row):
            sum_copy(lax.rem(my_row + d, n_row), my_row, chunk).start()
        return carry

    lax.fori_loop(0, chunks, chunk_step, 0)

    slots = pair_out_ref.shape[1]
    lane = lax.broadcasted_iota(jnp.int32, (LANES, slots), 1)
    line = lax.broadcasted_iota(jnp.int32, (LANES, slots), 0)
    for chunk in range(chunks):
        total = partial[chunk, pl.ds(pl.multiple_of(my_row * CAM_ROW, CAM_ROW), CAM_ROW), :]
        for d in range(1, n_row):
            peer = lax.rem(my_row + d, n_row)
            sum_copy(peer, peer, chunk).wait_recv()
            total = total + landed[peer, chunk]
        count = min(PACK, NBR - chunk * PACK)
        for i in range(count):
            turned[i * CAM_ROW : (i + 1) * CAM_ROW, 0:81] = total[:, i * 81 : (i + 1) * 81]
        if chunk == last:
            turned[count * CAM_ROW : (count + 1) * CAM_ROW, 0:90] = total[
                :, count * 81 : count * 81 + 90
            ]
        flipped = turned[...].T
        offset = chunk * PACK + line // CAM_ROW
        chosen = jnp.logical_and(
            lane == lax.rem(line, CAM_ROW) * NBR + offset, line < count * CAM_ROW
        )
        select = jnp.where(chosen, 1.0, 0.0).astype(jnp.bfloat16)
        rows = flipped[0:88]
        high = rows.astype(jnp.bfloat16)
        low = (rows - high.astype(jnp.float32)).astype(jnp.bfloat16)
        placed = jnp.dot(high, select, preferred_element_type=jnp.float32)
        placed = placed + jnp.dot(low, select, preferred_element_type=jnp.float32)
        pair_out_ref[...] += placed[0:81]
        if chunk == last:
            mine_lanes = flipped[:, count * CAM_ROW : (count + 1) * CAM_ROW]
            hessian_ref[...] = total[:, count * 81 : count * 81 + 81]
            gradient_ref[...] = mine_lanes[81:90]

    for d in range(1, n):
        ids_copy(lax.rem(me + d, n), me).wait_send()
    for piece in range(PIECES):
        for peer in targets:
            rows_copy(me, piece, peer, row_send).wait_send()
        for d in range(1, chips):
            rows_copy(twin(d), piece, sibling, pass_send).wait_send()
    for chunk in range(chunks):
        for d in range(1, n_row):
            sum_copy(lax.rem(my_row + d, n_row), my_row, chunk).wait_send()


def store_kernel(*refs):
    copies = [
        pltpu.make_async_copy(refs[i], refs[3 + i], refs[6].at[i]) for i in range(3)
    ]
    for copy in copies:
        copy.start()
    for copy in copies:
        copy.wait()


def by_lanes(
    camera_jacobian, point_jacobian, residual, send_order, camera_of, track_of, partner, pair_slot
):
    n = lax.axis_size("obs")
    n_row = lax.axis_size("row")
    cameras = CAM_ROW * n_row
    ranks = partner.shape[0]
    chunks = -(-NBR // PACK)
    vmem = pl.BlockSpec(memory_space=pltpu.VMEM)
    hbm = pl.BlockSpec(memory_space=pltpu.HBM)
    f32, i32 = jnp.float32, jnp.int32
    dma = pltpu.SemaphoreType.DMA
    results = pl.pallas_call(
        functools.partial(step_kernel, n, n_row, cameras),
        out_shape=(
            jax.ShapeDtypeStruct((CAM_ROW, 81), f32),
            jax.ShapeDtypeStruct((9, CAM_ROW), f32),
            jax.ShapeDtypeStruct((81, CAM_ROW * NBR), f32),
        ),
        in_specs=[hbm] * 7,
        out_specs=(vmem, vmem, vmem),
        scratch_shapes=[
            pltpu.VMEM(camera_jacobian.shape, f32),
            pltpu.VMEM(point_jacobian.shape, f32),
            pltpu.VMEM(residual.shape, f32),
            pltpu.VMEM((n, LANES), i32),
            pltpu.VMEM((n, LANES), i32),
            pltpu.VMEM(partner.shape, i32),
            pltpu.VMEM(pair_slot.shape, i32),
            dma((7,)),
            pltpu.VMEM((n, 26, n, LANES), f32),
            pltpu.VMEM((n * SUBLANES, LANES), i32),
            pltpu.VMEM((n, SUBLANES, LANES), i32),
            pltpu.VMEM((ranks * n, LANES), i32),
            pltpu.VMEM((n, 26, n, LANES), f32),
            pltpu.VMEM((n, n, LANES), i32),
            pltpu.VMEM((6, n, LANES), f32),
            pltpu.VMEM((27, n, LANES), f32),
            pltpu.VMEM((n, 27, n, LANES), f32),
            pltpu.VMEM((chunks * CHUNK * n, LANES), f32),
            pltpu.VMEM((n // 2, cameras, 2 * LANES), jnp.bfloat16),
            pltpu.VMEM((chunks, cameras, CHUNK), f32),
            pltpu.VMEM((n_row, chunks, CAM_ROW, CHUNK), f32),
            pltpu.VMEM((LANES, LANES), f32),
            dma((n,)),
            dma((n,)),
            dma((n, PIECES)),
            dma((n, PIECES)),
            dma((n, PIECES)),
            dma((n_row, chunks)),
            dma((n_row, chunks)),
        ],
        compiler_params=pltpu.CompilerParams(
            collective_id=0, has_side_effects=True, vmem_limit_bytes=VMEM_BYTES
        ),
        name="gauss_newton_step",
    )(
        camera_jacobian,
        point_jacobian,
        residual,
        send_order.reshape(n, LANES),
        camera_of.reshape(n, LANES),
        partner,
        pair_slot,
    )
    hessian, gradient, pair_hessian = pl.pallas_call(
        store_kernel,
        out_shape=tuple(jax.ShapeDtypeStruct(r.shape, r.dtype) for r in results),
        in_specs=[hbm] * 3,
        out_specs=(hbm,) * 3,
        scratch_shapes=[dma((3,))],
        compiler_params=pltpu.CompilerParams(vmem_limit_bytes=VMEM_BYTES),
        name="store",
    )(*results)
    return (hessian.T, gradient, pair_hessian)


damping = 1.0


def eliminate(camera_rows, point_rows, resid_rows, track_of, track_count):
    camera = camera_rows.reshape(2, 9, -1)
    point_jac = point_rows.reshape(2, 3, -1)
    normal = jnp.stack(
        [
            point_jac[0, 0] * point_jac[0, 0] + point_jac[1, 0] * point_jac[1, 0],
            point_jac[0, 0] * point_jac[0, 1] + point_jac[1, 0] * point_jac[1, 1],
            point_jac[0, 0] * point_jac[0, 2] + point_jac[1, 0] * point_jac[1, 2],
            point_jac[0, 1] * point_jac[0, 1] + point_jac[1, 1] * point_jac[1, 1],
            point_jac[0, 1] * point_jac[0, 2] + point_jac[1, 1] * point_jac[1, 2],
            point_jac[0, 2] * point_jac[0, 2] + point_jac[1, 2] * point_jac[1, 2],
            point_jac[0, 0] * resid_rows[0] + point_jac[1, 0] * resid_rows[1],
            point_jac[0, 1] * resid_rows[0] + point_jac[1, 1] * resid_rows[1],
            point_jac[0, 2] * resid_rows[0] + point_jac[1, 2] * resid_rows[1],
        ]
    )
    totals = jnp.zeros((9, track_count), jnp.float32).at[:, track_of].add(normal)
    pivot_first = jnp.sqrt(totals[0] + damping)
    lower_one = totals[1] / pivot_first
    lower_two = totals[2] / pivot_first
    pivot_second = jnp.sqrt(totals[3] + damping - lower_one * lower_one)
    lower_mid = (totals[4] - lower_two * lower_one) / pivot_second
    pivot_third = jnp.sqrt(totals[5] + damping - lower_two * lower_two - lower_mid * lower_mid)
    solved_one = totals[6] / pivot_first
    solved_two = (totals[7] - lower_one * solved_one) / pivot_second
    solved_three = (totals[8] - lower_two * solved_one - lower_mid * solved_two) / pivot_third
    per_track = jnp.stack(
        [
            pivot_first,
            lower_one,
            lower_two,
            pivot_second,
            lower_mid,
            pivot_third,
            solved_one,
            solved_two,
            solved_three,
        ]
    )
    per_obs = per_track[:, track_of]
    weights = (
        camera[0][:, None, :] * point_jac[0][None, :, :]
        + camera[1][:, None, :] * point_jac[1][None, :, :]
    )
    column_one = weights[:, 0] / per_obs[0]
    column_two = (weights[:, 1] - per_obs[1] * column_one) / per_obs[3]
    column_three = (weights[:, 2] - per_obs[2] * column_one - per_obs[4] * column_two) / per_obs[5]
    factor = jnp.stack([column_one, column_two, column_three])
    point_shift = column_one * per_obs[6] + column_two * per_obs[7] + column_three * per_obs[8]
    return (factor, point_shift)


def camera_terms(camera_rows, resid_rows, factor, point_shift):
    camera = camera_rows.reshape(2, 9, -1)
    normal = (
        camera[0][:, None, :] * camera[0][None, :, :]
        + camera[1][:, None, :] * camera[1][None, :, :]
    )
    schur_part = (
        factor[0][:, None, :] * factor[0][None, :, :]
        + factor[1][:, None, :] * factor[1][None, :, :]
        + factor[2][:, None, :] * factor[2][None, :, :]
    )
    gradient = camera[0] * resid_rows[0] + camera[1] * resid_rows[1] - point_shift
    return jnp.concatenate([(normal - schur_part).reshape(81, -1), gradient], axis=0)


def pair_product(left, right):
    total = (
        left[0][:, None] * right[0][None, :]
        + left[1][:, None] * right[1][None, :]
        + left[2][:, None] * right[2][None, :]
    )
    return -total.reshape(81, -1)


def on_device(
    camera_jacobian, point_jacobian, residual, send_order, camera_of, track_of, partner, pair_slot
):
    obs_count = camera_jacobian.shape[1]
    ranks = partner.shape[0]
    camera_count = CAM_ROW * lax.axis_size("row")
    slot_count = camera_count * NBR
    stacked = jnp.concatenate([camera_jacobian, point_jacobian, residual], axis=0)
    sent = jnp.take(stacked, send_order, axis=1)
    owned = lax.all_to_all(sent, "obs", split_axis=1, concat_axis=1, tiled=True)
    factor, point_shift = eliminate(
        owned[:18], owned[18:24], owned[24:26], track_of, obs_count // 2
    )
    flat_factor = factor.reshape(27, obs_count)
    chosen = jnp.take(flat_factor, partner.reshape(-1), axis=1)
    together = jnp.concatenate(
        [
            flat_factor,
            point_shift,
            chosen.reshape(27, ranks, obs_count).reshape(27 * ranks, obs_count),
        ],
        axis=0,
    )
    back = lax.all_to_all(together, "obs", split_axis=1, concat_axis=1, tiled=True)
    factor_back = back[:27].reshape(3, 9, obs_count)
    shift_back = back[27:36]
    remote = back[36:].reshape(3, 9, ranks, obs_count)
    arrived = pair_product(factor_back[:, :, None, :], remote)
    local_terms = camera_terms(sent[:18], sent[24:26], factor_back, shift_back)
    camera_ids = jnp.take(camera_of, send_order)
    indicator = (camera_ids[:, None] == jnp.arange(camera_count, dtype=jnp.int32)[None, :]).astype(
        jnp.float32
    )
    camera_partial = jnp.dot(
        local_terms, indicator, precision=lax.Precision.HIGHEST, preferred_element_type=jnp.float32
    )
    camera_mine = lax.psum_scatter(camera_partial, "row", scatter_dimension=1, tiled=True)
    pair_total = (
        jnp.zeros((81, slot_count + 1), jnp.float32).at[:, pair_slot.reshape(-1)].add(arrived)
    )
    pair_mine = lax.psum_scatter(pair_total[:, :slot_count], "row", scatter_dimension=1, tiled=True)
    return (camera_mine[:81], camera_mine[81:], pair_mine)


def on_mesh(*arguments):
    share = arguments[0].shape[1] // lax.axis_size("obs")
    if share == LANES and lax.axis_size("obs") % 2 == 0:
        return by_lanes(*arguments)
    return on_device(*arguments)


def solution(mesh):
    return jax.shard_map(
        on_mesh,
        mesh=mesh,
        in_specs=(
            P(None, ("obs", "row")),
            P(None, ("obs", "row")),
            P(None, ("obs", "row")),
            P(("obs", "row")),
            P(("obs", "row")),
            P(("obs", "row")),
            P(None, ("obs", "row")),
            P(None, ("obs", "row")),
        ),
        out_specs=(P(None, ("obs", "row")), P(None, ("obs", "row")), P(None, ("obs", "row"))),
        check_vma=False,
    )
```

```python
import functools

import jax
import jax.numpy as jnp
from jax import lax
from jax.experimental import pallas as pl
from jax.experimental.pallas import tpu as pltpu
from jax.sharding import PartitionSpec as P

CAM_ROW = 16
NBR = 14
LANES = 128
SUBLANES = 8
CHUNK = 256
PACK = 3
PIECES = 2
MESH = pl.DeviceIdType.MESH
VMEM_BYTES = 64 * 1024 * 1024


def lane_gather(values, index):
    return jnp.take_along_axis(values, index, axis=1, mode="promise_in_bounds")


def normal_rows(camera_point):
    a, b, e = camera_point[0:3], camera_point[3:6], camera_point[6:8]
    return [
        a[0] * a[0] + b[0] * b[0],
        a[0] * a[1] + b[0] * b[1],
        a[0] * a[2] + b[0] * b[2],
        a[1] * a[1] + b[1] * b[1],
        a[1] * a[2] + b[1] * b[2],
        a[2] * a[2] + b[2] * b[2],
        a[0] * e[0] + b[0] * e[1],
        a[1] * e[0] + b[1] * e[1],
        a[2] * e[0] + b[2] * e[1],
    ]


def step_kernel(
    n, n_row, cameras,
    camera_in, point_in, resid_in, order_in, ids_in, partner_in, pair_in,
    hessian_ref, gradient_ref, pair_out_ref,
    camera_ref, point_ref, resid_ref, order_ref, ids_ref, partner_ref, pair_ref, load_sem,
    rows_in, part, staged, pairs, rows_of, offset_of, solve, own, factor_of, prod, marks,
    partial, landed, turned,
    id_send, id_recv, row_send, row_recv, pass_send, sum_send, sum_recv,
):
    me = lax.axis_index("obs")
    my_row = lax.axis_index("row")
    chips = n // 2
    chip = me // 2
    core = lax.rem(me, 2)
    sibling = chip * 2 + 1 - core
    ranks = partner_ref.shape[0]
    shift = LANES.bit_length() - 1
    size = 26 // PIECES
    chunks = partial.shape[0]

    moves = [
        pltpu.make_async_copy(source, target, load_sem.at[i])
        for i, (source, target) in enumerate(
            [
                (order_in, order_ref),
                (point_in, point_ref),
                (resid_in, resid_ref),
                (camera_in, camera_ref),
                (partner_in, partner_ref),
                (ids_in, ids_ref),
                (pair_in, pair_ref),
            ]
        )
    ]
    for move in moves:
        move.start()
    barrier = pltpu.get_barrier_semaphore()
    for d in range(1, n):
        pl.semaphore_signal(
            barrier, inc=1, device_id={"obs": lax.rem(me + d, n)}, device_id_type=MESH
        )
    for d in range(1, n_row):
        pl.semaphore_signal(
            barrier, inc=1, device_id={"row": lax.rem(my_row + d, n_row)}, device_id_type=MESH
        )

    def ids_copy(peer, source):
        return pltpu.make_async_remote_copy(
            src_ref=staged.at[peer],
            dst_ref=part.at[pl.ds(pl.multiple_of(source * SUBLANES, SUBLANES), SUBLANES)],
            send_sem=id_send.at[peer],
            recv_sem=id_recv.at[source],
            device_id={"obs": peer},
            device_id_type=MESH,
        )

    def rows_copy(source, piece, peer, sem):
        block = rows_in.at[source, pl.ds(piece * size, size)]
        return pltpu.make_async_remote_copy(
            src_ref=block,
            dst_ref=block,
            send_sem=sem.at[peer if sem is row_send else source, piece],
            recv_sem=row_recv.at[source, piece],
            device_id={"obs": peer},
            device_id_type=MESH,
        )

    def twin(d):
        return lax.rem(chip + d, chips) * 2 + core

    for move in moves[:4]:
        move.wait()
    order = order_ref[...]
    block_of = lax.shift_right_logical(order, shift)
    lane_of = lax.bitwise_and(order, LANES - 1)

    def permuted(row_of_block):
        total = None
        for b in range(n):
            row = jnp.broadcast_to(row_of_block(b), (n, LANES))
            picked = lane_gather(row, lane_of)
            total = picked if b == 0 else jnp.where(block_of == b, picked, total)
        return total

    table = [(point_ref, f) for f in range(6)] + [(resid_ref, f) for f in range(2)]
    table = table + [(camera_ref, f) for f in range(18)]
    targets = [twin(d) for d in range(1, chips)] + [sibling]
    for piece in range(PIECES):
        for f in range(piece * size, (piece + 1) * size):
            ref, r = table[f]
            rows_in[me, f] = permuted(lambda b: ref[r : r + 1, b * LANES : (b + 1) * LANES])
        if piece == 0:
            pl.semaphore_wait(barrier, n - 1 + n_row - 1)
        for peer in targets:
            rows_copy(me, piece, peer, row_send).start()
        if piece == 0:
            for move in moves[4:]:
                move.wait()
            for x in range(n):
                staged[x] = jnp.zeros((SUBLANES, LANES), jnp.int32)
                staged[x, 0:ranks] = partner_ref[:, x * LANES : (x + 1) * LANES]
            for d in range(1, n):
                ids_copy(lax.rem(me + d, n), me).start()
    part[pl.ds(pl.multiple_of(me * SUBLANES, SUBLANES), SUBLANES), :] = staged[me]

    cam = permuted(lambda b: ids_ref[b : b + 1, :])
    ids = lax.broadcasted_iota(jnp.int32, (cameras, LANES), 0)
    halves = [
        jnp.where(ids == cam[j : j + 1, :], 1.0, 0.0).astype(jnp.bfloat16) for j in range(n)
    ]
    for i in range(n // 2):
        marks[i] = jnp.concatenate([halves[2 * i], halves[2 * i + 1]], axis=1)
    for j in range(n):
        pairs[pl.ds(j, ranks, stride=n), :] = pair_ref[:, j * LANES : (j + 1) * LANES]
    turned[...] = jnp.zeros_like(turned)
    pair_out_ref[...] = jnp.zeros_like(pair_out_ref)

    for d in range(1, n):
        peer = lax.rem(me + d, n)
        ids_copy(peer, peer).wait_recv()
    sources, places, offsets = [], [], []
    for k in range(ranks):
        slot = part[pl.ds(k, n, stride=SUBLANES), :]
        pair = pairs[pl.ds(k * n, n), :]
        sources.append(
            jnp.where(pair == cameras * NBR, -1, lax.shift_right_logical(slot, shift))
        )
        places.append(lax.bitwise_and(slot, LANES - 1))
        offsets.append(pair - cam * NBR)

    def add_source(x, totals):
        place = jnp.zeros((n, LANES), jnp.int32)
        offset = jnp.full((n, LANES), -1, jnp.int32)
        for k in range(ranks):
            match = sources[k] == x
            place = jnp.where(match, places[k], place)
            offset = jnp.where(match, offsets[k], offset)
        offset_of[x] = offset
        found = offset >= 0
        values = []
        for f in range(26):
            value = jnp.where(found, lane_gather(rows_in[x, f], place), 0.0)
            rows_of[x, f] = value
            values.append(value)
        return tuple(t + v for t, v in zip(totals, normal_rows(values[0:8])))

    totals = normal_rows([rows_in[me, f] for f in range(8)])
    totals = add_source(me, tuple(totals))
    for piece in range(PIECES):
        rows_copy(sibling, piece, sibling, row_send).wait_recv()
    totals = add_source(sibling, totals)
    for piece in range(PIECES):
        for d in range(1, chips):
            rows_copy(twin(d), piece, sibling, row_send).wait_recv()
            rows_copy(twin(d), piece, sibling, pass_send).start()
    totals = lax.fori_loop(1, chips, lambda d, t: add_source(twin(d), t), totals)

    def add_passed(d, totals):
        x = lax.rem(chip + d, chips) * 2 + 1 - core
        for piece in range(PIECES):
            rows_copy(x, piece, sibling, pass_send).wait_recv()
        return add_source(x, totals)

    totals = lax.fori_loop(1, chips, add_passed, totals)
    pivot_one = jnp.sqrt(totals[0] + 1.0)
    inv_one = 1.0 / pivot_one
    low_one = totals[1] * inv_one
    low_two = totals[2] * inv_one
    inv_two = 1.0 / jnp.sqrt(totals[3] + 1.0 - low_one * low_one)
    low_mid = (totals[4] - low_two * low_one) * inv_two
    inv_three = 1.0 / jnp.sqrt(totals[5] + 1.0 - low_two * low_two - low_mid * low_mid)
    h_one = totals[6] * inv_one
    h_two = (totals[7] - low_one * h_one) * inv_two
    h_three = (totals[8] - low_two * h_one - low_mid * h_two) * inv_three
    for i, value in enumerate([inv_one, low_one, low_two, inv_two, low_mid, inv_three]):
        solve[i] = value

    def factors(rows):
        tri = [solve[i] for i in range(6)]
        columns = []
        for i in range(2):
            jp = [rows(3 * i + c) for c in range(3)]
            one = jp[0] * tri[0]
            two = (jp[1] - tri[1] * one) * tri[3]
            three = (jp[2] - tri[2] * one - tri[4] * two) * tri[5]
            columns.append((one, two, three))
        result = [[None] * 9 for _ in range(3)]
        for p in range(9):
            first, second = rows(8 + p), rows(17 + p)
            for c in range(3):
                result[c][p] = first * columns[0][c] + second * columns[1][c]
        return result

    mine = factors(lambda f: rows_in[me, f])
    jac = [rows_in[me, 8 + f] for f in range(18)]
    for c in range(3):
        for p in range(9):
            own[c * 9 + p] = -mine[c][p]
    last = chunks - 1
    base = last * CHUNK + (NBR - last * PACK) * 81

    def put(row, value):
        prod[pl.ds(row * n, n), :] = value

    for p in range(9):
        for q in range(p, 9):
            value = jac[p] * jac[q] + jac[9 + p] * jac[9 + q]
            value = value - (
                mine[0][p] * mine[0][q] + mine[1][p] * mine[1][q] + mine[2][p] * mine[2][q]
            )
            put(base + 9 * p + q, value)
            if q != p:
                put(base + 9 * q + p, value)
        back = mine[0][p] * h_one + mine[1][p] * h_two + mine[2][p] * h_three
        put(base + 81 + p, jac[p] * rows_in[me, 6] + jac[9 + p] * rows_in[me, 7] - back)

    def source_factors(x, carry):
        got = factors(lambda f: rows_of[x, f])
        for c in range(3):
            for p in range(9):
                factor_of[x, c * 9 + p] = got[c][p]
        return carry

    lax.fori_loop(0, n, source_factors, 0)

    def at_offset(o, row):
        picked = [None] * 27
        for x in range(n):
            match = offset_of[x] == o
            for i in range(27):
                value = jnp.where(match, factor_of[x, i], 0.0)
                picked[i] = value if x == 0 else picked[i] + value
        for p in range(9):
            left = [own[c * 9 + p] for c in range(3)]
            for q in range(9):
                value = left[0] * picked[q] + left[1] * picked[9 + q] + left[2] * picked[18 + q]
                prod[pl.ds(pl.multiple_of((row + 9 * p + q) * n, n), n), :] = value

    contract = (((1,), (1,)), ((), ()))

    def sum_copy(peer, slot, chunk):
        return pltpu.make_async_remote_copy(
            src_ref=partial.at[chunk, pl.ds(pl.multiple_of(peer * CAM_ROW, CAM_ROW), CAM_ROW)],
            dst_ref=landed.at[slot, chunk],
            send_sem=sum_send.at[peer, chunk],
            recv_sem=sum_recv.at[slot, chunk],
            device_id={"row": peer},
            device_id_type=MESH,
        )

    def chunk_step(chunk, carry):
        def offset_step(i, inner):
            at_offset(chunk * PACK + i, chunk * CHUNK + i * 81)
            return inner

        lax.fori_loop(0, jnp.minimum(PACK, NBR - chunk * PACK), offset_step, 0)
        total = jnp.zeros((cameras, CHUNK), jnp.float32)
        for i in range(n // 2):
            start = chunk * (CHUNK * n) + 2 * i
            first = prod[pl.ds(start, CHUNK, stride=n), :]
            second = prod[pl.ds(start + 1, CHUNK, stride=n), :]
            both = jnp.concatenate([first, second], axis=1)
            high = both.astype(jnp.bfloat16)
            low = (both - high.astype(jnp.float32)).astype(jnp.bfloat16)
            for half in (high, low):
                total += lax.dot_general(
                    marks[i], half, contract, preferred_element_type=jnp.float32
                )
        partial[chunk] = total
        for d in range(1, n_row):
            sum_copy(lax.rem(my_row + d, n_row), my_row, chunk).start()
        return carry

    lax.fori_loop(0, chunks, chunk_step, 0)

    slots = pair_out_ref.shape[1]
    lane = lax.broadcasted_iota(jnp.int32, (LANES, slots), 1)
    line = lax.broadcasted_iota(jnp.int32, (LANES, slots), 0)
    for chunk in range(chunks):
        total = partial[chunk, pl.ds(pl.multiple_of(my_row * CAM_ROW, CAM_ROW), CAM_ROW), :]
        for d in range(1, n_row):
            peer = lax.rem(my_row + d, n_row)
            sum_copy(peer, peer, chunk).wait_recv()
            total = total + landed[peer, chunk]
        count = min(PACK, NBR - chunk * PACK)
        for i in range(count):
            turned[i * CAM_ROW : (i + 1) * CAM_ROW, 0:81] = total[:, i * 81 : (i + 1) * 81]
        if chunk == last:
            turned[count * CAM_ROW : (count + 1) * CAM_ROW, 0:90] = total[
                :, count * 81 : count * 81 + 90
            ]
        flipped = turned[...].T
        offset = chunk * PACK + line // CAM_ROW
        chosen = jnp.logical_and(
            lane == lax.rem(line, CAM_ROW) * NBR + offset, line < count * CAM_ROW
        )
        select = jnp.where(chosen, 1.0, 0.0).astype(jnp.bfloat16)
        rows = flipped[0:88]
        high = rows.astype(jnp.bfloat16)
        low = (rows - high.astype(jnp.float32)).astype(jnp.bfloat16)
        placed = jnp.dot(high, select, preferred_element_type=jnp.float32)
        placed = placed + jnp.dot(low, select, preferred_element_type=jnp.float32)
        pair_out_ref[...] += placed[0:81]
        if chunk == last:
            mine_lanes = flipped[:, count * CAM_ROW : (count + 1) * CAM_ROW]
            hessian_ref[...] = total[:, count * 81 : count * 81 + 81]
            gradient_ref[...] = mine_lanes[81:90]

    for d in range(1, n):
        ids_copy(lax.rem(me + d, n), me).wait_send()
    for piece in range(PIECES):
        for peer in targets:
            rows_copy(me, piece, peer, row_send).wait_send()
        for d in range(1, chips):
            rows_copy(twin(d), piece, sibling, pass_send).wait_send()
    for chunk in range(chunks):
        for d in range(1, n_row):
            sum_copy(lax.rem(my_row + d, n_row), my_row, chunk).wait_send()


def store_kernel(*refs):
    held, load_sem, store_sem = refs[6:9], refs[9], refs[10]
    loads = [pltpu.make_async_copy(refs[i], held[i], load_sem.at[i]) for i in range(3)]
    stores = [pltpu.make_async_copy(held[i], refs[3 + i], store_sem.at[i]) for i in range(3)]
    for load in loads:
        load.start()
    for load, store in zip(loads, stores):
        load.wait()
        store.start()
    for store in stores:
        store.wait()


def by_lanes(
    camera_jacobian, point_jacobian, residual, send_order, camera_of, track_of, partner, pair_slot
):
    n = lax.axis_size("obs")
    n_row = lax.axis_size("row")
    cameras = CAM_ROW * n_row
    ranks = partner.shape[0]
    chunks = -(-NBR // PACK)
    vmem = pl.BlockSpec(memory_space=pltpu.VMEM)
    hbm = pl.BlockSpec(memory_space=pltpu.HBM)
    f32, i32 = jnp.float32, jnp.int32
    dma = pltpu.SemaphoreType.DMA
    results = pl.pallas_call(
        functools.partial(step_kernel, n, n_row, cameras),
        out_shape=(
            jax.ShapeDtypeStruct((CAM_ROW, 81), f32),
            jax.ShapeDtypeStruct((9, CAM_ROW), f32),
            jax.ShapeDtypeStruct((81, CAM_ROW * NBR), f32),
        ),
        in_specs=[hbm] * 7,
        out_specs=(vmem, vmem, vmem),
        scratch_shapes=[
            pltpu.VMEM(camera_jacobian.shape, f32),
            pltpu.VMEM(point_jacobian.shape, f32),
            pltpu.VMEM(residual.shape, f32),
            pltpu.VMEM((n, LANES), i32),
            pltpu.VMEM((n, LANES), i32),
            pltpu.VMEM(partner.shape, i32),
            pltpu.VMEM(pair_slot.shape, i32),
            dma((7,)),
            pltpu.VMEM((n, 26, n, LANES), f32),
            pltpu.VMEM((n * SUBLANES, LANES), i32),
            pltpu.VMEM((n, SUBLANES, LANES), i32),
            pltpu.VMEM((ranks * n, LANES), i32),
            pltpu.VMEM((n, 26, n, LANES), f32),
            pltpu.VMEM((n, n, LANES), i32),
            pltpu.VMEM((6, n, LANES), f32),
            pltpu.VMEM((27, n, LANES), f32),
            pltpu.VMEM((n, 27, n, LANES), f32),
            pltpu.VMEM((chunks * CHUNK * n, LANES), f32),
            pltpu.VMEM((n // 2, cameras, 2 * LANES), jnp.bfloat16),
            pltpu.VMEM((chunks, cameras, CHUNK), f32),
            pltpu.VMEM((n_row, chunks, CAM_ROW, CHUNK), f32),
            pltpu.VMEM((LANES, LANES), f32),
            dma((n,)),
            dma((n,)),
            dma((n, PIECES)),
            dma((n, PIECES)),
            dma((n, PIECES)),
            dma((n_row, chunks)),
            dma((n_row, chunks)),
        ],
        compiler_params=pltpu.CompilerParams(
            collective_id=0, has_side_effects=True, vmem_limit_bytes=VMEM_BYTES
        ),
        name="gauss_newton_step",
    )(
        camera_jacobian,
        point_jacobian,
        residual,
        send_order.reshape(n, LANES),
        camera_of.reshape(n, LANES),
        partner,
        pair_slot,
    )
    hessian, gradient, pair_hessian = pl.pallas_call(
        store_kernel,
        out_shape=tuple(jax.ShapeDtypeStruct(r.shape, r.dtype) for r in results),
        in_specs=[hbm] * 3,
        out_specs=(hbm,) * 3,
        scratch_shapes=[pltpu.VMEM(r.shape, r.dtype) for r in results] + [dma((3,)), dma((3,))],
        compiler_params=pltpu.CompilerParams(vmem_limit_bytes=VMEM_BYTES),
        name="store",
    )(*results)
    return (hessian.T, gradient, pair_hessian)


damping = 1.0


def eliminate(camera_rows, point_rows, resid_rows, track_of, track_count):
    camera = camera_rows.reshape(2, 9, -1)
    point_jac = point_rows.reshape(2, 3, -1)
    normal = jnp.stack(
        [
            point_jac[0, 0] * point_jac[0, 0] + point_jac[1, 0] * point_jac[1, 0],
            point_jac[0, 0] * point_jac[0, 1] + point_jac[1, 0] * point_jac[1, 1],
            point_jac[0, 0] * point_jac[0, 2] + point_jac[1, 0] * point_jac[1, 2],
            point_jac[0, 1] * point_jac[0, 1] + point_jac[1, 1] * point_jac[1, 1],
            point_jac[0, 1] * point_jac[0, 2] + point_jac[1, 1] * point_jac[1, 2],
            point_jac[0, 2] * point_jac[0, 2] + point_jac[1, 2] * point_jac[1, 2],
            point_jac[0, 0] * resid_rows[0] + point_jac[1, 0] * resid_rows[1],
            point_jac[0, 1] * resid_rows[0] + point_jac[1, 1] * resid_rows[1],
            point_jac[0, 2] * resid_rows[0] + point_jac[1, 2] * resid_rows[1],
        ]
    )
    totals = jnp.zeros((9, track_count), jnp.float32).at[:, track_of].add(normal)
    pivot_first = jnp.sqrt(totals[0] + damping)
    lower_one = totals[1] / pivot_first
    lower_two = totals[2] / pivot_first
    pivot_second = jnp.sqrt(totals[3] + damping - lower_one * lower_one)
    lower_mid = (totals[4] - lower_two * lower_one) / pivot_second
    pivot_third = jnp.sqrt(totals[5] + damping - lower_two * lower_two - lower_mid * lower_mid)
    solved_one = totals[6] / pivot_first
    solved_two = (totals[7] - lower_one * solved_one) / pivot_second
    solved_three = (totals[8] - lower_two * solved_one - lower_mid * solved_two) / pivot_third
    per_track = jnp.stack(
        [
            pivot_first,
            lower_one,
            lower_two,
            pivot_second,
            lower_mid,
            pivot_third,
            solved_one,
            solved_two,
            solved_three,
        ]
    )
    per_obs = per_track[:, track_of]
    weights = (
        camera[0][:, None, :] * point_jac[0][None, :, :]
        + camera[1][:, None, :] * point_jac[1][None, :, :]
    )
    column_one = weights[:, 0] / per_obs[0]
    column_two = (weights[:, 1] - per_obs[1] * column_one) / per_obs[3]
    column_three = (weights[:, 2] - per_obs[2] * column_one - per_obs[4] * column_two) / per_obs[5]
    factor = jnp.stack([column_one, column_two, column_three])
    point_shift = column_one * per_obs[6] + column_two * per_obs[7] + column_three * per_obs[8]
    return (factor, point_shift)


def camera_terms(camera_rows, resid_rows, factor, point_shift):
    camera = camera_rows.reshape(2, 9, -1)
    normal = (
        camera[0][:, None, :] * camera[0][None, :, :]
        + camera[1][:, None, :] * camera[1][None, :, :]
    )
    schur_part = (
        factor[0][:, None, :] * factor[0][None, :, :]
        + factor[1][:, None, :] * factor[1][None, :, :]
        + factor[2][:, None, :] * factor[2][None, :, :]
    )
    gradient = camera[0] * resid_rows[0] + camera[1] * resid_rows[1] - point_shift
    return jnp.concatenate([(normal - schur_part).reshape(81, -1), gradient], axis=0)


def pair_product(left, right):
    total = (
        left[0][:, None] * right[0][None, :]
        + left[1][:, None] * right[1][None, :]
        + left[2][:, None] * right[2][None, :]
    )
    return -total.reshape(81, -1)


def on_device(
    camera_jacobian, point_jacobian, residual, send_order, camera_of, track_of, partner, pair_slot
):
    obs_count = camera_jacobian.shape[1]
    ranks = partner.shape[0]
    camera_count = CAM_ROW * lax.axis_size("row")
    slot_count = camera_count * NBR
    stacked = jnp.concatenate([camera_jacobian, point_jacobian, residual], axis=0)
    sent = jnp.take(stacked, send_order, axis=1)
    owned = lax.all_to_all(sent, "obs", split_axis=1, concat_axis=1, tiled=True)
    factor, point_shift = eliminate(
        owned[:18], owned[18:24], owned[24:26], track_of, obs_count // 2
    )
    flat_factor = factor.reshape(27, obs_count)
    chosen = jnp.take(flat_factor, partner.reshape(-1), axis=1)
    together = jnp.concatenate(
        [
            flat_factor,
            point_shift,
            chosen.reshape(27, ranks, obs_count).reshape(27 * ranks, obs_count),
        ],
        axis=0,
    )
    back = lax.all_to_all(together, "obs", split_axis=1, concat_axis=1, tiled=True)
    factor_back = back[:27].reshape(3, 9, obs_count)
    shift_back = back[27:36]
    remote = back[36:].reshape(3, 9, ranks, obs_count)
    arrived = pair_product(factor_back[:, :, None, :], remote)
    local_terms = camera_terms(sent[:18], sent[24:26], factor_back, shift_back)
    camera_ids = jnp.take(camera_of, send_order)
    indicator = (camera_ids[:, None] == jnp.arange(camera_count, dtype=jnp.int32)[None, :]).astype(
        jnp.float32
    )
    camera_partial = jnp.dot(
        local_terms, indicator, precision=lax.Precision.HIGHEST, preferred_element_type=jnp.float32
    )
    camera_mine = lax.psum_scatter(camera_partial, "row", scatter_dimension=1, tiled=True)
    pair_total = (
        jnp.zeros((81, slot_count + 1), jnp.float32).at[:, pair_slot.reshape(-1)].add(arrived)
    )
    pair_mine = lax.psum_scatter(pair_total[:, :slot_count], "row", scatter_dimension=1, tiled=True)
    return (camera_mine[:81], camera_mine[81:], pair_mine)


def on_mesh(*arguments):
    share = arguments[0].shape[1] // lax.axis_size("obs")
    if share == LANES and lax.axis_size("obs") % 2 == 0:
        return by_lanes(*arguments)
    return on_device(*arguments)


def solution(mesh):
    return jax.shard_map(
        on_mesh,
        mesh=mesh,
        in_specs=(
            P(None, ("obs", "row")),
            P(None, ("obs", "row")),
            P(None, ("obs", "row")),
            P(("obs", "row")),
            P(("obs", "row")),
            P(("obs", "row")),
            P(None, ("obs", "row")),
            P(None, ("obs", "row")),
        ),
        out_specs=(P(None, ("obs", "row")), P(None, ("obs", "row")), P(None, ("obs", "row"))),
        check_vma=False,
    )
```

```python
import functools

import jax
import jax.numpy as jnp
from jax import lax
from jax.experimental import pallas as pl
from jax.experimental.pallas import tpu as pltpu
from jax.sharding import PartitionSpec as P

CAM_ROW = 16
NBR = 14
LANES = 128
SUBLANES = 8
CHUNK = 256
MESH = pl.DeviceIdType.MESH
VMEM_BYTES = 64 * 1024 * 1024


COLUMNS = [[8], [0, 1], [2, 3], [4, 5], [6, 7]]
PIECES = [
    [("point", f) for f in range(6)]
    + [("resid", f) for f in range(2)]
    + [("camera", 8), ("camera", 17)]
] + [[("camera", q + 9 * i) for i in range(2) for q in pair] for pair in COLUMNS[1:]]
TABLE = [entry for piece in PIECES for entry in piece]
STARTS = [sum(len(piece) for piece in PIECES[:k]) for k in range(len(PIECES))]
PLACE = {entry: i for i, entry in enumerate(TABLE)}


def lane_gather(values, index):
    return jnp.take_along_axis(values, index, axis=1, mode="promise_in_bounds")


def normal_rows(camera_point):
    a, b, e = camera_point[0:3], camera_point[3:6], camera_point[6:8]
    return [
        a[0] * a[0] + b[0] * b[0],
        a[0] * a[1] + b[0] * b[1],
        a[0] * a[2] + b[0] * b[2],
        a[1] * a[1] + b[1] * b[1],
        a[1] * a[2] + b[1] * b[2],
        a[2] * a[2] + b[2] * b[2],
        a[0] * e[0] + b[0] * e[1],
        a[1] * e[0] + b[1] * e[1],
        a[2] * e[0] + b[2] * e[1],
    ]


def step_kernel(
    n, n_row, cameras,
    camera_in, point_in, resid_in, order_in, ids_in, partner_in, pair_in,
    hessian_ref, gradient_ref, pair_out_ref,
    camera_ref, point_ref, resid_ref, order_ref, ids_ref, partner_ref, pair_ref, load_sem,
    rows_in, part, staged, pairs, rows_of, offset_of, place_of, own, normal_of, factor_of, prod,
    marks,
    partial, landed, turned,
    id_send, id_recv, row_send, row_recv, pass_send, sum_send, sum_recv,
):
    me = lax.axis_index("obs")
    my_row = lax.axis_index("row")
    chips = n // 2
    chip = me // 2
    core = lax.rem(me, 2)
    sibling = chip * 2 + 1 - core
    ranks = partner_ref.shape[0]
    shift = LANES.bit_length() - 1

    moves = [
        pltpu.make_async_copy(source, target, load_sem.at[i])
        for i, (source, target) in enumerate(
            [
                (order_in, order_ref),
                (point_in, point_ref),
                (resid_in, resid_ref),
                (camera_in, camera_ref),
                (partner_in, partner_ref),
                (ids_in, ids_ref),
                (pair_in, pair_ref),
            ]
        )
    ]
    for move in moves:
        move.start()
    barrier = pltpu.get_barrier_semaphore()
    for d in range(1, n):
        pl.semaphore_signal(
            barrier, inc=1, device_id={"obs": lax.rem(me + d, n)}, device_id_type=MESH
        )
    for d in range(1, n_row):
        pl.semaphore_signal(
            barrier, inc=1, device_id={"row": lax.rem(my_row + d, n_row)}, device_id_type=MESH
        )

    def ids_copy(peer, source):
        return pltpu.make_async_remote_copy(
            src_ref=staged.at[peer],
            dst_ref=part.at[pl.ds(pl.multiple_of(source * SUBLANES, SUBLANES), SUBLANES)],
            send_sem=id_send.at[peer],
            recv_sem=id_recv.at[source],
            device_id={"obs": peer},
            device_id_type=MESH,
        )

    def rows_copy(source, piece, peer, sem):
        block = rows_in.at[source, pl.ds(STARTS[piece], len(PIECES[piece]))]
        return pltpu.make_async_remote_copy(
            src_ref=block,
            dst_ref=block,
            send_sem=sem.at[peer if sem is row_send else source, piece],
            recv_sem=row_recv.at[source, piece],
            device_id={"obs": peer},
            device_id_type=MESH,
        )

    def twin(d):
        return lax.rem(chip + d, chips) * 2 + core

    for move in moves[:4]:
        move.wait()
    order = order_ref[...]
    block_of = lax.shift_right_logical(order, shift)
    lane_of = lax.bitwise_and(order, LANES - 1)

    def permuted(row_of_block):
        total = None
        for b in range(n):
            row = jnp.broadcast_to(row_of_block(b), (n, LANES))
            picked = lane_gather(row, lane_of)
            total = picked if b == 0 else jnp.where(block_of == b, picked, total)
        return total

    inputs = {"point": point_ref, "resid": resid_ref, "camera": camera_ref}
    targets = [twin(d) for d in range(1, chips)] + [sibling]
    for piece in range(len(PIECES)):
        for i, (name, r) in enumerate(PIECES[piece]):
            ref = inputs[name]
            rows_in[me, STARTS[piece] + i] = permuted(
                lambda b: ref[r : r + 1, b * LANES : (b + 1) * LANES]
            )
        if piece == 0:
            pl.semaphore_wait(barrier, n - 1 + n_row - 1)
        for peer in targets:
            rows_copy(me, piece, peer, row_send).start()
        if piece == 0:
            for move in moves[4:]:
                move.wait()
            for x in range(n):
                staged[x] = jnp.zeros((SUBLANES, LANES), jnp.int32)
                staged[x, 0:ranks] = partner_ref[:, x * LANES : (x + 1) * LANES]
            for d in range(1, n):
                ids_copy(lax.rem(me + d, n), me).start()
    part[pl.ds(pl.multiple_of(me * SUBLANES, SUBLANES), SUBLANES), :] = staged[me]

    cam = permuted(lambda b: ids_ref[b : b + 1, :])
    ids = lax.broadcasted_iota(jnp.int32, (cameras, LANES), 0)
    halves = [
        jnp.where(ids == cam[j : j + 1, :], 1.0, 0.0).astype(jnp.bfloat16) for j in range(n)
    ]
    for i in range(n // 2):
        marks[i] = jnp.concatenate([halves[2 * i], halves[2 * i + 1]], axis=1)
    for j in range(n):
        pairs[pl.ds(j, ranks, stride=n), :] = pair_ref[:, j * LANES : (j + 1) * LANES]
    turned[...] = jnp.zeros_like(turned)

    for d in range(1, n):
        peer = lax.rem(me + d, n)
        ids_copy(peer, peer).wait_recv()
    sources, places, offsets = [], [], []
    for k in range(ranks):
        slot = part[pl.ds(k, n, stride=SUBLANES), :]
        pair = pairs[pl.ds(k * n, n), :]
        sources.append(
            jnp.where(pair == cameras * NBR, -1, lax.shift_right_logical(slot, shift))
        )
        places.append(lax.bitwise_and(slot, LANES - 1))
        offsets.append(pair - cam * NBR)

    def find_partner(x, carry):
        place = jnp.zeros((n, LANES), jnp.int32)
        offset = jnp.full((n, LANES), -1, jnp.int32)
        for k in range(ranks):
            match = sources[k] == x
            place = jnp.where(match, places[k], place)
            offset = jnp.where(match, offsets[k], offset)
        offset_of[x] = offset
        place_of[x] = place
        return carry

    lax.fori_loop(0, n, find_partner, 0)

    def pass_on(piece):
        for d in range(1, chips):
            rows_copy(twin(d), piece, sibling, row_send).wait_recv()
            rows_copy(twin(d), piece, sibling, pass_send).start()

    def each_source(piece, visit, carry):
        carry = visit(me, carry)
        rows_copy(sibling, piece, sibling, row_send).wait_recv()
        carry = visit(sibling, carry)
        carry = lax.fori_loop(1, chips, lambda d, c: visit(twin(d), c), carry)

        def passed(d, c):
            x = lax.rem(chip + d, chips) * 2 + 1 - core
            rows_copy(x, piece, sibling, pass_send).wait_recv()
            return visit(x, c)

        return lax.fori_loop(1, chips, passed, carry)

    def gathered(x, piece):
        place = place_of[x]
        found = offset_of[x] >= 0
        return [
            jnp.where(found, lane_gather(rows_in[x, STARTS[piece] + i], place), 0.0)
            for i in range(len(PIECES[piece]))
        ]

    def add_source(x, totals):
        values = gathered(x, 0)
        for i, value in enumerate(values):
            rows_of[x, i] = value
        return tuple(t + v for t, v in zip(totals, normal_rows(values[0:8])))

    pass_on(0)
    totals = tuple(normal_rows([rows_in[me, f] for f in range(8)]))
    totals = each_source(0, add_source, totals)
    pivot_one = jnp.sqrt(totals[0] + 1.0)
    inv_one = 1.0 / pivot_one
    low_one = totals[1] * inv_one
    low_two = totals[2] * inv_one
    inv_two = 1.0 / jnp.sqrt(totals[3] + 1.0 - low_one * low_one)
    low_mid = (totals[4] - low_two * low_one) * inv_two
    inv_three = 1.0 / jnp.sqrt(totals[5] + 1.0 - low_two * low_two - low_mid * low_mid)
    h_one = totals[6] * inv_one
    h_two = (totals[7] - low_one * h_one) * inv_two
    h_three = (totals[8] - low_two * h_one - low_mid * h_two) * inv_three

    def solved(rows):
        result = []
        for i in range(2):
            jp = [rows(3 * i + c) for c in range(3)]
            one = jp[0] * inv_one
            two = (jp[1] - low_one * one) * inv_two
            three = (jp[2] - low_two * one - low_mid * two) * inv_three
            result.append((one, two, three))
        return result

    def put(row, value):
        prod[pl.ds(pl.multiple_of(row * n, n), n), :] = value

    jac = [rows_in[me, PLACE["camera", f]] for f in range(18)]
    weight = solved(lambda f: rows_in[me, f])
    mine = [
        [jac[p] * weight[0][c] + jac[9 + p] * weight[1][c] for p in range(9)] for c in range(3)
    ]
    for c in range(3):
        for p in range(9):
            own[c * 9 + p] = -mine[c][p]
    base = NBR * 9
    for p in range(9):
        for q in range(p, 9):
            value = jac[p] * jac[q] + jac[9 + p] * jac[9 + q]
            value = value - (
                mine[0][p] * mine[0][q] + mine[1][p] * mine[1][q] + mine[2][p] * mine[2][q]
            )
            put(base + 9 * p + q, value)
            if q != p:
                put(base + 9 * q + p, value)
        back = mine[0][p] * h_one + mine[1][p] * h_two + mine[2][p] * h_three
        put(base + 81 + p, jac[p] * rows_in[me, 6] + jac[9 + p] * rows_in[me, 7] - back)

    def solve_source(x, carry):
        got = solved(lambda f: rows_of[x, f])
        for i in range(2):
            for c in range(3):
                normal_of[x, 3 * i + c] = got[i][c]
        for c in range(3):
            factor_of[x, c] = rows_of[x, 8] * got[0][c] + rows_of[x, 9] * got[1][c]
        return carry

    lax.fori_loop(0, n, solve_source, 0)

    contract = (((1,), (1,)), ((), ()))

    def sum_copy(peer, slot, chunk):
        return pltpu.make_async_remote_copy(
            src_ref=partial.at[chunk, pl.ds(pl.multiple_of(peer * CAM_ROW, CAM_ROW), CAM_ROW)],
            dst_ref=landed.at[slot, chunk],
            send_sem=sum_send.at[peer, chunk],
            recv_sem=sum_recv.at[slot, chunk],
            device_id={"row": peer},
            device_id_type=MESH,
        )

    for chunk, columns in enumerate(COLUMNS):
        width = len(columns)
        if chunk > 0:

            def make_factors(x, carry):
                values = gathered(x, chunk)
                for c in range(3):
                    for i in range(width):
                        factor_of[x, c * width + i] = (
                            values[i] * normal_of[x, c] + values[width + i] * normal_of[x, 3 + c]
                        )
                return carry

            each_source(chunk, make_factors, 0)
        if chunk + 1 < len(COLUMNS):
            pass_on(chunk + 1)

        def at_offset(o, carry):
            picked = [None] * (3 * width)
            for x in range(n):
                match = offset_of[x] == o
                for i in range(3 * width):
                    value = jnp.where(match, factor_of[x, i], 0.0)
                    picked[i] = value if x == 0 else picked[i] + value
            for p in range(9):
                left = [own[c * 9 + p] for c in range(3)]
                for i in range(width):
                    value = (
                        left[0] * picked[i]
                        + left[1] * picked[width + i]
                        + left[2] * picked[2 * width + i]
                    )
                    put(o * (9 * width) + i * 9 + p, value)
            return carry

        lax.fori_loop(0, NBR, at_offset, 0)
        total = jnp.zeros((cameras, CHUNK), jnp.float32)
        for i in range(n // 2):
            first = prod[pl.ds(2 * i, CHUNK, stride=n), :]
            second = prod[pl.ds(2 * i + 1, CHUNK, stride=n), :]
            both = jnp.concatenate([first, second], axis=1)
            high = both.astype(jnp.bfloat16)
            low = (both - high.astype(jnp.float32)).astype(jnp.bfloat16)
            for half in (high, low):
                total += lax.dot_general(
                    marks[i], half, contract, preferred_element_type=jnp.float32
                )
        partial[chunk] = total
        for d in range(1, n_row):
            sum_copy(lax.rem(my_row + d, n_row), my_row, chunk).start()

    slots = pair_out_ref.shape[1]
    lane = lax.broadcasted_iota(jnp.int32, (slots, slots), 1)
    line = lax.broadcasted_iota(jnp.int32, (slots, slots), 0)
    chosen = lane == lax.rem(line, CAM_ROW) * NBR + line // CAM_ROW
    select = jnp.where(chosen, 1.0, 0.0).astype(jnp.bfloat16)
    for chunk, columns in enumerate(COLUMNS):
        total = partial[chunk, pl.ds(pl.multiple_of(my_row * CAM_ROW, CAM_ROW), CAM_ROW), :]
        for d in range(1, n_row):
            peer = lax.rem(my_row + d, n_row)
            sum_copy(peer, peer, chunk).wait_recv()
            total = total + landed[peer, chunk]
        height = 9 * len(columns)
        for o in range(NBR):
            turned[o * CAM_ROW : (o + 1) * CAM_ROW, 0:height] = total[
                :, o * height : (o + 1) * height
            ]
        flipped = turned[...].T
        rows = flipped[0:24, 0:slots]
        high = rows.astype(jnp.bfloat16)
        low = (rows - high.astype(jnp.float32)).astype(jnp.bfloat16)
        placed = jnp.dot(high, select, preferred_element_type=jnp.float32)
        placed = placed + jnp.dot(low, select, preferred_element_type=jnp.float32)
        for i, q in enumerate(columns):
            for p in range(9):
                row = i * 9 + p
                pair_out_ref[9 * p + q : 9 * p + q + 1, :] = placed[row : row + 1]
        if chunk == 0:
            hessian_ref[...] = total[:, base : base + 81]
            turned[0:CAM_ROW, 0:9] = total[:, base + 81 : base + 90]
            gradient_ref[...] = turned[0:LANES].T[0:9, 0:CAM_ROW]

    for d in range(1, n):
        ids_copy(lax.rem(me + d, n), me).wait_send()
    for piece in range(len(PIECES)):
        for peer in targets:
            rows_copy(me, piece, peer, row_send).wait_send()
        for d in range(1, chips):
            rows_copy(twin(d), piece, sibling, pass_send).wait_send()
    for chunk in range(len(COLUMNS)):
        for d in range(1, n_row):
            sum_copy(lax.rem(my_row + d, n_row), my_row, chunk).wait_send()


def store_kernel(*refs):
    held, load_sem, store_sem = refs[6:9], refs[9], refs[10]
    loads = [pltpu.make_async_copy(refs[i], held[i], load_sem.at[i]) for i in range(3)]
    stores = [pltpu.make_async_copy(held[i], refs[3 + i], store_sem.at[i]) for i in range(3)]
    for load in loads:
        load.start()
    for load, store in zip(loads, stores):
        load.wait()
        store.start()
    for store in stores:
        store.wait()


def by_lanes(
    camera_jacobian, point_jacobian, residual, send_order, camera_of, track_of, partner, pair_slot
):
    n = lax.axis_size("obs")
    n_row = lax.axis_size("row")
    cameras = CAM_ROW * n_row
    ranks = partner.shape[0]
    chunks = len(COLUMNS)
    vmem = pl.BlockSpec(memory_space=pltpu.VMEM)
    hbm = pl.BlockSpec(memory_space=pltpu.HBM)
    f32, i32 = jnp.float32, jnp.int32
    dma = pltpu.SemaphoreType.DMA
    results = pl.pallas_call(
        functools.partial(step_kernel, n, n_row, cameras),
        out_shape=(
            jax.ShapeDtypeStruct((CAM_ROW, 81), f32),
            jax.ShapeDtypeStruct((9, CAM_ROW), f32),
            jax.ShapeDtypeStruct((81, CAM_ROW * NBR), f32),
        ),
        in_specs=[hbm] * 7,
        out_specs=(vmem, vmem, vmem),
        scratch_shapes=[
            pltpu.VMEM(camera_jacobian.shape, f32),
            pltpu.VMEM(point_jacobian.shape, f32),
            pltpu.VMEM(residual.shape, f32),
            pltpu.VMEM((n, LANES), i32),
            pltpu.VMEM((n, LANES), i32),
            pltpu.VMEM(partner.shape, i32),
            pltpu.VMEM(pair_slot.shape, i32),
            dma((7,)),
            pltpu.VMEM((n, 26, n, LANES), f32),
            pltpu.VMEM((n * SUBLANES, LANES), i32),
            pltpu.VMEM((n, SUBLANES, LANES), i32),
            pltpu.VMEM((ranks * n, LANES), i32),
            pltpu.VMEM((n, len(PIECES[0]), n, LANES), f32),
            pltpu.VMEM((n, n, LANES), i32),
            pltpu.VMEM((n, n, LANES), i32),
            pltpu.VMEM((27, n, LANES), f32),
            pltpu.VMEM((n, 6, n, LANES), f32),
            pltpu.VMEM((n, 6, n, LANES), f32),
            pltpu.VMEM((CHUNK * n, LANES), f32),
            pltpu.VMEM((n // 2, cameras, 2 * LANES), jnp.bfloat16),
            pltpu.VMEM((chunks, cameras, CHUNK), f32),
            pltpu.VMEM((n_row, chunks, CAM_ROW, CHUNK), f32),
            pltpu.VMEM((2 * LANES, LANES), f32),
            dma((n,)),
            dma((n,)),
            dma((n, len(PIECES))),
            dma((n, len(PIECES))),
            dma((n, len(PIECES))),
            dma((n_row, chunks)),
            dma((n_row, chunks)),
        ],
        compiler_params=pltpu.CompilerParams(
            collective_id=0, has_side_effects=True, vmem_limit_bytes=VMEM_BYTES
        ),
        name="gauss_newton_step",
    )(
        camera_jacobian,
        point_jacobian,
        residual,
        send_order.reshape(n, LANES),
        camera_of.reshape(n, LANES),
        partner,
        pair_slot,
    )
    hessian, gradient, pair_hessian = pl.pallas_call(
        store_kernel,
        out_shape=tuple(jax.ShapeDtypeStruct(r.shape, r.dtype) for r in results),
        in_specs=[hbm] * 3,
        out_specs=(hbm,) * 3,
        scratch_shapes=[pltpu.VMEM(r.shape, r.dtype) for r in results] + [dma((3,)), dma((3,))],
        compiler_params=pltpu.CompilerParams(vmem_limit_bytes=VMEM_BYTES),
        name="store",
    )(*results)
    return (hessian.T, gradient, pair_hessian)


damping = 1.0


def eliminate(camera_rows, point_rows, resid_rows, track_of, track_count):
    camera = camera_rows.reshape(2, 9, -1)
    point_jac = point_rows.reshape(2, 3, -1)
    normal = jnp.stack(
        [
            point_jac[0, 0] * point_jac[0, 0] + point_jac[1, 0] * point_jac[1, 0],
            point_jac[0, 0] * point_jac[0, 1] + point_jac[1, 0] * point_jac[1, 1],
            point_jac[0, 0] * point_jac[0, 2] + point_jac[1, 0] * point_jac[1, 2],
            point_jac[0, 1] * point_jac[0, 1] + point_jac[1, 1] * point_jac[1, 1],
            point_jac[0, 1] * point_jac[0, 2] + point_jac[1, 1] * point_jac[1, 2],
            point_jac[0, 2] * point_jac[0, 2] + point_jac[1, 2] * point_jac[1, 2],
            point_jac[0, 0] * resid_rows[0] + point_jac[1, 0] * resid_rows[1],
            point_jac[0, 1] * resid_rows[0] + point_jac[1, 1] * resid_rows[1],
            point_jac[0, 2] * resid_rows[0] + point_jac[1, 2] * resid_rows[1],
        ]
    )
    totals = jnp.zeros((9, track_count), jnp.float32).at[:, track_of].add(normal)
    pivot_first = jnp.sqrt(totals[0] + damping)
    lower_one = totals[1] / pivot_first
    lower_two = totals[2] / pivot_first
    pivot_second = jnp.sqrt(totals[3] + damping - lower_one * lower_one)
    lower_mid = (totals[4] - lower_two * lower_one) / pivot_second
    pivot_third = jnp.sqrt(totals[5] + damping - lower_two * lower_two - lower_mid * lower_mid)
    solved_one = totals[6] / pivot_first
    solved_two = (totals[7] - lower_one * solved_one) / pivot_second
    solved_three = (totals[8] - lower_two * solved_one - lower_mid * solved_two) / pivot_third
    per_track = jnp.stack(
        [
            pivot_first,
            lower_one,
            lower_two,
            pivot_second,
            lower_mid,
            pivot_third,
            solved_one,
            solved_two,
            solved_three,
        ]
    )
    per_obs = per_track[:, track_of]
    weights = (
        camera[0][:, None, :] * point_jac[0][None, :, :]
        + camera[1][:, None, :] * point_jac[1][None, :, :]
    )
    column_one = weights[:, 0] / per_obs[0]
    column_two = (weights[:, 1] - per_obs[1] * column_one) / per_obs[3]
    column_three = (weights[:, 2] - per_obs[2] * column_one - per_obs[4] * column_two) / per_obs[5]
    factor = jnp.stack([column_one, column_two, column_three])
    point_shift = column_one * per_obs[6] + column_two * per_obs[7] + column_three * per_obs[8]
    return (factor, point_shift)


def camera_terms(camera_rows, resid_rows, factor, point_shift):
    camera = camera_rows.reshape(2, 9, -1)
    normal = (
        camera[0][:, None, :] * camera[0][None, :, :]
        + camera[1][:, None, :] * camera[1][None, :, :]
    )
    schur_part = (
        factor[0][:, None, :] * factor[0][None, :, :]
        + factor[1][:, None, :] * factor[1][None, :, :]
        + factor[2][:, None, :] * factor[2][None, :, :]
    )
    gradient = camera[0] * resid_rows[0] + camera[1] * resid_rows[1] - point_shift
    return jnp.concatenate([(normal - schur_part).reshape(81, -1), gradient], axis=0)


def pair_product(left, right):
    total = (
        left[0][:, None] * right[0][None, :]
        + left[1][:, None] * right[1][None, :]
        + left[2][:, None] * right[2][None, :]
    )
    return -total.reshape(81, -1)


def on_device(
    camera_jacobian, point_jacobian, residual, send_order, camera_of, track_of, partner, pair_slot
):
    obs_count = camera_jacobian.shape[1]
    ranks = partner.shape[0]
    camera_count = CAM_ROW * lax.axis_size("row")
    slot_count = camera_count * NBR
    stacked = jnp.concatenate([camera_jacobian, point_jacobian, residual], axis=0)
    sent = jnp.take(stacked, send_order, axis=1)
    owned = lax.all_to_all(sent, "obs", split_axis=1, concat_axis=1, tiled=True)
    factor, point_shift = eliminate(
        owned[:18], owned[18:24], owned[24:26], track_of, obs_count // 2
    )
    flat_factor = factor.reshape(27, obs_count)
    chosen = jnp.take(flat_factor, partner.reshape(-1), axis=1)
    together = jnp.concatenate(
        [
            flat_factor,
            point_shift,
            chosen.reshape(27, ranks, obs_count).reshape(27 * ranks, obs_count),
        ],
        axis=0,
    )
    back = lax.all_to_all(together, "obs", split_axis=1, concat_axis=1, tiled=True)
    factor_back = back[:27].reshape(3, 9, obs_count)
    shift_back = back[27:36]
    remote = back[36:].reshape(3, 9, ranks, obs_count)
    arrived = pair_product(factor_back[:, :, None, :], remote)
    local_terms = camera_terms(sent[:18], sent[24:26], factor_back, shift_back)
    camera_ids = jnp.take(camera_of, send_order)
    indicator = (camera_ids[:, None] == jnp.arange(camera_count, dtype=jnp.int32)[None, :]).astype(
        jnp.float32
    )
    camera_partial = jnp.dot(
        local_terms, indicator, precision=lax.Precision.HIGHEST, preferred_element_type=jnp.float32
    )
    camera_mine = lax.psum_scatter(camera_partial, "row", scatter_dimension=1, tiled=True)
    pair_total = (
        jnp.zeros((81, slot_count + 1), jnp.float32).at[:, pair_slot.reshape(-1)].add(arrived)
    )
    pair_mine = lax.psum_scatter(pair_total[:, :slot_count], "row", scatter_dimension=1, tiled=True)
    return (camera_mine[:81], camera_mine[81:], pair_mine)


def on_mesh(*arguments):
    share = arguments[0].shape[1] // lax.axis_size("obs")
    if share == LANES and lax.axis_size("obs") % 2 == 0:
        return by_lanes(*arguments)
    return on_device(*arguments)


def solution(mesh):
    return jax.shard_map(
        on_mesh,
        mesh=mesh,
        in_specs=(
            P(None, ("obs", "row")),
            P(None, ("obs", "row")),
            P(None, ("obs", "row")),
            P(("obs", "row")),
            P(("obs", "row")),
            P(("obs", "row")),
            P(None, ("obs", "row")),
            P(None, ("obs", "row")),
        ),
        out_specs=(P(None, ("obs", "row")), P(None, ("obs", "row")), P(None, ("obs", "row"))),
        check_vma=False,
    )
```

```python
import functools

import jax
import jax.numpy as jnp
from jax import lax
from jax.experimental import pallas as pl
from jax.experimental.pallas import tpu as pltpu
from jax.sharding import PartitionSpec as P

CAM_ROW = 16
NBR = 14
LANES = 128
SUBLANES = 8
CHUNK = 256
MESH = pl.DeviceIdType.MESH
VMEM_BYTES = 64 * 1024 * 1024


COLUMNS = [[8], [0, 1, 2, 3], [4, 5, 6, 7]]
PIECES = [
    [("point", f) for f in range(6)]
    + [("resid", f) for f in range(2)]
    + [("camera", 8), ("camera", 17)]
] + [[("camera", q + 9 * i) for i in range(2) for q in pair] for pair in COLUMNS[1:]]
TERMS = [NBR * 9 * len(columns) + (90 if k == 0 else 0) for k, columns in enumerate(COLUMNS)]
SIZES = [-(-rows // CHUNK) * CHUNK for rows in TERMS]
TABLE = [entry for piece in PIECES for entry in piece]
STARTS = [sum(len(piece) for piece in PIECES[:k]) for k in range(len(PIECES))]
PLACE = {entry: i for i, entry in enumerate(TABLE)}


def lane_gather(values, index):
    return jnp.take_along_axis(values, index, axis=1, mode="promise_in_bounds")


def normal_rows(camera_point):
    a, b, e = camera_point[0:3], camera_point[3:6], camera_point[6:8]
    return [
        a[0] * a[0] + b[0] * b[0],
        a[0] * a[1] + b[0] * b[1],
        a[0] * a[2] + b[0] * b[2],
        a[1] * a[1] + b[1] * b[1],
        a[1] * a[2] + b[1] * b[2],
        a[2] * a[2] + b[2] * b[2],
        a[0] * e[0] + b[0] * e[1],
        a[1] * e[0] + b[1] * e[1],
        a[2] * e[0] + b[2] * e[1],
    ]


def step_kernel(
    n, n_row, cameras,
    camera_in, point_in, resid_in, order_in, ids_in, partner_in, pair_in,
    hessian_ref, gradient_ref, pair_out_ref,
    camera_ref, point_ref, resid_ref, order_ref, ids_ref, partner_ref, pair_ref, load_sem,
    rows_in, part, staged, pairs, rows_of, offset_of, place_of, own, normal_of, factor_of, prod,
    marks,
    partial, landed, turned,
    id_send, id_recv, row_send, row_recv, pass_send, sum_send, sum_recv,
):
    me = lax.axis_index("obs")
    my_row = lax.axis_index("row")
    chips = n // 2
    chip = me // 2
    core = lax.rem(me, 2)
    sibling = chip * 2 + 1 - core
    ranks = partner_ref.shape[0]
    shift = LANES.bit_length() - 1

    moves = [
        pltpu.make_async_copy(source, target, load_sem.at[i])
        for i, (source, target) in enumerate(
            [
                (order_in, order_ref),
                (point_in, point_ref),
                (resid_in, resid_ref),
                (camera_in, camera_ref),
                (partner_in, partner_ref),
                (ids_in, ids_ref),
                (pair_in, pair_ref),
            ]
        )
    ]
    for move in moves:
        move.start()
    barrier = pltpu.get_barrier_semaphore()
    for d in range(1, n):
        pl.semaphore_signal(
            barrier, inc=1, device_id={"obs": lax.rem(me + d, n)}, device_id_type=MESH
        )
    for d in range(1, n_row):
        pl.semaphore_signal(
            barrier, inc=1, device_id={"row": lax.rem(my_row + d, n_row)}, device_id_type=MESH
        )

    def ids_copy(peer, source):
        return pltpu.make_async_remote_copy(
            src_ref=staged.at[peer],
            dst_ref=part.at[pl.ds(pl.multiple_of(source * SUBLANES, SUBLANES), SUBLANES)],
            send_sem=id_send.at[peer],
            recv_sem=id_recv.at[source],
            device_id={"obs": peer},
            device_id_type=MESH,
        )

    def rows_copy(source, piece, peer, sem):
        block = rows_in.at[source, pl.ds(STARTS[piece], len(PIECES[piece]))]
        return pltpu.make_async_remote_copy(
            src_ref=block,
            dst_ref=block,
            send_sem=sem.at[peer if sem is row_send else source, piece],
            recv_sem=row_recv.at[source, piece],
            device_id={"obs": peer},
            device_id_type=MESH,
        )

    def twin(d):
        return lax.rem(chip + d, chips) * 2 + core

    for move in moves[:4]:
        move.wait()
    order = order_ref[...]
    block_of = lax.shift_right_logical(order, shift)
    lane_of = lax.bitwise_and(order, LANES - 1)

    def permuted(row_of_block):
        total = None
        for b in range(n):
            row = jnp.broadcast_to(row_of_block(b), (n, LANES))
            picked = lane_gather(row, lane_of)
            total = picked if b == 0 else jnp.where(block_of == b, picked, total)
        return total

    inputs = {"point": point_ref, "resid": resid_ref, "camera": camera_ref}
    targets = [twin(d) for d in range(1, chips)] + [sibling]
    for piece in range(len(PIECES)):
        for i, (name, r) in enumerate(PIECES[piece]):
            ref = inputs[name]
            rows_in[me, STARTS[piece] + i] = permuted(
                lambda b: ref[r : r + 1, b * LANES : (b + 1) * LANES]
            )
        if piece == 0:
            pl.semaphore_wait(barrier, n - 1 + n_row - 1)
        for peer in targets:
            rows_copy(me, piece, peer, row_send).start()
        if piece == 0:
            for move in moves[4:]:
                move.wait()
            for x in range(n):
                staged[x] = jnp.zeros((SUBLANES, LANES), jnp.int32)
                staged[x, 0:ranks] = partner_ref[:, x * LANES : (x + 1) * LANES]
            for d in range(1, n):
                ids_copy(lax.rem(me + d, n), me).start()
    part[pl.ds(pl.multiple_of(me * SUBLANES, SUBLANES), SUBLANES), :] = staged[me]

    cam = permuted(lambda b: ids_ref[b : b + 1, :])
    ids = lax.broadcasted_iota(jnp.int32, (cameras, LANES), 0)
    halves = [
        jnp.where(ids == cam[j : j + 1, :], 1.0, 0.0).astype(jnp.bfloat16) for j in range(n)
    ]
    for i in range(n // 2):
        marks[i] = jnp.concatenate([halves[2 * i], halves[2 * i + 1]], axis=1)
    for j in range(n):
        pairs[pl.ds(j, ranks, stride=n), :] = pair_ref[:, j * LANES : (j + 1) * LANES]
    turned[...] = jnp.zeros_like(turned)

    for d in range(1, n):
        peer = lax.rem(me + d, n)
        ids_copy(peer, peer).wait_recv()
    sources, places, offsets = [], [], []
    for k in range(ranks):
        slot = part[pl.ds(k, n, stride=SUBLANES), :]
        pair = pairs[pl.ds(k * n, n), :]
        sources.append(
            jnp.where(pair == cameras * NBR, -1, lax.shift_right_logical(slot, shift))
        )
        places.append(lax.bitwise_and(slot, LANES - 1))
        offsets.append(pair - cam * NBR)

    def find_partner(x, carry):
        place = jnp.zeros((n, LANES), jnp.int32)
        offset = jnp.full((n, LANES), -1, jnp.int32)
        for k in range(ranks):
            match = sources[k] == x
            place = jnp.where(match, places[k], place)
            offset = jnp.where(match, offsets[k], offset)
        offset_of[x] = offset
        place_of[x] = place
        return carry

    lax.fori_loop(0, n, find_partner, 0)

    def pass_on(piece):
        for d in range(1, chips):
            rows_copy(twin(d), piece, sibling, row_send).wait_recv()
            rows_copy(twin(d), piece, sibling, pass_send).start()

    def each_source(piece, visit, carry):
        carry = visit(me, carry)
        rows_copy(sibling, piece, sibling, row_send).wait_recv()
        carry = visit(sibling, carry)
        carry = lax.fori_loop(1, chips, lambda d, c: visit(twin(d), c), carry)

        def passed(d, c):
            x = lax.rem(chip + d, chips) * 2 + 1 - core
            rows_copy(x, piece, sibling, pass_send).wait_recv()
            return visit(x, c)

        return lax.fori_loop(1, chips, passed, carry)

    def gathered(x, piece):
        place = place_of[x]
        found = offset_of[x] >= 0
        return [
            jnp.where(found, lane_gather(rows_in[x, STARTS[piece] + i], place), 0.0)
            for i in range(len(PIECES[piece]))
        ]

    def add_source(x, totals):
        values = gathered(x, 0)
        for i, value in enumerate(values):
            rows_of[x, i] = value
        return tuple(t + v for t, v in zip(totals, normal_rows(values[0:8])))

    pass_on(0)
    totals = tuple(normal_rows([rows_in[me, f] for f in range(8)]))
    totals = each_source(0, add_source, totals)
    pivot_one = jnp.sqrt(totals[0] + 1.0)
    inv_one = 1.0 / pivot_one
    low_one = totals[1] * inv_one
    low_two = totals[2] * inv_one
    inv_two = 1.0 / jnp.sqrt(totals[3] + 1.0 - low_one * low_one)
    low_mid = (totals[4] - low_two * low_one) * inv_two
    inv_three = 1.0 / jnp.sqrt(totals[5] + 1.0 - low_two * low_two - low_mid * low_mid)
    h_one = totals[6] * inv_one
    h_two = (totals[7] - low_one * h_one) * inv_two
    h_three = (totals[8] - low_two * h_one - low_mid * h_two) * inv_three

    def solved(rows):
        result = []
        for i in range(2):
            jp = [rows(3 * i + c) for c in range(3)]
            one = jp[0] * inv_one
            two = (jp[1] - low_one * one) * inv_two
            three = (jp[2] - low_two * one - low_mid * two) * inv_three
            result.append((one, two, three))
        return result

    def put(row, value):
        prod[pl.ds(pl.multiple_of(row * n, n), n), :] = value

    jac = [rows_in[me, PLACE["camera", f]] for f in range(18)]
    weight = solved(lambda f: rows_in[me, f])
    mine = [
        [jac[p] * weight[0][c] + jac[9 + p] * weight[1][c] for p in range(9)] for c in range(3)
    ]
    for c in range(3):
        for p in range(9):
            own[c * 9 + p] = -mine[c][p]
    base = NBR * 9
    for p in range(9):
        for q in range(p, 9):
            value = jac[p] * jac[q] + jac[9 + p] * jac[9 + q]
            value = value - (
                mine[0][p] * mine[0][q] + mine[1][p] * mine[1][q] + mine[2][p] * mine[2][q]
            )
            put(base + 9 * p + q, value)
            if q != p:
                put(base + 9 * q + p, value)
        back = mine[0][p] * h_one + mine[1][p] * h_two + mine[2][p] * h_three
        put(base + 81 + p, jac[p] * rows_in[me, 6] + jac[9 + p] * rows_in[me, 7] - back)

    def solve_source(x, carry):
        got = solved(lambda f: rows_of[x, f])
        for i in range(2):
            for c in range(3):
                normal_of[x, 3 * i + c] = got[i][c]
        for c in range(3):
            factor_of[x, c] = rows_of[x, 8] * got[0][c] + rows_of[x, 9] * got[1][c]
        return carry

    lax.fori_loop(0, n, solve_source, 0)

    contract = (((1,), (1,)), ((), ()))

    def sum_copy(peer, slot, chunk):
        return pltpu.make_async_remote_copy(
            src_ref=partial.at[
                chunk,
                pl.ds(pl.multiple_of(peer * CAM_ROW, CAM_ROW), CAM_ROW),
                pl.ds(0, SIZES[chunk]),
            ],
            dst_ref=landed.at[slot, chunk, :, pl.ds(0, SIZES[chunk])],
            send_sem=sum_send.at[peer, chunk],
            recv_sem=sum_recv.at[slot, chunk],
            device_id={"row": peer},
            device_id_type=MESH,
        )

    for chunk, columns in enumerate(COLUMNS):
        width = len(columns)
        if chunk > 0:

            def make_factors(x, carry):
                values = gathered(x, chunk)
                for c in range(3):
                    for i in range(width):
                        factor_of[x, c * width + i] = (
                            values[i] * normal_of[x, c] + values[width + i] * normal_of[x, 3 + c]
                        )
                return carry

            each_source(chunk, make_factors, 0)
        if chunk + 1 < len(COLUMNS):
            pass_on(chunk + 1)

        def at_offset(o, carry):
            picked = [None] * (3 * width)
            for x in range(n):
                match = offset_of[x] == o
                for i in range(3 * width):
                    value = jnp.where(match, factor_of[x, i], 0.0)
                    picked[i] = value if x == 0 else picked[i] + value
            for p in range(9):
                left = [own[c * 9 + p] for c in range(3)]
                for i in range(width):
                    value = (
                        left[0] * picked[i]
                        + left[1] * picked[width + i]
                        + left[2] * picked[2 * width + i]
                    )
                    put(o * (9 * width) + i * 9 + p, value)
            return carry

        lax.fori_loop(0, NBR, at_offset, 0)
        for part_start in range(0, SIZES[chunk], CHUNK):
            total = jnp.zeros((cameras, CHUNK), jnp.float32)
            for i in range(n // 2):
                start = part_start * n + 2 * i
                first = prod[pl.ds(start, CHUNK, stride=n), :]
                second = prod[pl.ds(start + 1, CHUNK, stride=n), :]
                both = jnp.concatenate([first, second], axis=1)
                high = both.astype(jnp.bfloat16)
                low = (both - high.astype(jnp.float32)).astype(jnp.bfloat16)
                for half in (high, low):
                    total += lax.dot_general(
                        marks[i], half, contract, preferred_element_type=jnp.float32
                    )
            partial[chunk, :, part_start : part_start + CHUNK] = total
        for d in range(1, n_row):
            sum_copy(lax.rem(my_row + d, n_row), my_row, chunk).start()

    slots = pair_out_ref.shape[1]
    lane = lax.broadcasted_iota(jnp.int32, (slots, slots), 1)
    line = lax.broadcasted_iota(jnp.int32, (slots, slots), 0)
    chosen = lane == lax.rem(line, CAM_ROW) * NBR + line // CAM_ROW
    select = jnp.where(chosen, 1.0, 0.0).astype(jnp.bfloat16)
    for chunk, columns in enumerate(COLUMNS):
        lanes = pl.ds(0, SIZES[chunk])
        total = partial[
            chunk, pl.ds(pl.multiple_of(my_row * CAM_ROW, CAM_ROW), CAM_ROW), lanes
        ]
        for d in range(1, n_row):
            peer = lax.rem(my_row + d, n_row)
            sum_copy(peer, peer, chunk).wait_recv()
            total = total + landed[peer, chunk, :, lanes]
        height = 9 * len(columns)
        for o in range(NBR):
            turned[o * CAM_ROW : (o + 1) * CAM_ROW, 0:height] = total[
                :, o * height : (o + 1) * height
            ]
        flipped = turned[...].T
        rows = flipped[0 : -(-height // SUBLANES) * SUBLANES, 0:slots]
        high = rows.astype(jnp.bfloat16)
        low = (rows - high.astype(jnp.float32)).astype(jnp.bfloat16)
        placed = jnp.dot(high, select, preferred_element_type=jnp.float32)
        placed = placed + jnp.dot(low, select, preferred_element_type=jnp.float32)
        for i, q in enumerate(columns):
            for p in range(9):
                row = i * 9 + p
                pair_out_ref[9 * p + q : 9 * p + q + 1, :] = placed[row : row + 1]
        if chunk == 0:
            hessian_ref[...] = total[:, base : base + 81]
            turned[0:CAM_ROW, 0:9] = total[:, base + 81 : base + 90]
            gradient_ref[...] = turned[0:LANES].T[0:9, 0:CAM_ROW]

    for d in range(1, n):
        ids_copy(lax.rem(me + d, n), me).wait_send()
    for piece in range(len(PIECES)):
        for peer in targets:
            rows_copy(me, piece, peer, row_send).wait_send()
        for d in range(1, chips):
            rows_copy(twin(d), piece, sibling, pass_send).wait_send()
    for chunk in range(len(COLUMNS)):
        for d in range(1, n_row):
            sum_copy(lax.rem(my_row + d, n_row), my_row, chunk).wait_send()


def store_kernel(*refs):
    held, load_sem, store_sem = refs[6:9], refs[9], refs[10]
    loads = [pltpu.make_async_copy(refs[i], held[i], load_sem.at[i]) for i in range(3)]
    stores = [pltpu.make_async_copy(held[i], refs[3 + i], store_sem.at[i]) for i in range(3)]
    for load in loads:
        load.start()
    for load, store in zip(loads, stores):
        load.wait()
        store.start()
    for store in stores:
        store.wait()


def by_lanes(
    camera_jacobian, point_jacobian, residual, send_order, camera_of, track_of, partner, pair_slot
):
    n = lax.axis_size("obs")
    n_row = lax.axis_size("row")
    cameras = CAM_ROW * n_row
    ranks = partner.shape[0]
    chunks = len(COLUMNS)
    vmem = pl.BlockSpec(memory_space=pltpu.VMEM)
    hbm = pl.BlockSpec(memory_space=pltpu.HBM)
    f32, i32 = jnp.float32, jnp.int32
    dma = pltpu.SemaphoreType.DMA
    results = pl.pallas_call(
        functools.partial(step_kernel, n, n_row, cameras),
        out_shape=(
            jax.ShapeDtypeStruct((CAM_ROW, 81), f32),
            jax.ShapeDtypeStruct((9, CAM_ROW), f32),
            jax.ShapeDtypeStruct((81, CAM_ROW * NBR), f32),
        ),
        in_specs=[hbm] * 7,
        out_specs=(vmem, vmem, vmem),
        scratch_shapes=[
            pltpu.VMEM(camera_jacobian.shape, f32),
            pltpu.VMEM(point_jacobian.shape, f32),
            pltpu.VMEM(residual.shape, f32),
            pltpu.VMEM((n, LANES), i32),
            pltpu.VMEM((n, LANES), i32),
            pltpu.VMEM(partner.shape, i32),
            pltpu.VMEM(pair_slot.shape, i32),
            dma((7,)),
            pltpu.VMEM((n, 26, n, LANES), f32),
            pltpu.VMEM((n * SUBLANES, LANES), i32),
            pltpu.VMEM((n, SUBLANES, LANES), i32),
            pltpu.VMEM((ranks * n, LANES), i32),
            pltpu.VMEM((n, len(PIECES[0]), n, LANES), f32),
            pltpu.VMEM((n, n, LANES), i32),
            pltpu.VMEM((n, n, LANES), i32),
            pltpu.VMEM((27, n, LANES), f32),
            pltpu.VMEM((n, 6, n, LANES), f32),
            pltpu.VMEM((n, 3 * max(len(c) for c in COLUMNS), n, LANES), f32),
            pltpu.VMEM((max(SIZES) * n, LANES), f32),
            pltpu.VMEM((n // 2, cameras, 2 * LANES), jnp.bfloat16),
            pltpu.VMEM((chunks, cameras, max(SIZES)), f32),
            pltpu.VMEM((n_row, chunks, CAM_ROW, max(SIZES)), f32),
            pltpu.VMEM((2 * LANES, LANES), f32),
            dma((n,)),
            dma((n,)),
            dma((n, len(PIECES))),
            dma((n, len(PIECES))),
            dma((n, len(PIECES))),
            dma((n_row, chunks)),
            dma((n_row, chunks)),
        ],
        compiler_params=pltpu.CompilerParams(
            collective_id=0, has_side_effects=True, vmem_limit_bytes=VMEM_BYTES
        ),
        name="gauss_newton_step",
    )(
        camera_jacobian,
        point_jacobian,
        residual,
        send_order.reshape(n, LANES),
        camera_of.reshape(n, LANES),
        partner,
        pair_slot,
    )
    hessian, gradient, pair_hessian = pl.pallas_call(
        store_kernel,
        out_shape=tuple(jax.ShapeDtypeStruct(r.shape, r.dtype) for r in results),
        in_specs=[hbm] * 3,
        out_specs=(hbm,) * 3,
        scratch_shapes=[pltpu.VMEM(r.shape, r.dtype) for r in results] + [dma((3,)), dma((3,))],
        compiler_params=pltpu.CompilerParams(vmem_limit_bytes=VMEM_BYTES),
        name="store",
    )(*results)
    return (hessian.T, gradient, pair_hessian)


damping = 1.0


def eliminate(camera_rows, point_rows, resid_rows, track_of, track_count):
    camera = camera_rows.reshape(2, 9, -1)
    point_jac = point_rows.reshape(2, 3, -1)
    normal = jnp.stack(
        [
            point_jac[0, 0] * point_jac[0, 0] + point_jac[1, 0] * point_jac[1, 0],
            point_jac[0, 0] * point_jac[0, 1] + point_jac[1, 0] * point_jac[1, 1],
            point_jac[0, 0] * point_jac[0, 2] + point_jac[1, 0] * point_jac[1, 2],
            point_jac[0, 1] * point_jac[0, 1] + point_jac[1, 1] * point_jac[1, 1],
            point_jac[0, 1] * point_jac[0, 2] + point_jac[1, 1] * point_jac[1, 2],
            point_jac[0, 2] * point_jac[0, 2] + point_jac[1, 2] * point_jac[1, 2],
            point_jac[0, 0] * resid_rows[0] + point_jac[1, 0] * resid_rows[1],
            point_jac[0, 1] * resid_rows[0] + point_jac[1, 1] * resid_rows[1],
            point_jac[0, 2] * resid_rows[0] + point_jac[1, 2] * resid_rows[1],
        ]
    )
    totals = jnp.zeros((9, track_count), jnp.float32).at[:, track_of].add(normal)
    pivot_first = jnp.sqrt(totals[0] + damping)
    lower_one = totals[1] / pivot_first
    lower_two = totals[2] / pivot_first
    pivot_second = jnp.sqrt(totals[3] + damping - lower_one * lower_one)
    lower_mid = (totals[4] - lower_two * lower_one) / pivot_second
    pivot_third = jnp.sqrt(totals[5] + damping - lower_two * lower_two - lower_mid * lower_mid)
    solved_one = totals[6] / pivot_first
    solved_two = (totals[7] - lower_one * solved_one) / pivot_second
    solved_three = (totals[8] - lower_two * solved_one - lower_mid * solved_two) / pivot_third
    per_track = jnp.stack(
        [
            pivot_first,
            lower_one,
            lower_two,
            pivot_second,
            lower_mid,
            pivot_third,
            solved_one,
            solved_two,
            solved_three,
        ]
    )
    per_obs = per_track[:, track_of]
    weights = (
        camera[0][:, None, :] * point_jac[0][None, :, :]
        + camera[1][:, None, :] * point_jac[1][None, :, :]
    )
    column_one = weights[:, 0] / per_obs[0]
    column_two = (weights[:, 1] - per_obs[1] * column_one) / per_obs[3]
    column_three = (weights[:, 2] - per_obs[2] * column_one - per_obs[4] * column_two) / per_obs[5]
    factor = jnp.stack([column_one, column_two, column_three])
    point_shift = column_one * per_obs[6] + column_two * per_obs[7] + column_three * per_obs[8]
    return (factor, point_shift)


def camera_terms(camera_rows, resid_rows, factor, point_shift):
    camera = camera_rows.reshape(2, 9, -1)
    normal = (
        camera[0][:, None, :] * camera[0][None, :, :]
        + camera[1][:, None, :] * camera[1][None, :, :]
    )
    schur_part = (
        factor[0][:, None, :] * factor[0][None, :, :]
        + factor[1][:, None, :] * factor[1][None, :, :]
        + factor[2][:, None, :] * factor[2][None, :, :]
    )
    gradient = camera[0] * resid_rows[0] + camera[1] * resid_rows[1] - point_shift
    return jnp.concatenate([(normal - schur_part).reshape(81, -1), gradient], axis=0)


def pair_product(left, right):
    total = (
        left[0][:, None] * right[0][None, :]
        + left[1][:, None] * right[1][None, :]
        + left[2][:, None] * right[2][None, :]
    )
    return -total.reshape(81, -1)


def on_device(
    camera_jacobian, point_jacobian, residual, send_order, camera_of, track_of, partner, pair_slot
):
    obs_count = camera_jacobian.shape[1]
    ranks = partner.shape[0]
    camera_count = CAM_ROW * lax.axis_size("row")
    slot_count = camera_count * NBR
    stacked = jnp.concatenate([camera_jacobian, point_jacobian, residual], axis=0)
    sent = jnp.take(stacked, send_order, axis=1)
    owned = lax.all_to_all(sent, "obs", split_axis=1, concat_axis=1, tiled=True)
    factor, point_shift = eliminate(
        owned[:18], owned[18:24], owned[24:26], track_of, obs_count // 2
    )
    flat_factor = factor.reshape(27, obs_count)
    chosen = jnp.take(flat_factor, partner.reshape(-1), axis=1)
    together = jnp.concatenate(
        [
            flat_factor,
            point_shift,
            chosen.reshape(27, ranks, obs_count).reshape(27 * ranks, obs_count),
        ],
        axis=0,
    )
    back = lax.all_to_all(together, "obs", split_axis=1, concat_axis=1, tiled=True)
    factor_back = back[:27].reshape(3, 9, obs_count)
    shift_back = back[27:36]
    remote = back[36:].reshape(3, 9, ranks, obs_count)
    arrived = pair_product(factor_back[:, :, None, :], remote)
    local_terms = camera_terms(sent[:18], sent[24:26], factor_back, shift_back)
    camera_ids = jnp.take(camera_of, send_order)
    indicator = (camera_ids[:, None] == jnp.arange(camera_count, dtype=jnp.int32)[None, :]).astype(
        jnp.float32
    )
    camera_partial = jnp.dot(
        local_terms, indicator, precision=lax.Precision.HIGHEST, preferred_element_type=jnp.float32
    )
    camera_mine = lax.psum_scatter(camera_partial, "row", scatter_dimension=1, tiled=True)
    pair_total = (
        jnp.zeros((81, slot_count + 1), jnp.float32).at[:, pair_slot.reshape(-1)].add(arrived)
    )
    pair_mine = lax.psum_scatter(pair_total[:, :slot_count], "row", scatter_dimension=1, tiled=True)
    return (camera_mine[:81], camera_mine[81:], pair_mine)


def on_mesh(*arguments):
    share = arguments[0].shape[1] // lax.axis_size("obs")
    if share == LANES and lax.axis_size("obs") % 2 == 0:
        return by_lanes(*arguments)
    return on_device(*arguments)


def solution(mesh):
    return jax.shard_map(
        on_mesh,
        mesh=mesh,
        in_specs=(
            P(None, ("obs", "row")),
            P(None, ("obs", "row")),
            P(None, ("obs", "row")),
            P(("obs", "row")),
            P(("obs", "row")),
            P(("obs", "row")),
            P(None, ("obs", "row")),
            P(None, ("obs", "row")),
        ),
        out_specs=(P(None, ("obs", "row")), P(None, ("obs", "row")), P(None, ("obs", "row"))),
        check_vma=False,
    )
```

```python
import functools

import jax
import jax.numpy as jnp
from jax import lax
from jax.experimental import pallas as pl
from jax.experimental.pallas import tpu as pltpu
from jax.sharding import PartitionSpec as P

CAM_ROW = 16
NBR = 14
LANES = 128
SUBLANES = 8
CHUNK = 256
MESH = pl.DeviceIdType.MESH
VMEM_BYTES = 32 * 1024 * 1024


COLUMNS = [[8], [0, 1, 2, 3], [4, 5, 6, 7]]
PIECES = [
    [("point", f) for f in range(6)]
    + [("resid", f) for f in range(2)]
    + [("camera", 8), ("camera", 17)]
] + [[("camera", q + 9 * i) for i in range(2) for q in pair] for pair in COLUMNS[1:]]
TERMS = [NBR * 9 * len(columns) + (90 if k == 0 else 0) for k, columns in enumerate(COLUMNS)]
SIZES = [-(-rows // CHUNK) * CHUNK for rows in TERMS]
TABLE = [entry for piece in PIECES for entry in piece]
STARTS = [sum(len(piece) for piece in PIECES[:k]) for k in range(len(PIECES))]
PLACE = {entry: i for i, entry in enumerate(TABLE)}


def lane_gather(values, index):
    return jnp.take_along_axis(values, index, axis=1, mode="promise_in_bounds")


def normal_rows(camera_point):
    a, b, e = camera_point[0:3], camera_point[3:6], camera_point[6:8]
    return [
        a[0] * a[0] + b[0] * b[0],
        a[0] * a[1] + b[0] * b[1],
        a[0] * a[2] + b[0] * b[2],
        a[1] * a[1] + b[1] * b[1],
        a[1] * a[2] + b[1] * b[2],
        a[2] * a[2] + b[2] * b[2],
        a[0] * e[0] + b[0] * e[1],
        a[1] * e[0] + b[1] * e[1],
        a[2] * e[0] + b[2] * e[1],
    ]


def step_kernel(
    n, n_row, cameras,
    camera_in, point_in, resid_in, order_in, ids_in, partner_in, pair_in,
    hessian_ref, gradient_ref, pair_out_ref,
    camera_ref, point_ref, resid_ref, order_ref, ids_ref, partner_ref, pair_ref, load_sem,
    rows_in, part, staged, pairs, rows_of, offset_of, place_of, own, normal_of, factor_of, prod,
    marks,
    partial, landed, turned, placing,
    id_send, id_recv, row_send, row_recv, pass_send, sum_send, sum_recv,
):
    me = lax.axis_index("obs")
    my_row = lax.axis_index("row")
    chips = n // 2
    chip = me // 2
    core = lax.rem(me, 2)
    sibling = chip * 2 + 1 - core
    ranks = partner_ref.shape[0]
    shift = LANES.bit_length() - 1

    moves = [
        pltpu.make_async_copy(source, target, load_sem.at[i])
        for i, (source, target) in enumerate(
            [
                (order_in, order_ref),
                (point_in, point_ref),
                (resid_in, resid_ref),
                (camera_in, camera_ref),
                (partner_in, partner_ref),
                (ids_in, ids_ref),
                (pair_in, pair_ref),
            ]
        )
    ]
    for move in moves:
        move.start()
    barrier = pltpu.get_barrier_semaphore()
    for d in range(1, n):
        pl.semaphore_signal(
            barrier, inc=1, device_id={"obs": lax.rem(me + d, n)}, device_id_type=MESH
        )
    for d in range(1, n_row):
        pl.semaphore_signal(
            barrier, inc=1, device_id={"row": lax.rem(my_row + d, n_row)}, device_id_type=MESH
        )

    def ids_copy(peer, source):
        return pltpu.make_async_remote_copy(
            src_ref=staged.at[peer],
            dst_ref=part.at[pl.ds(pl.multiple_of(source * SUBLANES, SUBLANES), SUBLANES)],
            send_sem=id_send.at[peer],
            recv_sem=id_recv.at[source],
            device_id={"obs": peer},
            device_id_type=MESH,
        )

    def rows_copy(source, piece, peer, sem):
        block = rows_in.at[source, pl.ds(STARTS[piece], len(PIECES[piece]))]
        return pltpu.make_async_remote_copy(
            src_ref=block,
            dst_ref=block,
            send_sem=sem.at[peer if sem is row_send else source, piece],
            recv_sem=row_recv.at[source, piece],
            device_id={"obs": peer},
            device_id_type=MESH,
        )

    def twin(d):
        return lax.rem(chip + d, chips) * 2 + core

    for move in moves[:4]:
        move.wait()
    order = order_ref[...]
    block_of = lax.shift_right_logical(order, shift)
    lane_of = lax.bitwise_and(order, LANES - 1)

    def permuted(row_of_block):
        total = None
        for b in range(n):
            row = jnp.broadcast_to(row_of_block(b), (n, LANES))
            picked = lane_gather(row, lane_of)
            total = picked if b == 0 else jnp.where(block_of == b, picked, total)
        return total

    inputs = {"point": point_ref, "resid": resid_ref, "camera": camera_ref}
    targets = [twin(d) for d in range(1, chips)] + [sibling]
    for piece in range(len(PIECES)):
        for i, (name, r) in enumerate(PIECES[piece]):
            ref = inputs[name]
            rows_in[me, STARTS[piece] + i] = permuted(
                lambda b: ref[r : r + 1, b * LANES : (b + 1) * LANES]
            )
        if piece == 0:
            pl.semaphore_wait(barrier, n - 1 + n_row - 1)
        for peer in targets:
            rows_copy(me, piece, peer, row_send).start()
        if piece == 0:
            for move in moves[4:]:
                move.wait()
            for x in range(n):
                staged[x] = jnp.zeros((SUBLANES, LANES), jnp.int32)
                staged[x, 0:ranks] = partner_ref[:, x * LANES : (x + 1) * LANES]
            for d in range(1, n):
                ids_copy(lax.rem(me + d, n), me).start()
    part[pl.ds(pl.multiple_of(me * SUBLANES, SUBLANES), SUBLANES), :] = staged[me]

    cam = permuted(lambda b: ids_ref[b : b + 1, :])
    ids = lax.broadcasted_iota(jnp.int32, (cameras, LANES), 0)
    halves = [
        jnp.where(ids == cam[j : j + 1, :], 1.0, 0.0).astype(jnp.bfloat16) for j in range(n)
    ]
    for i in range(n // 2):
        marks[i] = jnp.concatenate([halves[2 * i], halves[2 * i + 1]], axis=1)
    for j in range(n):
        pairs[pl.ds(j, ranks, stride=n), :] = pair_ref[:, j * LANES : (j + 1) * LANES]
    turned[...] = jnp.zeros_like(turned)
    slots = pair_out_ref.shape[1]
    lane = lax.broadcasted_iota(jnp.int32, (slots, slots), 1)
    line = lax.broadcasted_iota(jnp.int32, (slots, slots), 0)
    chosen = lane == (
        lax.bitwise_and(line, CAM_ROW - 1) * NBR
        + lax.shift_right_logical(line, CAM_ROW.bit_length() - 1)
    )
    placing[...] = jnp.where(chosen, 1.0, 0.0).astype(jnp.bfloat16)

    for d in range(1, n):
        peer = lax.rem(me + d, n)
        ids_copy(peer, peer).wait_recv()
    sources, places, offsets = [], [], []
    for k in range(ranks):
        slot = part[pl.ds(k, n, stride=SUBLANES), :]
        pair = pairs[pl.ds(k * n, n), :]
        sources.append(
            jnp.where(pair == cameras * NBR, -1, lax.shift_right_logical(slot, shift))
        )
        places.append(lax.bitwise_and(slot, LANES - 1))
        offsets.append(pair - cam * NBR)

    def find_partner(x, carry):
        place = jnp.zeros((n, LANES), jnp.int32)
        offset = jnp.full((n, LANES), -1, jnp.int32)
        for k in range(ranks):
            match = sources[k] == x
            place = jnp.where(match, places[k], place)
            offset = jnp.where(match, offsets[k], offset)
        offset_of[x] = offset
        place_of[x] = place
        return carry

    lax.fori_loop(0, n, find_partner, 0)

    def pass_on(piece):
        for d in range(1, chips):
            rows_copy(twin(d), piece, sibling, row_send).wait_recv()
            rows_copy(twin(d), piece, sibling, pass_send).start()

    def each_source(piece, visit, carry):
        carry = visit(me, carry)
        rows_copy(sibling, piece, sibling, row_send).wait_recv()
        carry = visit(sibling, carry)
        carry = lax.fori_loop(1, chips, lambda d, c: visit(twin(d), c), carry)

        def passed(d, c):
            x = lax.rem(chip + d, chips) * 2 + 1 - core
            rows_copy(x, piece, sibling, pass_send).wait_recv()
            return visit(x, c)

        return lax.fori_loop(1, chips, passed, carry)

    def gathered(x, piece):
        place = place_of[x]
        found = offset_of[x] >= 0
        return [
            jnp.where(found, lane_gather(rows_in[x, STARTS[piece] + i], place), 0.0)
            for i in range(len(PIECES[piece]))
        ]

    def add_source(x, totals):
        values = gathered(x, 0)
        for i, value in enumerate(values):
            rows_of[x, i] = value
        return tuple(t + v for t, v in zip(totals, normal_rows(values[0:8])))

    pass_on(0)
    totals = tuple(normal_rows([rows_in[me, f] for f in range(8)]))
    totals = each_source(0, add_source, totals)
    pivot_one = jnp.sqrt(totals[0] + 1.0)
    inv_one = 1.0 / pivot_one
    low_one = totals[1] * inv_one
    low_two = totals[2] * inv_one
    inv_two = 1.0 / jnp.sqrt(totals[3] + 1.0 - low_one * low_one)
    low_mid = (totals[4] - low_two * low_one) * inv_two
    inv_three = 1.0 / jnp.sqrt(totals[5] + 1.0 - low_two * low_two - low_mid * low_mid)
    h_one = totals[6] * inv_one
    h_two = (totals[7] - low_one * h_one) * inv_two
    h_three = (totals[8] - low_two * h_one - low_mid * h_two) * inv_three

    def solved(rows):
        result = []
        for i in range(2):
            jp = [rows(3 * i + c) for c in range(3)]
            one = jp[0] * inv_one
            two = (jp[1] - low_one * one) * inv_two
            three = (jp[2] - low_two * one - low_mid * two) * inv_three
            result.append((one, two, three))
        return result

    def put(row, value):
        prod[pl.ds(pl.multiple_of(row * n, n), n), :] = value

    jac = [rows_in[me, PLACE["camera", f]] for f in range(18)]
    weight = solved(lambda f: rows_in[me, f])
    mine = [
        [jac[p] * weight[0][c] + jac[9 + p] * weight[1][c] for p in range(9)] for c in range(3)
    ]
    for c in range(3):
        for p in range(9):
            own[c * 9 + p] = -mine[c][p]
    base = NBR * 9
    for p in range(9):
        for q in range(p, 9):
            value = jac[p] * jac[q] + jac[9 + p] * jac[9 + q]
            value = value - (
                mine[0][p] * mine[0][q] + mine[1][p] * mine[1][q] + mine[2][p] * mine[2][q]
            )
            put(base + 9 * p + q, value)
            if q != p:
                put(base + 9 * q + p, value)
        back = mine[0][p] * h_one + mine[1][p] * h_two + mine[2][p] * h_three
        put(base + 81 + p, jac[p] * rows_in[me, 6] + jac[9 + p] * rows_in[me, 7] - back)

    def solve_source(x, carry):
        got = solved(lambda f: rows_of[x, f])
        for i in range(2):
            for c in range(3):
                normal_of[x, 3 * i + c] = got[i][c]
        for c in range(3):
            factor_of[x, c] = rows_of[x, 8] * got[0][c] + rows_of[x, 9] * got[1][c]
        return carry

    lax.fori_loop(0, n, solve_source, 0)

    contract = (((1,), (1,)), ((), ()))

    def sum_copy(peer, slot, chunk):
        return pltpu.make_async_remote_copy(
            src_ref=partial.at[
                chunk,
                pl.ds(pl.multiple_of(peer * CAM_ROW, CAM_ROW), CAM_ROW),
                pl.ds(0, SIZES[chunk]),
            ],
            dst_ref=landed.at[slot, chunk, :, pl.ds(0, SIZES[chunk])],
            send_sem=sum_send.at[peer, chunk],
            recv_sem=sum_recv.at[slot, chunk],
            device_id={"row": peer},
            device_id_type=MESH,
        )

    for chunk, columns in enumerate(COLUMNS):
        width = len(columns)
        if chunk > 0:

            def make_factors(x, carry):
                values = gathered(x, chunk)
                for c in range(3):
                    for i in range(width):
                        factor_of[x, c * width + i] = (
                            values[i] * normal_of[x, c] + values[width + i] * normal_of[x, 3 + c]
                        )
                return carry

            each_source(chunk, make_factors, 0)
        if chunk + 1 < len(COLUMNS):
            pass_on(chunk + 1)

        def at_offset(o, carry):
            picked = [None] * (3 * width)
            for x in range(n):
                match = offset_of[x] == o
                for i in range(3 * width):
                    value = jnp.where(match, factor_of[x, i], 0.0)
                    picked[i] = value if x == 0 else picked[i] + value
            for p in range(9):
                left = [own[c * 9 + p] for c in range(3)]
                for i in range(width):
                    value = (
                        left[0] * picked[i]
                        + left[1] * picked[width + i]
                        + left[2] * picked[2 * width + i]
                    )
                    put(o * (9 * width) + i * 9 + p, value)
            return carry

        lax.fori_loop(0, NBR, at_offset, 0)
        for part_start in range(0, SIZES[chunk], CHUNK):
            total = jnp.zeros((cameras, CHUNK), jnp.float32)
            for i in range(n // 2):
                start = part_start * n + 2 * i
                first = prod[pl.ds(start, CHUNK, stride=n), :]
                second = prod[pl.ds(start + 1, CHUNK, stride=n), :]
                both = jnp.concatenate([first, second], axis=1)
                high = both.astype(jnp.bfloat16)
                low = (both - high.astype(jnp.float32)).astype(jnp.bfloat16)
                for half in (high, low):
                    total += lax.dot_general(
                        marks[i], half, contract, preferred_element_type=jnp.float32
                    )
            partial[chunk, :, part_start : part_start + CHUNK] = total
        for d in range(1, n_row):
            sum_copy(lax.rem(my_row + d, n_row), my_row, chunk).start()

    select = placing[...]
    for chunk, columns in enumerate(COLUMNS):
        lanes = pl.ds(0, SIZES[chunk])
        total = partial[
            chunk, pl.ds(pl.multiple_of(my_row * CAM_ROW, CAM_ROW), CAM_ROW), lanes
        ]
        for d in range(1, n_row):
            peer = lax.rem(my_row + d, n_row)
            sum_copy(peer, peer, chunk).wait_recv()
            total = total + landed[peer, chunk, :, lanes]
        height = 9 * len(columns)
        for o in range(NBR):
            turned[o * CAM_ROW : (o + 1) * CAM_ROW, 0:height] = total[
                :, o * height : (o + 1) * height
            ]
        flipped = turned[...].T
        rows = flipped[0 : -(-height // SUBLANES) * SUBLANES, 0:slots]
        high = rows.astype(jnp.bfloat16)
        low = (rows - high.astype(jnp.float32)).astype(jnp.bfloat16)
        placed = jnp.dot(high, select, preferred_element_type=jnp.float32)
        placed = placed + jnp.dot(low, select, preferred_element_type=jnp.float32)
        for i, q in enumerate(columns):
            for p in range(9):
                row = i * 9 + p
                pair_out_ref[9 * p + q : 9 * p + q + 1, :] = placed[row : row + 1]
        if chunk == 0:
            hessian_ref[...] = total[:, base : base + 81]
            turned[0:CAM_ROW, 0:9] = total[:, base + 81 : base + 90]
            gradient_ref[...] = turned[0:LANES].T[0:9, 0:CAM_ROW]

    for d in range(1, n):
        ids_copy(lax.rem(me + d, n), me).wait_send()
    for piece in range(len(PIECES)):
        for peer in targets:
            rows_copy(me, piece, peer, row_send).wait_send()
        for d in range(1, chips):
            rows_copy(twin(d), piece, sibling, pass_send).wait_send()
    for chunk in range(len(COLUMNS)):
        for d in range(1, n_row):
            sum_copy(lax.rem(my_row + d, n_row), my_row, chunk).wait_send()


def store_kernel(*refs):
    copies = [
        pltpu.make_async_copy(refs[i], refs[3 + i], refs[6].at[i]) for i in range(3)
    ]
    for copy in copies:
        copy.start()
    for copy in copies:
        copy.wait()


def by_lanes(
    camera_jacobian, point_jacobian, residual, send_order, camera_of, track_of, partner, pair_slot
):
    n = lax.axis_size("obs")
    n_row = lax.axis_size("row")
    cameras = CAM_ROW * n_row
    ranks = partner.shape[0]
    chunks = len(COLUMNS)
    vmem = pl.BlockSpec(memory_space=pltpu.VMEM)
    hbm = pl.BlockSpec(memory_space=pltpu.HBM)
    f32, i32 = jnp.float32, jnp.int32
    dma = pltpu.SemaphoreType.DMA
    results = pl.pallas_call(
        functools.partial(step_kernel, n, n_row, cameras),
        out_shape=(
            pltpu.VMEM((CAM_ROW, 81), f32),
            pltpu.VMEM((9, CAM_ROW), f32),
            pltpu.VMEM((81, CAM_ROW * NBR), f32),
        ),
        in_specs=[hbm] * 7,
        out_specs=(vmem, vmem, vmem),
        scratch_shapes=[
            pltpu.VMEM(camera_jacobian.shape, f32),
            pltpu.VMEM(point_jacobian.shape, f32),
            pltpu.VMEM(residual.shape, f32),
            pltpu.VMEM((n, LANES), i32),
            pltpu.VMEM((n, LANES), i32),
            pltpu.VMEM(partner.shape, i32),
            pltpu.VMEM(pair_slot.shape, i32),
            dma((7,)),
            pltpu.VMEM((n, 26, n, LANES), f32),
            pltpu.VMEM((n * SUBLANES, LANES), i32),
            pltpu.VMEM((n, SUBLANES, LANES), i32),
            pltpu.VMEM((ranks * n, LANES), i32),
            pltpu.VMEM((n, len(PIECES[0]), n, LANES), f32),
            pltpu.VMEM((n, n, LANES), i32),
            pltpu.VMEM((n, n, LANES), i32),
            pltpu.VMEM((27, n, LANES), f32),
            pltpu.VMEM((n, 6, n, LANES), f32),
            pltpu.VMEM((n, 3 * max(len(c) for c in COLUMNS), n, LANES), f32),
            pltpu.VMEM((max(SIZES) * n, LANES), f32),
            pltpu.VMEM((n // 2, cameras, 2 * LANES), jnp.bfloat16),
            pltpu.VMEM((chunks, cameras, max(SIZES)), f32),
            pltpu.VMEM((n_row, chunks, CAM_ROW, max(SIZES)), f32),
            pltpu.VMEM((2 * LANES, LANES), f32),
            pltpu.VMEM((CAM_ROW * NBR, CAM_ROW * NBR), jnp.bfloat16),
            dma((n,)),
            dma((n,)),
            dma((n, len(PIECES))),
            dma((n, len(PIECES))),
            dma((n, len(PIECES))),
            dma((n_row, chunks)),
            dma((n_row, chunks)),
        ],
        compiler_params=pltpu.CompilerParams(
            collective_id=0, has_side_effects=True, vmem_limit_bytes=VMEM_BYTES
        ),
        name="gauss_newton_step",
    )(
        *(
            pltpu.with_memory_space_constraint(value, pltpu.HBM)
            for value in (
                camera_jacobian,
                point_jacobian,
                residual,
                send_order.reshape(n, LANES),
                camera_of.reshape(n, LANES),
                partner,
                pair_slot,
            )
        )
    )
    hessian, gradient, pair_hessian = pl.pallas_call(
        store_kernel,
        out_shape=tuple(pltpu.HBM(r.shape, r.dtype) for r in results),
        in_specs=[vmem] * 3,
        out_specs=(hbm,) * 3,
        scratch_shapes=[dma((3,))],
        name="store",
    )(*results)
    return (hessian.T, gradient, pair_hessian)


damping = 1.0


def eliminate(camera_rows, point_rows, resid_rows, track_of, track_count):
    camera = camera_rows.reshape(2, 9, -1)
    point_jac = point_rows.reshape(2, 3, -1)
    normal = jnp.stack(
        [
            point_jac[0, 0] * point_jac[0, 0] + point_jac[1, 0] * point_jac[1, 0],
            point_jac[0, 0] * point_jac[0, 1] + point_jac[1, 0] * point_jac[1, 1],
            point_jac[0, 0] * point_jac[0, 2] + point_jac[1, 0] * point_jac[1, 2],
            point_jac[0, 1] * point_jac[0, 1] + point_jac[1, 1] * point_jac[1, 1],
            point_jac[0, 1] * point_jac[0, 2] + point_jac[1, 1] * point_jac[1, 2],
            point_jac[0, 2] * point_jac[0, 2] + point_jac[1, 2] * point_jac[1, 2],
            point_jac[0, 0] * resid_rows[0] + point_jac[1, 0] * resid_rows[1],
            point_jac[0, 1] * resid_rows[0] + point_jac[1, 1] * resid_rows[1],
            point_jac[0, 2] * resid_rows[0] + point_jac[1, 2] * resid_rows[1],
        ]
    )
    totals = jnp.zeros((9, track_count), jnp.float32).at[:, track_of].add(normal)
    pivot_first = jnp.sqrt(totals[0] + damping)
    lower_one = totals[1] / pivot_first
    lower_two = totals[2] / pivot_first
    pivot_second = jnp.sqrt(totals[3] + damping - lower_one * lower_one)
    lower_mid = (totals[4] - lower_two * lower_one) / pivot_second
    pivot_third = jnp.sqrt(totals[5] + damping - lower_two * lower_two - lower_mid * lower_mid)
    solved_one = totals[6] / pivot_first
    solved_two = (totals[7] - lower_one * solved_one) / pivot_second
    solved_three = (totals[8] - lower_two * solved_one - lower_mid * solved_two) / pivot_third
    per_track = jnp.stack(
        [
            pivot_first,
            lower_one,
            lower_two,
            pivot_second,
            lower_mid,
            pivot_third,
            solved_one,
            solved_two,
            solved_three,
        ]
    )
    per_obs = per_track[:, track_of]
    weights = (
        camera[0][:, None, :] * point_jac[0][None, :, :]
        + camera[1][:, None, :] * point_jac[1][None, :, :]
    )
    column_one = weights[:, 0] / per_obs[0]
    column_two = (weights[:, 1] - per_obs[1] * column_one) / per_obs[3]
    column_three = (weights[:, 2] - per_obs[2] * column_one - per_obs[4] * column_two) / per_obs[5]
    factor = jnp.stack([column_one, column_two, column_three])
    point_shift = column_one * per_obs[6] + column_two * per_obs[7] + column_three * per_obs[8]
    return (factor, point_shift)


def camera_terms(camera_rows, resid_rows, factor, point_shift):
    camera = camera_rows.reshape(2, 9, -1)
    normal = (
        camera[0][:, None, :] * camera[0][None, :, :]
        + camera[1][:, None, :] * camera[1][None, :, :]
    )
    schur_part = (
        factor[0][:, None, :] * factor[0][None, :, :]
        + factor[1][:, None, :] * factor[1][None, :, :]
        + factor[2][:, None, :] * factor[2][None, :, :]
    )
    gradient = camera[0] * resid_rows[0] + camera[1] * resid_rows[1] - point_shift
    return jnp.concatenate([(normal - schur_part).reshape(81, -1), gradient], axis=0)


def pair_product(left, right):
    total = (
        left[0][:, None] * right[0][None, :]
        + left[1][:, None] * right[1][None, :]
        + left[2][:, None] * right[2][None, :]
    )
    return -total.reshape(81, -1)


def on_device(
    camera_jacobian, point_jacobian, residual, send_order, camera_of, track_of, partner, pair_slot
):
    obs_count = camera_jacobian.shape[1]
    ranks = partner.shape[0]
    camera_count = CAM_ROW * lax.axis_size("row")
    slot_count = camera_count * NBR
    stacked = jnp.concatenate([camera_jacobian, point_jacobian, residual], axis=0)
    sent = jnp.take(stacked, send_order, axis=1)
    owned = lax.all_to_all(sent, "obs", split_axis=1, concat_axis=1, tiled=True)
    factor, point_shift = eliminate(
        owned[:18], owned[18:24], owned[24:26], track_of, obs_count // 2
    )
    flat_factor = factor.reshape(27, obs_count)
    chosen = jnp.take(flat_factor, partner.reshape(-1), axis=1)
    together = jnp.concatenate(
        [
            flat_factor,
            point_shift,
            chosen.reshape(27, ranks, obs_count).reshape(27 * ranks, obs_count),
        ],
        axis=0,
    )
    back = lax.all_to_all(together, "obs", split_axis=1, concat_axis=1, tiled=True)
    factor_back = back[:27].reshape(3, 9, obs_count)
    shift_back = back[27:36]
    remote = back[36:].reshape(3, 9, ranks, obs_count)
    arrived = pair_product(factor_back[:, :, None, :], remote)
    local_terms = camera_terms(sent[:18], sent[24:26], factor_back, shift_back)
    camera_ids = jnp.take(camera_of, send_order)
    indicator = (camera_ids[:, None] == jnp.arange(camera_count, dtype=jnp.int32)[None, :]).astype(
        jnp.float32
    )
    camera_partial = jnp.dot(
        local_terms, indicator, precision=lax.Precision.HIGHEST, preferred_element_type=jnp.float32
    )
    camera_mine = lax.psum_scatter(camera_partial, "row", scatter_dimension=1, tiled=True)
    pair_total = (
        jnp.zeros((81, slot_count + 1), jnp.float32).at[:, pair_slot.reshape(-1)].add(arrived)
    )
    pair_mine = lax.psum_scatter(pair_total[:, :slot_count], "row", scatter_dimension=1, tiled=True)
    return (camera_mine[:81], camera_mine[81:], pair_mine)


def on_mesh(*arguments):
    share = arguments[0].shape[1] // lax.axis_size("obs")
    if share == LANES and lax.axis_size("obs") % 2 == 0:
        return by_lanes(*arguments)
    return on_device(*arguments)


def solution(mesh):
    return jax.shard_map(
        on_mesh,
        mesh=mesh,
        in_specs=(
            P(None, ("obs", "row")),
            P(None, ("obs", "row")),
            P(None, ("obs", "row")),
            P(("obs", "row")),
            P(("obs", "row")),
            P(("obs", "row")),
            P(None, ("obs", "row")),
            P(None, ("obs", "row")),
        ),
        out_specs=(P(None, ("obs", "row")), P(None, ("obs", "row")), P(None, ("obs", "row"))),
        check_vma=False,
    )
```

```python
import functools

import jax
import jax.numpy as jnp
from jax import lax
from jax.experimental import pallas as pl
from jax.experimental.pallas import tpu as pltpu
from jax.sharding import PartitionSpec as P

CAM_ROW = 16
NBR = 14
LANES = 128
SUBLANES = 8
CHUNK = 256
MESH = pl.DeviceIdType.MESH
VMEM_BYTES = 32 * 1024 * 1024


COLUMNS = [[8], [0, 1, 2, 3], [4, 5, 6, 7]]
PIECES = [
    [("point", f) for f in range(6)]
    + [("resid", f) for f in range(2)]
    + [("camera", 8), ("camera", 17)]
] + [[("camera", q + 9 * i) for i in range(2) for q in pair] for pair in COLUMNS[1:]]
TERMS = [NBR * 9 * len(columns) + (90 if k == 0 else 0) for k, columns in enumerate(COLUMNS)]
SIZES = [-(-rows // CHUNK) * CHUNK for rows in TERMS]
TABLE = [entry for piece in PIECES for entry in piece]
STARTS = [sum(len(piece) for piece in PIECES[:k]) for k in range(len(PIECES))]
PLACE = {entry: i for i, entry in enumerate(TABLE)}


def lane_gather(values, index):
    return jnp.take_along_axis(values, index, axis=1, mode="promise_in_bounds")


def normal_rows(camera_point):
    a, b, e = camera_point[0:3], camera_point[3:6], camera_point[6:8]
    return [
        a[0] * a[0] + b[0] * b[0],
        a[0] * a[1] + b[0] * b[1],
        a[0] * a[2] + b[0] * b[2],
        a[1] * a[1] + b[1] * b[1],
        a[1] * a[2] + b[1] * b[2],
        a[2] * a[2] + b[2] * b[2],
        a[0] * e[0] + b[0] * e[1],
        a[1] * e[0] + b[1] * e[1],
        a[2] * e[0] + b[2] * e[1],
    ]


def step_kernel(
    n, n_row, cameras,
    camera_in, point_in, resid_in, order_in, ids_in, partner_in, pair_in,
    hessian_ref, gradient_ref, pair_out_ref,
    camera_ref, point_ref, resid_ref, order_ref, ids_ref, partner_ref, pair_ref, load_sem,
    rows_in, part, staged, pairs, rows_of, offset_of, place_of, own, normal_of, factor_of, prod,
    marks,
    partial, landed, turned, placing,
    id_send, id_recv, row_send, row_recv, pass_send, sum_send, sum_recv,
):
    me = lax.axis_index("obs")
    my_row = lax.axis_index("row")
    chips = n // 2
    chip = me // 2
    core = lax.rem(me, 2)
    sibling = chip * 2 + 1 - core
    ranks = partner_ref.shape[0]
    shift = LANES.bit_length() - 1

    moves = [
        pltpu.make_async_copy(source, target, load_sem.at[i])
        for i, (source, target) in enumerate(
            [
                (order_in, order_ref),
                (point_in, point_ref),
                (resid_in, resid_ref),
                (camera_in, camera_ref),
                (partner_in, partner_ref),
                (ids_in, ids_ref),
                (pair_in, pair_ref),
            ]
        )
    ]
    for move in moves:
        move.start()
    barrier = pltpu.get_barrier_semaphore()
    for d in range(1, n):
        pl.semaphore_signal(
            barrier, inc=1, device_id={"obs": lax.rem(me + d, n)}, device_id_type=MESH
        )
    for d in range(1, n_row):
        pl.semaphore_signal(
            barrier, inc=1, device_id={"row": lax.rem(my_row + d, n_row)}, device_id_type=MESH
        )

    def ids_copy(peer, source):
        return pltpu.make_async_remote_copy(
            src_ref=staged.at[peer],
            dst_ref=part.at[pl.ds(pl.multiple_of(source * SUBLANES, SUBLANES), SUBLANES)],
            send_sem=id_send.at[peer],
            recv_sem=id_recv.at[source],
            device_id={"obs": peer},
            device_id_type=MESH,
        )

    def rows_copy(source, piece, peer, sem):
        block = rows_in.at[source, pl.ds(STARTS[piece], len(PIECES[piece]))]
        return pltpu.make_async_remote_copy(
            src_ref=block,
            dst_ref=block,
            send_sem=sem.at[peer if sem is row_send else source, piece],
            recv_sem=row_recv.at[source, piece],
            device_id={"obs": peer},
            device_id_type=MESH,
        )

    def twin(d):
        return lax.rem(chip + d, chips) * 2 + core

    for move in moves[:4]:
        move.wait()
    order = order_ref[...]
    block_of = lax.shift_right_logical(order, shift)
    lane_of = lax.bitwise_and(order, LANES - 1)

    def permuted(row_of_block):
        total = None
        for b in range(n):
            row = jnp.broadcast_to(row_of_block(b), (n, LANES))
            picked = lane_gather(row, lane_of)
            total = picked if b == 0 else jnp.where(block_of == b, picked, total)
        return total

    inputs = {"point": point_ref, "resid": resid_ref, "camera": camera_ref}
    targets = [twin(d) for d in range(1, chips)] + [sibling]
    for piece in range(len(PIECES)):
        for i, (name, r) in enumerate(PIECES[piece]):
            ref = inputs[name]
            rows_in[me, STARTS[piece] + i] = permuted(
                lambda b: ref[r : r + 1, b * LANES : (b + 1) * LANES]
            )
        if piece == 0:
            pl.semaphore_wait(barrier, n - 1 + n_row - 1)
        for peer in targets:
            rows_copy(me, piece, peer, row_send).start()
        if piece == 0:
            for move in moves[4:]:
                move.wait()
            for x in range(n):
                staged[x] = jnp.zeros((SUBLANES, LANES), jnp.int32)
                staged[x, 0:ranks] = partner_ref[:, x * LANES : (x + 1) * LANES]
            for d in range(1, n):
                ids_copy(lax.rem(me + d, n), me).start()
    part[pl.ds(pl.multiple_of(me * SUBLANES, SUBLANES), SUBLANES), :] = staged[me]

    cam = permuted(lambda b: ids_ref[b : b + 1, :])
    ids = lax.broadcasted_iota(jnp.int32, (cameras, LANES), 0)
    halves = [
        jnp.where(ids == cam[j : j + 1, :], 1.0, 0.0).astype(jnp.bfloat16) for j in range(n)
    ]
    for i in range(n // 2):
        marks[i] = jnp.concatenate([halves[2 * i], halves[2 * i + 1]], axis=1)
    for j in range(n):
        pairs[pl.ds(j, ranks, stride=n), :] = pair_ref[:, j * LANES : (j + 1) * LANES]
    turned[...] = jnp.zeros_like(turned)
    slots = pair_out_ref.shape[1]
    lane = lax.broadcasted_iota(jnp.int32, (slots, slots), 1)
    line = lax.broadcasted_iota(jnp.int32, (slots, slots), 0)
    chosen = lane == (
        lax.bitwise_and(line, CAM_ROW - 1) * NBR
        + lax.shift_right_logical(line, CAM_ROW.bit_length() - 1)
    )
    placing[...] = jnp.where(chosen, 1.0, 0.0).astype(jnp.bfloat16)

    for d in range(1, n):
        peer = lax.rem(me + d, n)
        ids_copy(peer, peer).wait_recv()
    sources, places, offsets = [], [], []
    for k in range(ranks):
        slot = part[pl.ds(k, n, stride=SUBLANES), :]
        pair = pairs[pl.ds(k * n, n), :]
        sources.append(
            jnp.where(pair == cameras * NBR, -1, lax.shift_right_logical(slot, shift))
        )
        places.append(lax.bitwise_and(slot, LANES - 1))
        offsets.append(pair - cam * NBR)

    def find_partner(x, carry):
        place = jnp.zeros((n, LANES), jnp.int32)
        offset = jnp.full((n, LANES), -1, jnp.int32)
        for k in range(ranks):
            match = sources[k] == x
            place = jnp.where(match, places[k], place)
            offset = jnp.where(match, offsets[k], offset)
        offset_of[x] = offset
        place_of[x] = place
        return carry

    lax.fori_loop(0, n, find_partner, 0)

    def pass_on(piece):
        for d in range(1, chips):
            rows_copy(twin(d), piece, sibling, row_send).wait_recv()
            rows_copy(twin(d), piece, sibling, pass_send).start()

    def each_source(piece, visit, carry):
        carry = visit(me, carry)
        rows_copy(sibling, piece, sibling, row_send).wait_recv()
        carry = visit(sibling, carry)
        carry = lax.fori_loop(1, chips, lambda d, c: visit(twin(d), c), carry)

        def passed(d, c):
            x = lax.rem(chip + d, chips) * 2 + 1 - core
            rows_copy(x, piece, sibling, pass_send).wait_recv()
            return visit(x, c)

        return lax.fori_loop(1, chips, passed, carry)

    def gathered(x, piece):
        place = place_of[x]
        found = offset_of[x] >= 0
        return [
            jnp.where(found, lane_gather(rows_in[x, STARTS[piece] + i], place), 0.0)
            for i in range(len(PIECES[piece]))
        ]

    def add_source(x, totals):
        values = gathered(x, 0)
        for i, value in enumerate(values):
            rows_of[x, i] = value
        return tuple(t + v for t, v in zip(totals, normal_rows(values[0:8])))

    pass_on(0)
    totals = tuple(normal_rows([rows_in[me, f] for f in range(8)]))
    totals = each_source(0, add_source, totals)
    pivot_one = jnp.sqrt(totals[0] + 1.0)
    inv_one = 1.0 / pivot_one
    low_one = totals[1] * inv_one
    low_two = totals[2] * inv_one
    inv_two = 1.0 / jnp.sqrt(totals[3] + 1.0 - low_one * low_one)
    low_mid = (totals[4] - low_two * low_one) * inv_two
    inv_three = 1.0 / jnp.sqrt(totals[5] + 1.0 - low_two * low_two - low_mid * low_mid)
    h_one = totals[6] * inv_one
    h_two = (totals[7] - low_one * h_one) * inv_two
    h_three = (totals[8] - low_two * h_one - low_mid * h_two) * inv_three

    def solved(rows):
        result = []
        for i in range(2):
            jp = [rows(3 * i + c) for c in range(3)]
            one = jp[0] * inv_one
            two = (jp[1] - low_one * one) * inv_two
            three = (jp[2] - low_two * one - low_mid * two) * inv_three
            result.append((one, two, three))
        return result

    def put(row, value):
        prod[pl.ds(pl.multiple_of(row * n, n), n), :] = value

    jac = [rows_in[me, PLACE["camera", f]] for f in range(18)]
    weight = solved(lambda f: rows_in[me, f])
    mine = [
        [jac[p] * weight[0][c] + jac[9 + p] * weight[1][c] for p in range(9)] for c in range(3)
    ]
    for c in range(3):
        for p in range(9):
            own[c * 9 + p] = -mine[c][p]
    base = NBR * 9
    for p in range(9):
        for q in range(p, 9):
            value = jac[p] * jac[q] + jac[9 + p] * jac[9 + q]
            value = value - (
                mine[0][p] * mine[0][q] + mine[1][p] * mine[1][q] + mine[2][p] * mine[2][q]
            )
            put(base + 9 * p + q, value)
            if q != p:
                put(base + 9 * q + p, value)
        back = mine[0][p] * h_one + mine[1][p] * h_two + mine[2][p] * h_three
        put(base + 81 + p, jac[p] * rows_in[me, 6] + jac[9 + p] * rows_in[me, 7] - back)

    def solve_source(x, carry):
        got = solved(lambda f: rows_of[x, f])
        for i in range(2):
            for c in range(3):
                normal_of[x, 3 * i + c] = got[i][c]
        for c in range(3):
            factor_of[x, c] = rows_of[x, 8] * got[0][c] + rows_of[x, 9] * got[1][c]
        return carry

    lax.fori_loop(0, n, solve_source, 0)

    contract = (((1,), (1,)), ((), ()))

    def sum_copy(peer, slot, chunk):
        return pltpu.make_async_remote_copy(
            src_ref=partial.at[
                chunk,
                pl.ds(pl.multiple_of(peer * CAM_ROW, CAM_ROW), CAM_ROW),
                pl.ds(0, SIZES[chunk]),
            ],
            dst_ref=landed.at[slot, chunk, :, pl.ds(0, SIZES[chunk])],
            send_sem=sum_send.at[peer, chunk],
            recv_sem=sum_recv.at[slot, chunk],
            device_id={"row": peer},
            device_id_type=MESH,
        )

    for chunk, columns in enumerate(COLUMNS):
        width = len(columns)
        if chunk > 0:

            def make_factors(x, carry):
                values = gathered(x, chunk)
                for c in range(3):
                    for i in range(width):
                        factor_of[x, c * width + i] = (
                            values[i] * normal_of[x, c] + values[width + i] * normal_of[x, 3 + c]
                        )
                return carry

            each_source(chunk, make_factors, 0)
        if chunk + 1 < len(COLUMNS):
            pass_on(chunk + 1)

        def at_offset(o, carry):
            picked = [None] * (3 * width)
            for x in range(n):
                match = offset_of[x] == o
                for i in range(3 * width):
                    value = jnp.where(match, factor_of[x, i], 0.0)
                    picked[i] = value if x == 0 else picked[i] + value
            for p in range(9):
                left = [own[c * 9 + p] for c in range(3)]
                for i in range(width):
                    value = (
                        left[0] * picked[i]
                        + left[1] * picked[width + i]
                        + left[2] * picked[2 * width + i]
                    )
                    put(o * (9 * width) + i * 9 + p, value)
            return carry

        lax.fori_loop(0, NBR, at_offset, 0)
        for part_start in range(0, SIZES[chunk], CHUNK):
            total = jnp.zeros((cameras, CHUNK), jnp.float32)
            for i in range(n // 2):
                start = part_start * n + 2 * i
                first = prod[pl.ds(start, CHUNK, stride=n), :]
                second = prod[pl.ds(start + 1, CHUNK, stride=n), :]
                both = jnp.concatenate([first, second], axis=1)
                high = both.astype(jnp.bfloat16)
                low = (both - high.astype(jnp.float32)).astype(jnp.bfloat16)
                for half in (high, low):
                    total += lax.dot_general(
                        marks[i], half, contract, preferred_element_type=jnp.float32
                    )
            partial[chunk, :, part_start : part_start + CHUNK] = total
        for d in range(1, n_row):
            sum_copy(lax.rem(my_row + d, n_row), my_row, chunk).start()

    select = placing[...]
    for chunk, columns in enumerate(COLUMNS):
        lanes = pl.ds(0, SIZES[chunk])
        total = partial[
            chunk, pl.ds(pl.multiple_of(my_row * CAM_ROW, CAM_ROW), CAM_ROW), lanes
        ]
        for d in range(1, n_row):
            peer = lax.rem(my_row + d, n_row)
            sum_copy(peer, peer, chunk).wait_recv()
            total = total + landed[peer, chunk, :, lanes]
        height = 9 * len(columns)
        for o in range(NBR):
            turned[o * CAM_ROW : (o + 1) * CAM_ROW, 0:height] = total[
                :, o * height : (o + 1) * height
            ]
        flipped = turned[...].T
        rows = flipped[0 : -(-height // SUBLANES) * SUBLANES, 0:slots]
        high = rows.astype(jnp.bfloat16)
        low = (rows - high.astype(jnp.float32)).astype(jnp.bfloat16)
        placed = jnp.dot(high, select, preferred_element_type=jnp.float32)
        placed = placed + jnp.dot(low, select, preferred_element_type=jnp.float32)
        for i, q in enumerate(columns):
            for p in range(9):
                row = i * 9 + p
                pair_out_ref[9 * p + q : 9 * p + q + 1, :] = placed[row : row + 1]
        if chunk == 0:
            hessian_ref[...] = total[:, base : base + 81]
            turned[0:CAM_ROW, 0:9] = total[:, base + 81 : base + 90]
            gradient_ref[...] = turned[0:LANES].T[0:9, 0:CAM_ROW]

    for d in range(1, n):
        ids_copy(lax.rem(me + d, n), me).wait_send()
    for piece in range(len(PIECES)):
        for peer in targets:
            rows_copy(me, piece, peer, row_send).wait_send()
        for d in range(1, chips):
            rows_copy(twin(d), piece, sibling, pass_send).wait_send()
    for chunk in range(len(COLUMNS)):
        for d in range(1, n_row):
            sum_copy(lax.rem(my_row + d, n_row), my_row, chunk).wait_send()


def store_kernel(*refs):
    copies = [
        pltpu.make_async_copy(refs[i], refs[3 + i], refs[6].at[i]) for i in range(3)
    ]
    for copy in copies:
        copy.start()
    for copy in copies:
        copy.wait()


def by_lanes(
    camera_jacobian, point_jacobian, residual, send_order, camera_of, track_of, partner, pair_slot
):
    n = lax.axis_size("obs")
    n_row = lax.axis_size("row")
    cameras = CAM_ROW * n_row
    ranks = partner.shape[0]
    chunks = len(COLUMNS)
    vmem = pl.BlockSpec(memory_space=pltpu.VMEM)
    hbm = pl.BlockSpec(memory_space=pltpu.HBM)
    f32, i32 = jnp.float32, jnp.int32
    dma = pltpu.SemaphoreType.DMA
    results = pl.pallas_call(
        functools.partial(step_kernel, n, n_row, cameras),
        out_shape=(
            pltpu.VMEM((CAM_ROW, 81), f32),
            pltpu.VMEM((9, CAM_ROW), f32),
            pltpu.VMEM((81, CAM_ROW * NBR), f32),
        ),
        in_specs=[hbm] * 7,
        out_specs=(vmem, vmem, vmem),
        scratch_shapes=[
            pltpu.VMEM(camera_jacobian.shape, f32),
            pltpu.VMEM(point_jacobian.shape, f32),
            pltpu.VMEM(residual.shape, f32),
            pltpu.VMEM((n, LANES), i32),
            pltpu.VMEM((n, LANES), i32),
            pltpu.VMEM(partner.shape, i32),
            pltpu.VMEM(pair_slot.shape, i32),
            dma((7,)),
            pltpu.VMEM((n, 26, n, LANES), f32),
            pltpu.VMEM((n * SUBLANES, LANES), i32),
            pltpu.VMEM((n, SUBLANES, LANES), i32),
            pltpu.VMEM((ranks * n, LANES), i32),
            pltpu.VMEM((n, len(PIECES[0]), n, LANES), f32),
            pltpu.VMEM((n, n, LANES), i32),
            pltpu.VMEM((n, n, LANES), i32),
            pltpu.VMEM((27, n, LANES), f32),
            pltpu.VMEM((n, 6, n, LANES), f32),
            pltpu.VMEM((n, 3 * max(len(c) for c in COLUMNS), n, LANES), f32),
            pltpu.VMEM((max(SIZES) * n, LANES), f32),
            pltpu.VMEM((n // 2, cameras, 2 * LANES), jnp.bfloat16),
            pltpu.VMEM((chunks, cameras, max(SIZES)), f32),
            pltpu.VMEM((n_row, chunks, CAM_ROW, max(SIZES)), f32),
            pltpu.VMEM((2 * LANES, LANES), f32),
            pltpu.VMEM((CAM_ROW * NBR, CAM_ROW * NBR), jnp.bfloat16),
            dma((n,)),
            dma((n,)),
            dma((n, len(PIECES))),
            dma((n, len(PIECES))),
            dma((n, len(PIECES))),
            dma((n_row, chunks)),
            dma((n_row, chunks)),
        ],
        compiler_params=pltpu.CompilerParams(
            collective_id=0, has_side_effects=True, vmem_limit_bytes=VMEM_BYTES
        ),
        name="gauss_newton_step",
    )(
        *(
            pltpu.with_memory_space_constraint(value, pltpu.HBM)
            for value in (
                camera_jacobian,
                point_jacobian,
                residual,
                send_order.reshape(n, LANES),
                camera_of.reshape(n, LANES),
                partner,
                pair_slot,
            )
        )
    )
    hessian, gradient, pair_hessian = pl.pallas_call(
        store_kernel,
        out_shape=tuple(pltpu.HBM(r.shape, r.dtype) for r in results),
        in_specs=[vmem] * 3,
        out_specs=(hbm,) * 3,
        scratch_shapes=[dma((3,))],
        compiler_params=pltpu.CompilerParams(vmem_limit_bytes=4 * 1024 * 1024),
        name="store",
    )(*(pltpu.with_memory_space_constraint(r, pltpu.VMEM) for r in results))
    return (hessian.T, gradient, pair_hessian)


damping = 1.0


def eliminate(camera_rows, point_rows, resid_rows, track_of, track_count):
    camera = camera_rows.reshape(2, 9, -1)
    point_jac = point_rows.reshape(2, 3, -1)
    normal = jnp.stack(
        [
            point_jac[0, 0] * point_jac[0, 0] + point_jac[1, 0] * point_jac[1, 0],
            point_jac[0, 0] * point_jac[0, 1] + point_jac[1, 0] * point_jac[1, 1],
            point_jac[0, 0] * point_jac[0, 2] + point_jac[1, 0] * point_jac[1, 2],
            point_jac[0, 1] * point_jac[0, 1] + point_jac[1, 1] * point_jac[1, 1],
            point_jac[0, 1] * point_jac[0, 2] + point_jac[1, 1] * point_jac[1, 2],
            point_jac[0, 2] * point_jac[0, 2] + point_jac[1, 2] * point_jac[1, 2],
            point_jac[0, 0] * resid_rows[0] + point_jac[1, 0] * resid_rows[1],
            point_jac[0, 1] * resid_rows[0] + point_jac[1, 1] * resid_rows[1],
            point_jac[0, 2] * resid_rows[0] + point_jac[1, 2] * resid_rows[1],
        ]
    )
    totals = jnp.zeros((9, track_count), jnp.float32).at[:, track_of].add(normal)
    pivot_first = jnp.sqrt(totals[0] + damping)
    lower_one = totals[1] / pivot_first
    lower_two = totals[2] / pivot_first
    pivot_second = jnp.sqrt(totals[3] + damping - lower_one * lower_one)
    lower_mid = (totals[4] - lower_two * lower_one) / pivot_second
    pivot_third = jnp.sqrt(totals[5] + damping - lower_two * lower_two - lower_mid * lower_mid)
    solved_one = totals[6] / pivot_first
    solved_two = (totals[7] - lower_one * solved_one) / pivot_second
    solved_three = (totals[8] - lower_two * solved_one - lower_mid * solved_two) / pivot_third
    per_track = jnp.stack(
        [
            pivot_first,
            lower_one,
            lower_two,
            pivot_second,
            lower_mid,
            pivot_third,
            solved_one,
            solved_two,
            solved_three,
        ]
    )
    per_obs = per_track[:, track_of]
    weights = (
        camera[0][:, None, :] * point_jac[0][None, :, :]
        + camera[1][:, None, :] * point_jac[1][None, :, :]
    )
    column_one = weights[:, 0] / per_obs[0]
    column_two = (weights[:, 1] - per_obs[1] * column_one) / per_obs[3]
    column_three = (weights[:, 2] - per_obs[2] * column_one - per_obs[4] * column_two) / per_obs[5]
    factor = jnp.stack([column_one, column_two, column_three])
    point_shift = column_one * per_obs[6] + column_two * per_obs[7] + column_three * per_obs[8]
    return (factor, point_shift)


def camera_terms(camera_rows, resid_rows, factor, point_shift):
    camera = camera_rows.reshape(2, 9, -1)
    normal = (
        camera[0][:, None, :] * camera[0][None, :, :]
        + camera[1][:, None, :] * camera[1][None, :, :]
    )
    schur_part = (
        factor[0][:, None, :] * factor[0][None, :, :]
        + factor[1][:, None, :] * factor[1][None, :, :]
        + factor[2][:, None, :] * factor[2][None, :, :]
    )
    gradient = camera[0] * resid_rows[0] + camera[1] * resid_rows[1] - point_shift
    return jnp.concatenate([(normal - schur_part).reshape(81, -1), gradient], axis=0)


def pair_product(left, right):
    total = (
        left[0][:, None] * right[0][None, :]
        + left[1][:, None] * right[1][None, :]
        + left[2][:, None] * right[2][None, :]
    )
    return -total.reshape(81, -1)


def on_device(
    camera_jacobian, point_jacobian, residual, send_order, camera_of, track_of, partner, pair_slot
):
    obs_count = camera_jacobian.shape[1]
    ranks = partner.shape[0]
    camera_count = CAM_ROW * lax.axis_size("row")
    slot_count = camera_count * NBR
    stacked = jnp.concatenate([camera_jacobian, point_jacobian, residual], axis=0)
    sent = jnp.take(stacked, send_order, axis=1)
    owned = lax.all_to_all(sent, "obs", split_axis=1, concat_axis=1, tiled=True)
    factor, point_shift = eliminate(
        owned[:18], owned[18:24], owned[24:26], track_of, obs_count // 2
    )
    flat_factor = factor.reshape(27, obs_count)
    chosen = jnp.take(flat_factor, partner.reshape(-1), axis=1)
    together = jnp.concatenate(
        [
            flat_factor,
            point_shift,
            chosen.reshape(27, ranks, obs_count).reshape(27 * ranks, obs_count),
        ],
        axis=0,
    )
    back = lax.all_to_all(together, "obs", split_axis=1, concat_axis=1, tiled=True)
    factor_back = back[:27].reshape(3, 9, obs_count)
    shift_back = back[27:36]
    remote = back[36:].reshape(3, 9, ranks, obs_count)
    arrived = pair_product(factor_back[:, :, None, :], remote)
    local_terms = camera_terms(sent[:18], sent[24:26], factor_back, shift_back)
    camera_ids = jnp.take(camera_of, send_order)
    indicator = (camera_ids[:, None] == jnp.arange(camera_count, dtype=jnp.int32)[None, :]).astype(
        jnp.float32
    )
    camera_partial = jnp.dot(
        local_terms, indicator, precision=lax.Precision.HIGHEST, preferred_element_type=jnp.float32
    )
    camera_mine = lax.psum_scatter(camera_partial, "row", scatter_dimension=1, tiled=True)
    pair_total = (
        jnp.zeros((81, slot_count + 1), jnp.float32).at[:, pair_slot.reshape(-1)].add(arrived)
    )
    pair_mine = lax.psum_scatter(pair_total[:, :slot_count], "row", scatter_dimension=1, tiled=True)
    return (camera_mine[:81], camera_mine[81:], pair_mine)


def on_mesh(*arguments):
    share = arguments[0].shape[1] // lax.axis_size("obs")
    if share == LANES and lax.axis_size("obs") % 2 == 0:
        return by_lanes(*arguments)
    return on_device(*arguments)


def solution(mesh):
    return jax.shard_map(
        on_mesh,
        mesh=mesh,
        in_specs=(
            P(None, ("obs", "row")),
            P(None, ("obs", "row")),
            P(None, ("obs", "row")),
            P(("obs", "row")),
            P(("obs", "row")),
            P(("obs", "row")),
            P(None, ("obs", "row")),
            P(None, ("obs", "row")),
        ),
        out_specs=(P(None, ("obs", "row")), P(None, ("obs", "row")), P(None, ("obs", "row"))),
        check_vma=False,
    )
```
